32 devices in a mesh: grp: 2 (over x), wide: 4 (over z), narrow: 4 (over y, core).
Axes of the slice: x: 2, y: 2, z: 4, core: 2. Of those that a mesh axis runs over, the one named last changes fastest.
Arguments:
- img_in: bfloat16 [4, 1024, 768], P('wide', 'narrow'), may hold values from -6 to 6
- tri_in: bfloat16 [4, 1536, 1024], P('wide', 'narrow'), may hold values from -16 to 16
- cam: float32 [4, 1024], P('wide'), may hold values from -6 to 6
- targets: float32 [4, 3, 1536], P('wide', None, 'narrow'), may hold values from 0 to 1
- fg_mask: int32 [4, 1536], P('wide', 'narrow'), may hold values 0 or 1
- counts: int32 [4, 4], P('wide'), may hold values from 96 to 384, as said below
- ln1_gain: bfloat16 [768], P(('wide', 'narrow')), may hold values from 0.5 to 1.5
- ln1_bias: bfloat16 [768], P(('wide', 'narrow')), may hold values from -1.25 to 1.25
- enc_qkv: bfloat16 [768, 2304], P(('wide', 'narrow')), may hold values from -0.21875 to 0.21875
- enc_qv_bias: bfloat16 [1536], P(('wide', 'narrow')), may hold values from -1.25 to 1.25
- enc_proj: bfloat16 [768, 768], P(('wide', 'narrow')), may hold values from -0.875 to 0.875
- enc_proj_bias: bfloat16 [768], P(('wide', 'narrow')), may hold values from -1.25 to 1.25
- ln2_gain: bfloat16 [768], P(('wide', 'narrow')), may hold values from 0.5 to 1.5
- ln2_bias: bfloat16 [768], P(('wide', 'narrow')), may hold values from -1.25 to 1.25
- enc_fc1: bfloat16 [768, 3072], P(('wide', 'narrow')), may hold values from -0.21875 to 0.21875
- enc_fc1_bias: bfloat16 [3072], P(('wide', 'narrow')), may hold values from -1.25 to 1.25
- enc_fc2: bfloat16 [3072, 768], P(('wide', 'narrow')), may hold values from -0.21875 to 0.21875
- enc_fc2_bias: bfloat16 [768], P(('wide', 'narrow')), may hold values from -1.25 to 1.25
- dec_mod: bfloat16 [1024, 6144], P(('wide', 'narrow')), may hold values from -0.046875 to 0.046875
- dec_qkv: bfloat16 [1024, 3072], P(('wide', 'narrow')), may hold values from -0.1875 to 0.1875
- dec_proj: bfloat16 [1024, 1024], P(('wide', 'narrow')), may hold values from -0.75 to 0.75
- dec_cross_q: bfloat16 [1024, 1024], P(('wide', 'narrow')), may hold values from -0.1875 to 0.1875
- dec_cross_kv: bfloat16 [768, 2048], P(('wide', 'narrow')), may hold values from -0.21875 to 0.21875
- dec_cross_proj: bfloat16 [1024, 1024], P(('wide', 'narrow')), may hold values from -0.75 to 0.75
- dec_fc1: bfloat16 [1024, 4096], P(('wide', 'narrow')), may hold values from -0.1875 to 0.1875
- dec_fc1_bias: bfloat16 [4096], P(('wide', 'narrow')), may hold values from -1.25 to 1.25
- dec_fc2: bfloat16 [4096, 1024], P(('wide', 'narrow')), may hold values from -0.1875 to 0.1875
- dec_fc2_bias: bfloat16 [1024], P(('wide', 'narrow')), may hold values from -1.25 to 1.25
- dec_head: bfloat16 [1024, 4], P(('wide', 'narrow')), may hold values from -0.005859375 to 0.005859375
Outputs:
- loss: float32 [], replicated
- img_grad: float32 [4, 1024, 768], P('wide', 'narrow')
- tri_grad: float32 [4, 1536, 1024], P('wide', 'narrow')
- ln1_gain_grad: float32 [768], P(('wide', 'narrow'))
- ln1_bias_grad: float32 [768], P(('wide', 'narrow'))
- enc_qkv_grad: float32 [768, 2304], P(('wide', 'narrow'))
- enc_qv_bias_grad: float32 [1536], P(('wide', 'narrow'))
- enc_proj_grad: float32 [768, 768], P(('wide', 'narrow'))
- enc_proj_bias_grad: float32 [768], P(('wide', 'narrow'))
- ln2_gain_grad: float32 [768], P(('wide', 'narrow'))
- ln2_bias_grad: float32 [768], P(('wide', 'narrow'))
- enc_fc1_grad: float32 [768, 3072], P(('wide', 'narrow'))
- enc_fc1_bias_grad: float32 [3072], P(('wide', 'narrow'))
- enc_fc2_grad: float32 [3072, 768], P(('wide', 'narrow'))
- enc_fc2_bias_grad: float32 [768], P(('wide', 'narrow'))
- dec_mod_grad: float32 [1024, 6144], P(('wide', 'narrow'))
- dec_qkv_grad: float32 [1024, 3072], P(('wide', 'narrow'))
- dec_proj_grad: float32 [1024, 1024], P(('wide', 'narrow'))
- dec_cross_q_grad: float32 [1024, 1024], P(('wide', 'narrow'))
- dec_cross_kv_grad: float32 [768, 2048], P(('wide', 'narrow'))
- dec_cross_proj_grad: float32 [1024, 1024], P(('wide', 'narrow'))
- dec_fc1_grad: float32 [1024, 4096], P(('wide', 'narrow'))
- dec_fc1_bias_grad: float32 [4096], P(('wide', 'narrow'))
- dec_fc2_grad: float32 [4096, 1024], P(('wide', 'narrow'))
- dec_fc2_bias_grad: float32 [1024], P(('wide', 'narrow'))
- dec_head_grad: float32 [1024, 4], P(('wide', 'narrow'))
The draws below stay inside these ranges and needn't reach their ends.
Inputs may be any that keep to these rules, and one draw needn't show every extreme that they name: `counts`: each count lies between 384 // 4 (at least 1) and 384; some view of some object has all 384 rays live.
All inputs are finite; a program needn't handle non-finite values. No bound on the sum of `fg_mask` on one device may be relied on, other than what follows from the above.
Results may differ from the reference program's by a relative error of at most 0.028.
Values may be sent and summed in bfloat16 or wider, within the bound.
A program may use at most 576 MiB of HBM per device.

```python
import jax
import jax.numpy as jnp
from jax import lax

ENC_W = 768
ENC_HEADS = 12
ENC_FF = 3072
DEC_W = 1024
DEC_HEADS = 16
DEC_FF = 4096
IMG_TOK = 1024
TRI_TOK = 1536
VIEWS = 4
OBJECTS = 4
RAYS = 384


def draw_counts(key, part):
    key = jax.random.fold_in(key, 5)
    low_key, pick_key = jax.random.split(key)
    values = jax.random.randint(low_key, (OBJECTS * VIEWS,), max(RAYS // 4, 1), RAYS + 1)
    chosen = jax.random.randint(pick_key, (), 0, OBJECTS * VIEWS)
    values = jnp.where(jnp.arange(OBJECTS * VIEWS) == chosen, RAYS, values)
    return values.reshape(OBJECTS, VIEWS).astype(jnp.int32)


def spread_targets(key, power):
    base_key, sign_key = jax.random.split(key)
    uniform_part = jax.random.uniform(base_key, (OBJECTS, 3, TRI_TOK), jnp.float32)
    signs = jnp.where(jax.random.bernoulli(sign_key, 0.5, (OBJECTS, 3, TRI_TOK)), 1.0, -1.0)
    fraction = (jnp.arange(OBJECTS, dtype=jnp.float32) / max(OBJECTS - 1, 1)) ** power
    fraction = fraction[:, None, None]
    values = 0.5 + (uniform_part - 0.5) * (1.0 - fraction) + 0.5 * fraction * signs
    return jnp.clip(values, 0.0, 1.0)


def draw_targets(key, part):
    key = jax.random.fold_in(key, 11)
    return spread_targets(key, 1.0)


def place_ends(values, rng, least, high):
    longest = values.shape.index(max(values.shape))
    spots = []
    for shift in (0, 1):
        where = [jax.random.randint(jax.random.fold_in(rng, axis), (), 0, length) for axis, length in enumerate(values.shape)]
        where[longest] = (where[longest] + shift) % values.shape[longest]
        spots.append(tuple(where))
    return values.at[spots[0]].set(least).at[spots[1]].set(high)


def level_of(stream_key, extent, cuts, low, top_value):
    def one(position, blocks):
        heights = jax.random.uniform(jax.random.fold_in(jax.random.fold_in(stream_key, 6), position), (blocks,), jnp.float32, low / len(cuts), top_value / len(cuts))
        return jnp.repeat(jnp.exp(heights), extent[position] // blocks).reshape((-1,) + (1,) * (len(extent) - position - 1))

    factor_of = one(*cuts[0])
    for cut in cuts[1:]:
        factor_of = factor_of * one(*cut)
    return factor_of


def centred(key, extent, spread, limit, shards=(), held_as=jnp.bfloat16):
    factor_of = level_of(key, extent, shards, -0.22, 0.18) if shards else 1.0
    drawn = jax.random.normal(key, extent, jnp.float32) * spread * factor_of
    return jnp.minimum(jnp.maximum(drawn, -limit), limit).astype(held_as)


def setup_inputs(seed: int = 0) -> dict:
    keys = jax.random.split(jax.random.key(seed), 30)
    img_in = centred(keys[0], (OBJECTS, IMG_TOK, ENC_W), 1.0, 6.0, ((0, 4), (1, 4)))
    tri_in = centred(keys[1], (OBJECTS, TRI_TOK, DEC_W), 3.0, 16.0, ((0, 4), (1, 4)))
    cam = centred(keys[2], (OBJECTS, DEC_W), 1.0, 6.0, ((0, 4),), jnp.float32)
    targets = draw_targets(jax.random.fold_in(keys[29], 71), 0)
    fg_mask = place_ends((jax.random.randint(keys[4], (OBJECTS, TRI_TOK), 0, 2) < 1).astype(jnp.int32), jax.random.fold_in(keys[4], 1), 0, 1)
    counts = draw_counts(jax.random.fold_in(keys[29], 71), 0)
    ln1_gain = jnp.clip(1.0 + 0.1 * jax.random.normal(keys[6], (ENC_W,), jnp.float32), 0.5, 1.5).astype(jnp.bfloat16)
    ln1_bias = centred(keys[7], (ENC_W,), 0.2, 1.25, ((0, 16),))
    enc_qkv = centred(keys[8], (ENC_W, 3 * ENC_W), ENC_W ** -0.5, 0.21875, ((0, 16),))
    enc_qv_bias = centred(keys[9], (2 * ENC_W,), 0.2, 1.25, ((0, 16),))
    enc_proj = centred(keys[10], (ENC_W, ENC_W), (ENC_W // 16) ** -0.5, 0.875, ((0, 16),))
    enc_proj_bias = centred(keys[11], (ENC_W,), 0.2, 1.25, ((0, 16),))
    ln2_gain = jnp.clip(1.0 + 0.1 * jax.random.normal(keys[12], (ENC_W,), jnp.float32), 0.5, 1.5).astype(jnp.bfloat16)
    ln2_bias = centred(keys[13], (ENC_W,), 0.2, 1.25, ((0, 16),))
    enc_fc1 = centred(keys[14], (ENC_W, ENC_FF), ENC_W ** -0.5, 0.21875, ((0, 16),))
    enc_fc1_bias = centred(keys[15], (ENC_FF,), 0.2, 1.25, ((0, 16),))
    enc_fc2 = centred(keys[16], (ENC_FF, ENC_W), (ENC_FF // 4) ** -0.5, 0.21875, ((0, 16),))
    enc_fc2_bias = centred(keys[17], (ENC_W,), 0.2, 1.25, ((0, 16),))
    dec_mod = centred(keys[18], (DEC_W, 6 * DEC_W), (16 * DEC_W) ** -0.5, 0.046875, ((0, 16),))
    dec_qkv = centred(keys[19], (DEC_W, 3 * DEC_W), DEC_W ** -0.5, 0.1875, ((0, 16),))
    dec_proj = centred(keys[20], (DEC_W, DEC_W), (DEC_W // 16) ** -0.5, 0.75, ((0, 16),))
    dec_cross_q = centred(keys[21], (DEC_W, DEC_W), DEC_W ** -0.5, 0.1875, ((0, 16),))
    dec_cross_kv = centred(keys[22], (ENC_W, 2 * DEC_W), ENC_W ** -0.5, 0.21875, ((0, 16),))
    dec_cross_proj = centred(keys[23], (DEC_W, DEC_W), (DEC_W // 16) ** -0.5, 0.75, ((0, 16),))
    dec_fc1 = centred(keys[24], (DEC_W, DEC_FF), DEC_W ** -0.5, 0.1875, ((0, 16),))
    dec_fc1_bias = centred(keys[25], (DEC_FF,), 0.2, 1.25, ((0, 16),))
    dec_fc2 = centred(keys[26], (DEC_FF, DEC_W), (DEC_FF // 4) ** -0.5, 0.1875, ((0, 16),))
    dec_fc2_bias = centred(keys[27], (DEC_W,), 0.2, 1.25, ((0, 16),))
    dec_head = centred(keys[28], (DEC_W, 4), (DEC_W * DEC_W) ** -0.5, 0.005859375, ((0, 16),))
    return {"img_in": img_in, "tri_in": tri_in, "cam": cam, "targets": targets, "fg_mask": fg_mask, "counts": counts, "ln1_gain": ln1_gain, "ln1_bias": ln1_bias, "enc_qkv": enc_qkv, "enc_qv_bias": enc_qv_bias, "enc_proj": enc_proj, "enc_proj_bias": enc_proj_bias, "ln2_gain": ln2_gain, "ln2_bias": ln2_bias, "enc_fc1": enc_fc1, "enc_fc1_bias": enc_fc1_bias, "enc_fc2": enc_fc2, "enc_fc2_bias": enc_fc2_bias, "dec_mod": dec_mod, "dec_qkv": dec_qkv, "dec_proj": dec_proj, "dec_cross_q": dec_cross_q, "dec_cross_kv": dec_cross_kv, "dec_cross_proj": dec_cross_proj, "dec_fc1": dec_fc1, "dec_fc1_bias": dec_fc1_bias, "dec_fc2": dec_fc2, "dec_fc2_bias": dec_fc2_bias, "dec_head": dec_head}


@jax.custom_vjp
def low(v):
    return lax.optimization_barrier(v.astype(jnp.bfloat16)).astype(jnp.float32)

@jax.custom_vjp
def low_back(v):
    return v

def low_keep(v):
    return (low(v), None)

def low_pass(kept, grad):
    return (grad,)

def back_keep(v):
    return (v, None)

def back_low(kept, grad):
    return (low(grad),)
low.defvjp(low_keep, low_pass)
low_back.defvjp(back_keep, back_low)
NORM_EPS = 1e-06
PRECISE = lax.Precision.HIGHEST

def product(first_op, second_op):
    return jnp.dot(first_op, second_op, precision=PRECISE)

def layer_norm(values):
    centered = values - lax.optimization_barrier(jnp.mean(values, -1, keepdims=True))
    return centered * lax.rsqrt(lax.optimization_barrier(jnp.mean(centered * centered, -1, keepdims=True)) + NORM_EPS)

def mod_norm(values, gamma, beta):
    return layer_norm(values) * (1.0 + gamma) + beta

def attention(queries, key_rows, value_rows, head_count):
    query_len, width_all = queries.shape
    head_size = width_all // head_count
    q_heads = queries.reshape(query_len, head_count, head_size)
    k_heads = key_rows.reshape(key_rows.shape[0], head_count, head_size)
    v_heads = value_rows.reshape(value_rows.shape[0], head_count, head_size)
    scores = low_back(jnp.einsum('rhd,shd->hrs', q_heads, k_heads, precision=PRECISE) * head_size ** (-0.5))
    weights = low(jax.nn.softmax(scores, axis=-1))
    mixed = jnp.einsum('hrs,shd->rhd', weights, v_heads, precision=PRECISE)
    return low_back(low(mixed.reshape(query_len, width_all)))

def encoder(tokens_in, enc_w):
    ln1_gain, ln1_bias, enc_qkv, enc_qv_bias, enc_proj, enc_proj_bias, ln2_gain, ln2_bias, enc_fc1, enc_fc1_bias, enc_fc2, enc_fc2_bias = enc_w
    width_all = tokens_in.shape[1]
    normed = low(layer_norm(tokens_in) * ln1_gain + ln1_bias)
    bias_full = jnp.concatenate([enc_qv_bias[:width_all], jnp.zeros((width_all,), jnp.float32), enc_qv_bias[width_all:]])
    projected = product(normed, enc_qkv) + bias_full
    queries = low_back(low(projected[:, :width_all]))
    key_rows = low_back(low(projected[:, width_all:2 * width_all]))
    value_rows = low_back(low(projected[:, 2 * width_all:]))
    branch = attention(queries, key_rows, value_rows, ENC_HEADS)
    hidden = tokens_in + low_back(product(branch, enc_proj) + enc_proj_bias)
    normed_two = low(layer_norm(hidden) * ln2_gain + ln2_bias)
    pre_act = low_back(product(normed_two, enc_fc1) + enc_fc1_bias)
    activated = low(jax.nn.gelu(pre_act, approximate=False))
    return hidden + low_back(product(activated, enc_fc2) + enc_fc2_bias)

def ray_terms(final_rows, dec_head, target_rgb, foreground, valid_rays):
    predicted = product(final_rows, dec_head)
    colour = jax.nn.sigmoid(predicted[:, :3])
    residue = colour - jnp.transpose(target_rgb)
    opacity = predicted[:, 3]
    ray_loss = lax.optimization_barrier(jnp.sum(residue * residue, -1)) + jax.nn.softplus(opacity) - foreground * opacity
    return jnp.sum(valid_rays * ray_loss)

def decoder(triplane, image_rows, camera, target_rgb, foreground, valid_rays, dec_w):
    dec_mod, dec_qkv, dec_proj, dec_cross_q, dec_cross_kv, dec_cross_proj, dec_fc1, dec_fc1_bias, dec_fc2, dec_fc2_bias, dec_head = dec_w
    width_all = triplane.shape[1]
    modulation = product(camera[None, :], dec_mod).reshape(6, width_all)
    normed = low(mod_norm(triplane, modulation[0], modulation[1]))
    projected = product(normed, dec_qkv)
    queries = low_back(low(projected[:, :width_all]))
    key_rows = low_back(low(projected[:, width_all:2 * width_all]))
    value_rows = low_back(low(projected[:, 2 * width_all:]))
    after_self = triplane + low_back(product(attention(queries, key_rows, value_rows, DEC_HEADS), dec_proj))
    normed_two = low(mod_norm(after_self, modulation[2], modulation[3]))
    cross_queries = low_back(low(product(normed_two, dec_cross_q)))
    cross_both = product(image_rows, dec_cross_kv)
    cross_keys = low_back(low(cross_both[:, :width_all]))
    cross_values = low_back(low(cross_both[:, width_all:]))
    after_cross = after_self + low_back(product(attention(cross_queries, cross_keys, cross_values, DEC_HEADS), dec_cross_proj))
    normed_three = low(mod_norm(after_cross, modulation[4], modulation[5]))
    pre_act = low_back(product(normed_three, dec_fc1) + dec_fc1_bias)
    activated = low(jax.nn.gelu(pre_act, approximate=False))
    final_rows = after_cross + low_back(product(activated, dec_fc2) + dec_fc2_bias)
    return ray_terms(final_rows, dec_head, target_rgb, foreground, valid_rays)

def reference(img_in, tri_in, cam, targets, fg_mask, counts, ln1_gain, ln1_bias, enc_qkv, enc_qv_bias, enc_proj, enc_proj_bias, ln2_gain, ln2_bias, enc_fc1, enc_fc1_bias, enc_fc2, enc_fc2_bias, dec_mod, dec_qkv, dec_proj, dec_cross_q, dec_cross_kv, dec_cross_proj, dec_fc1, dec_fc1_bias, dec_fc2, dec_fc2_bias, dec_head):
    enc_w = tuple((weight.astype(jnp.float32) for weight in (ln1_gain, ln1_bias, enc_qkv, enc_qv_bias, enc_proj, enc_proj_bias, ln2_gain, ln2_bias, enc_fc1, enc_fc1_bias, enc_fc2, enc_fc2_bias)))
    dec_w = tuple((weight.astype(jnp.float32) for weight in (dec_mod, dec_qkv, dec_proj, dec_cross_q, dec_cross_kv, dec_cross_proj, dec_fc1, dec_fc1_bias, dec_fc2, dec_fc2_bias, dec_head)))
    ray_slots = TRI_TOK // VIEWS
    positions = jnp.arange(TRI_TOK, dtype=jnp.int32)
    view_index = positions // ray_slots
    slot_index = positions % ray_slots
    view_ids = jnp.arange(VIEWS, dtype=jnp.int32)
    limits = lax.optimization_barrier(jnp.sum(jnp.where(view_index[None, :, None] == view_ids[None, None, :], counts[:, None, :], 0), -1))
    valid_all = (slot_index[None, :] < limits).astype(jnp.float32)
    foreground = fg_mask.astype(jnp.float32)

    def whole(enc_params, dec_params, image_in, plane_in):

        def per_object(carry, pieces):
            tokens_in, plane, camera, target_rgb, fore_rays, valid_rays = pieces
            sent = low_back(low(encoder(tokens_in, enc_params)))
            return (carry + decoder(plane, sent, camera, target_rgb, fore_rays, valid_rays, dec_params), None)
        summed, _ = lax.scan(jax.checkpoint(per_object), jnp.zeros((), jnp.float32), (image_in, plane_in, cam, targets, foreground, valid_all))
        return summed
    total, pullback = jax.vjp(whole, enc_w, dec_w, img_in.astype(jnp.float32), tri_in.astype(jnp.float32))
    enc_grads, dec_grads, img_grad, tri_grad = pullback(jnp.ones((), jnp.float32))
    loss = total / jnp.sum(valid_all)
    return (loss, img_grad, tri_grad, enc_grads[0], enc_grads[1], enc_grads[2], enc_grads[3], enc_grads[4], enc_grads[5], enc_grads[6], enc_grads[7], enc_grads[8], enc_grads[9], enc_grads[10], enc_grads[11], dec_grads[0], dec_grads[1], dec_grads[2], dec_grads[3], dec_grads[4], dec_grads[5], dec_grads[6], dec_grads[7], dec_grads[8], dec_grads[9], dec_grads[10])
```

```python
import functools
import types

import jax
import jax.numpy as jnp
from jax import lax
from jax.experimental import pallas as pl
from jax.experimental.pallas import tpu as pltpu
from jax.sharding import PartitionSpec as P

HEAD = 64
VIEWS = 4
NORM_EPS = 1e-06
PRECISE = lax.Precision.HIGHEST
F32 = jnp.float32
BF16 = jnp.bfloat16
MIB = 1 << 20
VMEM = pl.BlockSpec(memory_space=pltpu.VMEM)
HBM = pl.BlockSpec(memory_space=pl.ANY)
MESH = pl.DeviceIdType.MESH
BLOCKS = ("wide", "narrow")


def shape_of(shape, dtype):
    return jax.ShapeDtypeStruct(shape, dtype)


def to_bf16(value):
    return value.astype(BF16)


def dot_plain(a, b):
    return jnp.dot(a, b, preferred_element_type=F32)


def dot_right(a, b):
    return lax.dot_general(a, b, (((1,), (1,)), ((), ())), preferred_element_type=F32)


def dot_left(a, b):
    return lax.dot_general(a, b, (((0,), (0,)), ((), ())), preferred_element_type=F32)


class Crew:
    def __init__(self, send, recv, here, lines):
        self.send_sems, self.recv_sems, self.here_sems = send, recv, here
        self.used = self.kept = 0
        self.sent = []
        self.group = lax.axis_index("grp")
        self.wide = lax.axis_index("wide")
        self.narrow = lax.axis_index("narrow")
        self.at_core = self.narrow + 1 - 2 * lax.rem(self.narrow, 2)
        self.at_row = lax.rem(self.narrow + 2, 4)
        self.at_cross = lax.rem(self.at_core + 2, 4)
        self.grp = {"grp": 1 - self.group}
        self.core = {"narrow": self.at_core}
        self.row = {"narrow": self.at_row}
        self.places = [lax.rem(self.wide + d, 4) for d in (1, 2, 3)] if lines else []
        self.line = [{"wide": place} for place in self.places]

    def greet(self):
        barrier = pltpu.get_barrier_semaphore()
        targets = [self.grp, self.core, self.row] + self.line
        for target in targets:
            pl.semaphore_signal(barrier, inc=1, device_id=target, device_id_type=MESH)
        pl.semaphore_wait(barrier, len(targets))

    def send(self, source, landing, target):
        copy = pltpu.make_async_remote_copy(
            src_ref=source,
            dst_ref=landing,
            send_sem=self.send_sems.at[self.used],
            recv_sem=self.recv_sems.at[self.used],
            device_id=target,
            device_id_type=MESH,
        )
        self.used += 1
        self.sent.append(copy)
        copy.start()
        return copy

    def keep(self, source, landing):
        copy = pltpu.make_async_copy(source, landing, self.here_sems.at[self.kept])
        self.kept += 1
        copy.start()
        return copy

    def close(self):
        for copy in self.sent:
            copy.wait_send()


class Gather:
    def __init__(self, crew, piece, full, cut, buf):
        self.crew, self.piece, self.full, self.cut, self.buf = crew, piece, full, cut, buf
        self.steps = [self.start, self.turn, self.cross, self.finish]
        self.load = None

    def start(self):
        crew = self.crew
        source = self.piece.at[:, self.cut]
        own = self.full.at[crew.wide, crew.narrow, :, self.cut]
        self.own = crew.keep(source, own)
        self.lines = [crew.send(source, own, target) for target in crew.line]

    def turn(self):
        crew = self.crew
        self.own.wait()
        for copy in self.lines:
            copy.wait_recv()
        mine = self.full.at[:, crew.narrow, :, self.cut]
        self.row = crew.send(mine, mine, crew.row)
        self.core = crew.send(mine, mine, crew.core)

    def cross(self):
        crew = self.crew
        self.row.wait_recv()
        other = self.full.at[:, crew.at_row, :, self.cut]
        self.far = crew.send(other, other, crew.core)

    def finish(self):
        self.core.wait_recv()
        self.far.wait_recv()
        if self.buf is not None:
            self.load = self.crew.keep(
                self.full.at[:, :, :, self.cut], self.buf.at[:, :, :, self.cut]
            )


class Scatter:
    def __init__(self, crew, part, pair, single, lines, out):
        self.crew, self.part, self.pair, self.single, self.lines = crew, part, pair, single, lines
        self.out = out
        self.steps = [self.start, self.turn, self.along, self.over, self.finish]

    def start(self):
        crew, part = self.crew, self.part
        self.core = crew.send(part.at[:, crew.at_core], self.pair.at[0], crew.core)
        self.far = crew.send(part.at[:, crew.at_cross], self.pair.at[1], crew.core)

    def add(self, place, landing):
        part = self.part

        def one(i, carry):
            total = part[i, place].astype(F32) + landing[i].astype(F32)
            part[i, place] = total.astype(part.dtype)
            return carry

        lax.fori_loop(0, part.shape[0], one, 0)

    def turn(self):
        crew = self.crew
        self.far.wait_recv()
        self.add(crew.at_row, self.pair.at[1])
        self.row = crew.send(self.part.at[:, crew.at_row], self.single, crew.row)
        self.core.wait_recv()
        self.add(crew.narrow, self.pair.at[0])

    def along(self):
        crew, part = self.crew, self.part
        self.row.wait_recv()
        self.add(crew.narrow, self.single)
        self.copies = [
            crew.send(part.at[place, crew.narrow], self.lines.at[i], target)
            for i, (place, target) in enumerate(zip(crew.places, crew.line))
        ]

    def over(self):
        crew, part = self.crew, self.part
        for copy in self.copies:
            copy.wait_recv()
        total = part[crew.wide, crew.narrow].astype(F32)
        for i in range(3):
            total = total + self.lines[i].astype(F32)
        self.out[0] = total.astype(self.out.dtype)
        self.other = crew.send(self.out.at[0], self.out.at[1], crew.grp)

    def finish(self):
        self.other.wait_recv()


class Pipe:
    def __init__(self, ahead):
        self.ahead, self.queue, self.jobs = ahead, [], []

    def plan(self, job):
        job.at = 0
        self.queue.append(job)

    def begin(self, job):
        job.steps[0]()
        job.at = 1
        self.jobs.append(job)

    def fill(self):
        while self.queue and sum(job.at == 1 for job in self.jobs) < self.ahead:
            self.begin(self.queue.pop(0))

    def pump(self):
        fresh = False
        for job in list(self.jobs):
            if job.at == 1:
                if fresh:
                    continue
                fresh = True
            job.steps[job.at]()
            job.at += 1
            if job.at == len(job.steps):
                self.jobs.remove(job)
        self.fill()

    def need(self, job):
        while job.at < len(job.steps):
            self.pump()

    def drain(self):
        while self.jobs or self.queue:
            self.pump()


class Matrix:
    def __init__(self, buf, pipe):
        self.buf, self.pipe, self.jobs, self.load = buf, pipe, [], None

    def need(self, index=None):
        for i, job in enumerate(self.jobs):
            if index is None or index == i:
                self.pipe.need(job)
                if not getattr(job, "loaded", False):
                    job.load.wait()
                    job.loaded = True
        if self.load is not None:
            self.load.wait()
            self.load = None

    def cols(self, cut):
        value = self.buf[..., cut]
        return value.reshape(-1, value.shape[-1])

    def rows(self, i):
        if len(self.buf.shape) == 4:
            return self.buf[i].reshape(-1, self.buf.shape[3])
        height = self.buf.shape[0] // 4
        return self.buf[pl.ds(i * height, height), :]

    def half(self, index):
        if len(self.buf.shape) == 4:
            return self.buf[pl.ds(index * 2, 2)].reshape(-1, self.buf.shape[3])
        height = self.buf.shape[0] // 2
        return self.buf[pl.ds(pl.multiple_of(index * height, height), height), :]

    def all(self):
        return self.cols(slice(None))


class Part:
    def __init__(self, body, **named):
        self.body = body
        self.ins = named.get("ins", {})
        self.outs = named.get("outs", {})
        self.scratch = named.get("scratch", {})
        self.given = named.get("given", {})
        self.moved = named.get("moved", {})
        self.sums = named.get("sums", {})


def grad_scratch(rows, cols, dtype):
    return (
        pltpu.VMEM((2, 4, rows, cols), dtype),
        pltpu.VMEM((4, rows, cols), dtype),
        pltpu.VMEM((3, rows, cols), dtype),
    )


def run(parts, collective, lines, ahead=2, links=0, flops=0, moved=0, limit=61):
    arrays, in_specs, out_shapes, out_specs, scratch = [], [], [], [], []
    layout = []
    for part in parts:
        named = []
        for name, value in part.ins.items():
            arrays.append(value)
            in_specs.append(VMEM)
        for name, value in part.given.items():
            arrays.append(value)
            in_specs.append(HBM)
            scratch.append(pltpu.VMEM(value.shape, BF16))
        for name, (_, piece, _, loaded) in part.moved.items():
            arrays.append(piece)
            in_specs.append(HBM)
            shape = (4, 4) + piece.shape
            out_shapes.append(shape_of(shape, piece.dtype))
            out_specs.append(HBM)
            if loaded:
                scratch.append(pltpu.VMEM(shape, piece.dtype))
        for name, value in part.outs.items():
            out_shapes.append(value)
            out_specs.append(VMEM)
        for name, (rows, cols, weight, dtype) in part.sums.items():
            out_shapes.append(shape_of((2, rows, cols), dtype))
            out_specs.append(VMEM)
            scratch.extend(grad_scratch(rows, cols, dtype))
            if weight is None:
                scratch.append(pltpu.VMEM((4, 4, rows, cols), dtype))
        for name, value in part.scratch.items():
            scratch.append(value)
    n_in, n_out = len(arrays), len(out_shapes)
    count = max(links, 1)
    scratch = scratch + [pltpu.SemaphoreType.DMA((count,))] * 3

    def kernel(*refs):
        ins, outs = iter(refs[:n_in]), iter(refs[n_in : n_in + n_out])
        rest = iter(refs[n_in + n_out : -3])
        crew = Crew(*refs[-3:], lines)
        pipe = Pipe(ahead)
        crew.greet()
        planned, spaces, loads = [], [], []
        for part in parts:
            space = types.SimpleNamespace()
            for name in part.ins:
                setattr(space, name, next(ins))
            for name in part.given:
                matrix = Matrix(next(rest), pipe)
                loads.append((matrix, next(ins)))
                setattr(space, name, matrix)
            for name, (order, piece, cuts, loaded) in part.moved.items():
                source, full = next(ins), next(outs)
                buf = next(rest) if loaded else None
                matrix = Matrix(buf, pipe)
                setattr(space, name, matrix)
                for i, cut in enumerate(cuts):
                    job = Gather(crew, source, full, cut, buf)
                    matrix.jobs.append(job)
                    planned.append((order + 0.01 * i, job))
            for name in part.outs:
                setattr(space, name, next(outs))
            for name, (rows, cols, weight, dtype) in part.sums.items():
                out = next(outs)
                landings = [next(rest) for _ in range(3)]
                own = next(rest) if weight is None else getattr(space, weight).buf
                setattr(space, "d_" + name, Scatter(crew, own, *landings, out))
            for name in part.scratch:
                setattr(space, name, next(rest))
            spaces.append(space)
        for _, job in sorted(planned, key=lambda entry: entry[0]):
            pipe.plan(job)
        pipe.fill()
        for matrix, source in loads:
            matrix.load = crew.keep(source, matrix.buf)
        strands = [part.body(space, crew, pipe) for part, space in zip(parts, spaces)]
        while strands:
            for strand in list(strands):
                if next(strand, True):
                    strands.remove(strand)
        pipe.drain()
        for matrix, _ in loads:
            matrix.need()
        crew.close()

    results = pl.pallas_call(
        kernel,
        out_shape=out_shapes,
        in_specs=in_specs,
        out_specs=out_specs,
        scratch_shapes=scratch,
        compiler_params=pltpu.CompilerParams(
            vmem_limit_bytes=limit * MIB, collective_id=collective, has_side_effects=True
        ),
        cost_estimate=pl.CostEstimate(
            flops=int(flops), bytes_accessed=int(moved), transcendentals=0
        ),
    )(*arrays)
    results = iter(results)
    given = []
    for part in parts:
        space = types.SimpleNamespace()
        for name in part.moved:
            setattr(space, name, next(results))
        for name in part.outs:
            setattr(space, name, next(results))
        for name in part.sums:
            setattr(space, "d_" + name, next(results))
        given.append(space)
    return given


def normalise(x):
    centered = x - jnp.mean(x, -1, keepdims=True)
    scale = lax.rsqrt(jnp.mean(centered * centered, -1, keepdims=True) + NORM_EPS)
    return centered * scale, scale


def norm_back(values, gain, grad):
    xhat, scale = normalise(values)
    inner = grad * gain
    term = inner - jnp.mean(inner, -1, keepdims=True)
    term = term - xhat * jnp.mean(inner * xhat, -1, keepdims=True)
    return (
        term * scale,
        jnp.sum(grad * xhat, 0, keepdims=True),
        jnp.sum(grad, 0, keepdims=True),
    )


def column_sums(value):
    return jnp.sum(value.astype(F32), 0, keepdims=True)


def gelu_pair(pre):
    cdf = 0.5 * (1.0 + lax.erf(pre * 0.7071067811865476))
    return cdf, pre * cdf


def gelu_slope(pre):
    return gelu_pair(pre)[0] + pre * (0.3989422804014327 * jnp.exp(-0.5 * pre * pre))


def head_masks(rows):
    lane = lax.broadcasted_iota(jnp.int32, (rows, 2 * HEAD), 1)
    return [lane < HEAD, lane >= HEAD]


class Spread:
    def __init__(self, crew, keyvals):
        self.crew, self.keyvals = crew, keyvals
        self.row = crew.send(keyvals.at[0], keyvals.at[2], crew.row)
        self.core = crew.send(keyvals.at[0], keyvals.at[1], crew.core)

    def cross(self):
        self.row.wait_recv()
        self.far = self.crew.send(self.keyvals.at[2], self.keyvals.at[3], self.crew.core)

    def finish(self):
        self.core.wait_recv()
        self.far.wait_recv()


class Fold:
    def __init__(self, crew, dkeyvals, landing):
        self.crew, self.dkeyvals, self.landing = crew, dkeyvals, landing
        self.core = crew.send(dkeyvals.at[1], landing.at[0], crew.core)
        self.far = crew.send(dkeyvals.at[3], landing.at[1], crew.core)

    def turn(self):
        dkeyvals, landing = self.dkeyvals, self.landing
        self.far.wait_recv()
        dkeyvals[2] = (dkeyvals[2].astype(F32) + landing[1].astype(F32)).astype(BF16)
        self.row = self.crew.send(dkeyvals.at[2], landing.at[2], self.crew.row)

    def finish(self):
        landing = self.landing
        self.core.wait_recv()
        own = self.dkeyvals[0].astype(F32) + landing[0].astype(F32)
        self.row.wait_recv()
        return (own + landing[2].astype(F32)).astype(BF16)


def attend(q_ref, keyvals, out_ref, out_first, sums_ref, half, first, last):
    rows = q_ref.shape[0]
    masks = head_masks(rows)

    def pair(i, carry):
        cut = pl.ds(pl.multiple_of(i * 2 * HEAD, 2 * HEAD), 2 * HEAD)
        cut_v = pl.ds(pl.multiple_of(half + i * 2 * HEAD, 2 * HEAD), 2 * HEAD)
        q_now = q_ref[:, cut] * BF16(HEAD**-0.5)
        parts = []
        for a in range(2):
            q_head = jnp.where(masks[a], q_now, BF16(0))
            scores = [dot_right(keyvals[j, :, cut], q_head) for j in range(4)]
            top = functools.reduce(jnp.maximum, [jnp.max(s, 0, keepdims=True) for s in scores])
            total, mixed = 0.0, 0.0
            for j in range(4):
                e = jnp.exp(scores[j] - top)
                total = total + jnp.sum(e, 0, keepdims=True)
                mixed = mixed + dot_left(keyvals[j, :, cut_v], e.astype(BF16))
            parts.append(mixed[a * HEAD : (a + 1) * HEAD] * (1.0 / total))
            sums_ref[i, a : a + 1, :] = top + jnp.log(total)
        place = pl.ds(pl.multiple_of(out_first + i * 2 * HEAD, 2 * HEAD), 2 * HEAD)
        out_ref[:, place] = jnp.concatenate(parts, 0).T.astype(BF16)
        return carry

    lax.fori_loop(first, last, pair, 0)


def attend_back(q_ref, keyvals, sums_ref, g_ref, dq_ref, dkeyvals, half, first, last):
    rows = q_ref.shape[0]
    masks = head_masks(rows)

    def pair(i, carry):
        cut = pl.ds(pl.multiple_of(i * 2 * HEAD, 2 * HEAD), 2 * HEAD)
        cut_v = pl.ds(pl.multiple_of(half + i * 2 * HEAD, 2 * HEAD), 2 * HEAD)
        q_now = q_ref[:, cut] * BF16(HEAD**-0.5)
        parts, dk_first, dv_first = [], [], []
        for a in range(2):
            q_head = jnp.where(masks[a], q_now, BF16(0))
            g_head = jnp.where(masks[a], g_ref[:, cut], BF16(0))
            log_sum = sums_ref[i, a : a + 1, :]
            weights, dweights, delta = [], [], 0.0
            for j in range(4):
                p = jnp.exp(dot_right(keyvals[j, :, cut], q_head) - log_sum)
                dp = dot_right(keyvals[j, :, cut_v], g_head)
                delta = delta + jnp.sum(p * dp, 0, keepdims=True)
                weights.append(p)
                dweights.append(dp)
            mixed = 0.0
            for j in range(4):
                ds = (weights[j] * (dweights[j] - delta)).astype(BF16)
                dk = dot_plain(ds, q_head)
                dv = dot_plain(weights[j].astype(BF16), g_head)
                mixed = mixed + dot_left(keyvals[j, :, cut], ds)
                if a == 0:
                    dk_first.append(dk)
                    dv_first.append(dv)
                else:
                    dkeyvals[j, :, cut] = (dk_first[j] + dk).astype(BF16)
                    dkeyvals[j, :, cut_v] = (dv_first[j] + dv).astype(BF16)
            parts.append(mixed[a * HEAD : (a + 1) * HEAD] * HEAD**-0.5)
        dq_ref[:, cut] = jnp.concatenate(parts, 0).T.astype(BF16)
        return carry

    lax.fori_loop(first, last, pair, 0)


def own_cut(crew, half):
    return pl.ds(pl.multiple_of(crew.group * half, half), half)


def send_half(crew, buffer, half):
    cut = own_cut(crew, half)
    return crew.send(buffer.at[:, cut], buffer.at[:, cut], crew.grp)


def grad_into(job, pipe, x, grad):
    part = job.part
    wide, narrow, rows, cols = part.shape
    width = 512 if cols % 512 == 0 else 384
    turned = x[...].T
    for first in range(0, cols, width):
        cut = pl.ds(first, width)
        term = dot_plain(turned, grad[:, first : first + width])
        part[:, :, :, cut] = term.astype(part.dtype).reshape(wide, narrow, rows, width)
    pipe.begin(job)


def begin_part(cam, mod, small, enc_qkv, dec_qkv):
    width = mod.shape[1]
    depth = mod.shape[0]

    def body(r, crew, pipe):
        cams = r.cams
        copies = [
            crew.send(r.cam.at[place * 4 + crew.narrow], cams.at[crew.wide], target)
            for place, target in zip(crew.places, crew.line)
        ]
        cams[crew.wide] = r.cam[crew.wide * 4 + crew.narrow]
        for copy in copies:
            copy.wait_recv()
        rows = cams[...].reshape(4, cams.shape[2])[:, :depth]
        high = to_bf16(rows)
        left = rows - high.astype(F32)
        middle = to_bf16(left)
        low = to_bf16(left - middle.astype(F32))
        terms = [dot_plain(part, r.mod[...]) for part in (high, middle, low)]
        r.terms[...] = (terms[0] + (terms[1] + terms[2])).reshape(4, 1, width)
        copies = [
            crew.send(r.terms.at[place], r.landed.at[i], target)
            for i, (place, target) in enumerate(zip(crew.places, crew.line))
        ]
        for copy in copies:
            copy.wait_recv()
        r.held[0] = r.terms[crew.wide] + (r.landed[0] + r.landed[1] + r.landed[2])
        crew.send(r.held.at[0], r.held.at[1], crew.core).wait_recv()
        r.held[2] = r.held[0] + r.held[1]
        crew.send(r.held.at[2], r.held.at[3], crew.row).wait_recv()
        r.modulation[...] = r.held[2] + r.held[3]
        yield

    return Part(
        body,
        ins=dict(cam=cam, mod=mod),
        moved=dict(
            small=(0, small, [slice(None)], False),
            enc_qkv=(1, enc_qkv, [slice(None)], False),
            dec_qkv=(2, dec_qkv, [pl.ds(i * 512, 512) for i in range(3)], False),
        ),
        outs=dict(
            modulation=shape_of((1, width), F32),
            cams=shape_of((4, 1, 128), F32),
        ),
        scratch=dict(
            terms=pltpu.VMEM((4, 1, width), F32),
            landed=pltpu.VMEM((3, 1, width), F32),
            held=pltpu.VMEM((4, 1, width), F32),
        ),
    )


def encoder_part(x, params, given, moved, cross_half):
    rows, width = x.shape
    half = width // 2
    inner = params["bias_fc1"].shape[1]
    pairs = half // (2 * HEAD)

    def body(r, crew, pipe):
        x_now = r.x[...].astype(F32)
        normed = normalise(x_now)[0] * r.gain_one[...] + r.shift_one[...]
        r.normed_one[...] = to_bf16(normed)
        r.qkv.need()
        out = dot_plain(r.normed_one[...], r.qkv.all()) + r.bias_qkv[...]
        r.queries[...] = to_bf16(out[:, :half])
        r.keyvals[0] = to_bf16(out[:, half:])
        spread = Spread(crew, r.keyvals)
        yield
        spread.cross()
        pipe.pump()
        yield
        spread.finish()
        attend(r.queries, r.keyvals, r.attended, crew.group * half, r.sums, half, 0, pairs)
        copy = send_half(crew, r.attended, half)
        pipe.pump()
        yield
        r.proj.need()
        copy.wait_recv()
        hidden = r.x[...].astype(F32) + dot_plain(r.attended[...], r.proj.all())
        hidden = hidden + r.bias_proj[...]
        r.hidden[...] = hidden
        normed = normalise(hidden)[0] * r.gain_two[...] + r.shift_two[...]
        r.normed_two[...] = to_bf16(normed)
        r.fc1.need()
        step = inner // 4
        total = 0.0
        for i in range(4):
            cut = pl.ds(i * step, step)
            pre = dot_plain(r.normed_two[...], r.fc1.cols(cut)) + r.bias_fc1[:, cut]
            r.pre[:, cut] = pre
            act = to_bf16(gelu_pair(pre)[1])
            r.act[:, cut] = act
            if i == 0:
                r.fc2.need()
            total = total + dot_plain(act, r.fc2.rows(i))
        r.term[...] = to_bf16(total)
        copy = crew.send(r.term, r.landed, crew.grp)
        pipe.pump()
        yield
        copy.wait_recv()
        both = r.term[...].astype(F32) + r.landed[...].astype(F32)
        r.image[...] = to_bf16(r.hidden[...] + both + r.bias_fc2[...])
        r.cross_kv.need()
        r.cross_keyvals[0] = to_bf16(dot_plain(r.image[...], r.cross_kv.all()))
        spread = Spread(crew, r.cross_keyvals)
        yield
        spread.cross()
        yield
        spread.finish()

    ins = dict(x=x)
    ins.update(params)
    return Part(
        body,
        ins=ins,
        given=given,
        moved=moved,
        outs=dict(
            normed_one=shape_of((rows, width), BF16),
            queries=shape_of((rows, half), BF16),
            keyvals=shape_of((4, rows, width), BF16),
            attended=shape_of((rows, width), BF16),
            sums=shape_of((pairs, 2, rows), F32),
            hidden=shape_of((rows, width), F32),
            normed_two=shape_of((rows, width), BF16),
            pre=shape_of((rows, inner), F32),
            act=shape_of((rows, inner), BF16),
            image=shape_of((rows, width), BF16),
            cross_keyvals=shape_of((4, rows, 2 * cross_half), BF16),
        ),
        scratch=dict(term=pltpu.VMEM((rows, width), BF16), landed=pltpu.VMEM((rows, width), BF16)),
    )


def self_part(x, modulation, given, moved):
    rows, width = x.shape
    half = width // 2
    pairs = half // (2 * HEAD)

    def body(r, crew, pipe):
        normed = normalise(r.x[...].astype(F32))[0]
        r.normed_one[...] = to_bf16(normed * (1.0 + r.modulation[0:1]) + r.modulation[1:2])
        r.qkv.need()
        for i in range(3):
            cut = pl.ds(i * half, half)
            out = to_bf16(dot_plain(r.normed_one[...], r.qkv.cols(cut)))
            if i == 0:
                r.queries[...] = out
            else:
                r.keyvals[0, :, pl.ds((i - 1) * half, half)] = out
        spread = Spread(crew, r.keyvals)
        yield
        spread.cross()
        yield
        spread.finish()
        first = crew.group * half
        attend(r.queries, r.keyvals, r.attended, first, r.sums, half, 0, pairs // 2)
        pipe.pump()
        attend(r.queries, r.keyvals, r.attended, first, r.sums, half, pairs // 2, pairs)
        copy = send_half(crew, r.attended, half)
        pipe.pump()
        yield
        r.proj.need()
        copy.wait_recv()
        after = r.x[...].astype(F32) + dot_plain(r.attended[...], r.proj.all())
        r.after_self[...] = after
        normed = normalise(after)[0] * (1.0 + r.modulation[2:3]) + r.modulation[3:4]
        r.normed_two[...] = to_bf16(normed)
        r.cross_q.need()
        r.cross_queries[...] = to_bf16(dot_plain(r.normed_two[...], r.cross_q.all()))

    return Part(
        body,
        ins=dict(x=x, modulation=modulation),
        given=given,
        moved=moved,
        outs=dict(
            normed_one=shape_of((rows, width), BF16),
            queries=shape_of((rows, half), BF16),
            keyvals=shape_of((4, rows, width), BF16),
            attended=shape_of((rows, width), BF16),
            sums=shape_of((pairs, 2, rows), F32),
            after_self=shape_of((rows, width), F32),
            normed_two=shape_of((rows, width), BF16),
            cross_queries=shape_of((rows, half), BF16),
        ),
    )


def cross_part(queries, keyvals, after_self, modulation, bias_fc1, bias_fc2, given, moved):
    rows, width = after_self.shape
    half = width // 2
    pairs = half // (2 * HEAD)
    inner = bias_fc1.shape[1]

    def body(r, crew, pipe):
        first = crew.group * half
        attend(r.queries, r.keyvals, r.attended, first, r.sums, half, 0, pairs // 2)
        pipe.pump()
        attend(r.queries, r.keyvals, r.attended, first, r.sums, half, pairs // 2, pairs)
        copy = send_half(crew, r.attended, half)
        pipe.pump()
        r.proj.need()
        copy.wait_recv()
        after = r.after_self[...] + dot_plain(r.attended[...], r.proj.all())
        r.after_cross[...] = after
        normed = normalise(after)[0] * (1.0 + r.modulation[4:5]) + r.modulation[5:6]
        r.normed_three[...] = to_bf16(normed)
        step = inner // 4
        for i in range(4):
            if i % 2 == 0:
                r.fc1.need(i // 2)
            cut = pl.ds(i * step, step)
            pre = dot_plain(r.normed_three[...], r.fc1.cols(cut)) + r.bias_fc1[:, cut]
            r.pre[:, cut] = pre
            r.act[:, cut] = to_bf16(gelu_pair(pre)[1])
        copies = []
        for i in range(2):
            r.fc2.need(i)
            cut = pl.ds(i * half, half)
            r.term[:, cut] = to_bf16(dot_plain(r.act[...], r.fc2.cols(cut)))
            copies.append(crew.send(r.term.at[:, cut], r.landed.at[:, cut], crew.grp))
        for i, copy in enumerate(copies):
            cut = pl.ds(i * half, half)
            copy.wait_recv()
            both = r.term[:, cut].astype(F32) + r.landed[:, cut].astype(F32)
            r.final[:, cut] = r.after_cross[:, cut] + both + r.bias_fc2[:, cut]
        yield

    return Part(
        body,
        ins=dict(
            queries=queries,
            keyvals=keyvals,
            after_self=after_self,
            modulation=modulation,
            bias_fc1=bias_fc1,
            bias_fc2=bias_fc2,
        ),
        given=given,
        moved=moved,
        outs=dict(
            attended=shape_of((rows, width), BF16),
            sums=shape_of((pairs, 2, rows), F32),
            after_cross=shape_of((rows, width), F32),
            normed_three=shape_of((rows, width), BF16),
            pre=shape_of((rows, inner), F32),
            act=shape_of((rows, inner), BF16),
            final=shape_of((rows, width), F32),
        ),
        scratch=dict(term=pltpu.VMEM((rows, width), BF16), landed=pltpu.VMEM((rows, width), BF16)),
    )


def feed_back(r, grad):
    inner = r.pre.shape[1]
    step = inner // 4
    total = 0.0
    r.fc2.need()
    for i in range(4):
        cut = pl.ds(i * step, step)
        dact = dot_right(grad, r.fc2.rows(i))
        dpre = to_bf16(gelu_slope(r.pre[:, cut]) * dact)
        r.dpre[:, cut] = dpre
        r.pre_sums[:, cut] = column_sums(dpre)
        if i == 0:
            r.fc1.need()
        total = total + dot_right(dpre, r.fc1.cols(cut))
    return to_bf16(total)


def both_of(r):
    return r.term[...].astype(F32) + r.landed[...].astype(F32)


def cross_back_part(ins, given, sums):
    rows, width = ins["after_cross"].shape
    inner = ins["pre"].shape[1]
    held, image_width = ins["image"].shape
    half = width // 2
    pairs = half // (2 * HEAD)
    moving = bool(sums)

    def body(r, crew, pipe):
        r.branch[...] = to_bf16(r.grad[...])
        r.term[...] = feed_back(r, r.branch[...])
        copy = crew.send(r.term, r.landed, crew.grp)
        if moving:
            grad_into(r.d_fc2, pipe, r.act, r.branch)
            grad_into(r.d_fc1, pipe, r.normed_three, r.dpre)
        copy.wait_recv()
        gain = 1.0 + r.modulation[4:5]
        grad_in, r.gamma_three[...], r.beta_three[...] = norm_back(
            r.after_cross[...], gain, both_of(r)
        )
        after = r.grad[...] + grad_in
        r.grad_after[...] = after
        r.cross_branch[...] = to_bf16(after)
        r.proj.need()
        r.dattended[...] = to_bf16(dot_right(r.cross_branch[...], r.proj.half(crew.group)))
        pipe.pump()
        args = (r.queries, r.keyvals, r.sums, r.dattended, r.cross_dq, r.dkeyvals, half)
        attend_back(*args, 0, pairs // 2)
        pipe.pump()
        attend_back(*args, pairs // 2, pairs)
        fold = Fold(crew, r.dkeyvals, r.landing)
        r.cross_q.need()
        r.term_two[...] = to_bf16(dot_right(r.cross_dq[...], r.cross_q.all()))
        copy = crew.send(r.term_two, r.landed_two, crew.grp)
        fold.turn()
        pipe.pump()
        copy.wait_recv()
        gain = 1.0 + r.modulation[2:3]
        both = r.term_two[...].astype(F32) + r.landed_two[...].astype(F32)
        grad_in, r.gamma_two[...], r.beta_two[...] = norm_back(r.after_self[...], gain, both)
        r.cross_dkv[...] = fold.finish()
        r.cross_kv.need()
        r.term_image[...] = to_bf16(dot_right(r.cross_dkv[...], r.cross_kv.all()))
        copy = crew.send(r.term_image, r.landed_image, crew.grp)
        r.grad_self[...] = r.grad_after[...] + grad_in
        pipe.pump()
        copy.wait_recv()
        both = r.term_image[...].astype(F32) + r.landed_image[...].astype(F32)
        r.image_grad[...] = to_bf16(both)
        yield

    outs = dict(
        pre_sums=shape_of((1, inner), F32),
        gamma_three=shape_of((1, width), F32),
        beta_three=shape_of((1, width), F32),
        gamma_two=shape_of((1, width), F32),
        beta_two=shape_of((1, width), F32),
        cross_branch=shape_of((rows, width), BF16),
        cross_dq=shape_of((rows, half), BF16),
        cross_dkv=shape_of((held, width), BF16),
        grad_self=shape_of((rows, width), F32),
        image_grad=shape_of((held, image_width), BF16),
    )
    wide_row = pltpu.VMEM((rows, width), BF16)
    scratch = dict(
        branch=wide_row,
        term=wide_row,
        landed=wide_row,
        term_two=wide_row,
        landed_two=wide_row,
        grad_after=pltpu.VMEM((rows, width), F32),
        dattended=pltpu.VMEM((rows, half), BF16),
        dkeyvals=pltpu.VMEM((4, held, width), BF16),
        landing=pltpu.VMEM((3, held, width), BF16),
        term_image=pltpu.VMEM((held, image_width), BF16),
        landed_image=pltpu.VMEM((held, image_width), BF16),
    )
    if moving:
        scratch.update(dpre=pltpu.VMEM((rows, inner), BF16))
    else:
        outs.update(dpre=shape_of((rows, inner), BF16))
    return Part(body, ins=ins, given=given, sums=sums, outs=outs, scratch=scratch)


def self_back_part(ins, given, sums):
    rows, width = ins["x"].shape
    half = width // 2
    pairs = half // (2 * HEAD)
    moving = bool(sums)

    def body(r, crew, pipe):
        r.branch[...] = to_bf16(r.grad_self[...])
        r.proj.need()
        r.dattended[...] = to_bf16(dot_right(r.branch[...], r.proj.half(crew.group)))
        if moving:
            grad_into(
                r.d_cross_proj,
                pipe,
                r.cross_attended,
                r.cross_branch[:, own_cut(crew, half)],
            )
            grad_into(r.d_cross_q, pipe, r.normed_two, r.cross_dq)
            grad_into(r.d_cross_kv, pipe, r.image, r.cross_dkv)
        yield
        args = (r.queries, r.keyvals, r.sums, r.dattended, r.dq, r.dkeyvals, half)
        attend_back(*args, 0, pairs // 2)
        pipe.pump()
        attend_back(*args, pairs // 2, pairs)
        fold = Fold(crew, r.dkeyvals, r.landing)
        if moving:
            grad_into(r.d_proj, pipe, r.attended, r.branch[:, own_cut(crew, half)])
        yield
        fold.turn()
        r.drows[:, pl.ds(0, half)] = r.dq[...]
        pipe.pump()
        yield
        r.drows[:, pl.ds(half, 2 * half)] = fold.finish()
        r.qkv.need()
        r.term[...] = to_bf16(dot_right(r.drows[...], r.qkv.all()))
        copy = crew.send(r.term, r.landed, crew.grp)
        if moving:
            grad_into(r.d_qkv, pipe, r.normed_one, r.drows)
        yield
        copy.wait_recv()
        gain = 1.0 + r.modulation[0:1]
        grad_in, r.gamma_one[...], r.beta_one[...] = norm_back(
            r.x[...].astype(F32), gain, both_of(r)
        )
        r.x_grad[...] = r.grad_self[...] + grad_in

    outs = dict(
        gamma_one=shape_of((1, width), F32),
        beta_one=shape_of((1, width), F32),
        x_grad=shape_of((rows, width), F32),
    )
    wide_row = pltpu.VMEM((rows, width), BF16)
    scratch = dict(
        term=wide_row,
        landed=wide_row,
        dattended=pltpu.VMEM((rows, half), BF16),
        dq=pltpu.VMEM((rows, half), BF16),
        dkeyvals=pltpu.VMEM((4, rows, width), BF16),
        landing=pltpu.VMEM((3, rows, width), BF16),
    )
    if moving:
        scratch.update(branch=wide_row, drows=pltpu.VMEM((rows, 3 * half), BF16))
    else:
        outs.update(
            branch=shape_of((rows, width), BF16), drows=shape_of((rows, 3 * half), BF16)
        )
    return Part(body, ins=ins, given=given, sums=sums, outs=outs, scratch=scratch)


def encoder_back_part(ins, given, sums):
    rows, width = ins["x"].shape
    half = width // 2
    pairs = half // (2 * HEAD)
    inner = ins["pre"].shape[1]
    moving = bool(sums)

    def body(r, crew, pipe):
        r.term[...] = feed_back(r, r.image_grad[...])
        copy = crew.send(r.term, r.landed, crew.grp)
        if moving:
            grad_into(r.d_fc2, pipe, r.act, r.image_grad)
            grad_into(r.d_fc1, pipe, r.normed_two, r.dpre)
        yield
        copy.wait_recv()
        grad_in, r.gain_two_grad[...], r.shift_two_grad[...] = norm_back(
            r.hidden[...], r.gain_two[...], both_of(r)
        )
        grad_hidden = r.image_grad[...].astype(F32) + grad_in
        r.grad_hidden[...] = grad_hidden
        r.branch[...] = to_bf16(grad_hidden)
        r.branch_sums[...] = column_sums(r.branch[...])
        r.proj.need()
        r.dattended[...] = to_bf16(dot_right(r.branch[...], r.proj.half(crew.group)))
        pipe.pump()
        attend_back(
            r.queries, r.keyvals, r.sums, r.dattended, r.dq, r.dkeyvals, half, 0, pairs
        )
        fold = Fold(crew, r.dkeyvals, r.landing)
        if moving:
            grad_into(r.d_proj, pipe, r.attended, r.branch[:, own_cut(crew, half)])
        yield
        fold.turn()
        r.drows[:, pl.ds(0, half)] = r.dq[...]
        pipe.pump()
        yield
        r.drows[:, pl.ds(half, 2 * half)] = fold.finish()
        r.row_sums[...] = column_sums(r.drows[...])
        r.qkv.need()
        r.term_two[...] = to_bf16(dot_right(r.drows[...], r.qkv.all()))
        copy = crew.send(r.term_two, r.landed_two, crew.grp)
        if moving:
            grad_into(r.d_qkv, pipe, r.normed_one, r.drows)
        yield
        copy.wait_recv()
        both = r.term_two[...].astype(F32) + r.landed_two[...].astype(F32)
        grad_in, r.gain_one_grad[...], r.shift_one_grad[...] = norm_back(
            r.x[...].astype(F32), r.gain_one[...], both
        )
        r.x_grad[...] = r.grad_hidden[...] + grad_in

    vector = shape_of((1, width), F32)
    outs = dict(
        pre_sums=shape_of((1, inner), F32),
        gain_two_grad=vector,
        shift_two_grad=vector,
        branch_sums=vector,
        row_sums=shape_of((1, 3 * half), F32),
        gain_one_grad=vector,
        shift_one_grad=vector,
        x_grad=shape_of((rows, width), F32),
    )
    wide_row = pltpu.VMEM((rows, width), BF16)
    scratch = dict(
        term=wide_row,
        landed=wide_row,
        term_two=wide_row,
        landed_two=wide_row,
        grad_hidden=pltpu.VMEM((rows, width), F32),
        dattended=pltpu.VMEM((rows, half), BF16),
        dq=pltpu.VMEM((rows, half), BF16),
        dkeyvals=pltpu.VMEM((4, rows, width), BF16),
        landing=pltpu.VMEM((3, rows, width), BF16),
    )
    if moving:
        scratch.update(
            branch=wide_row,
            dpre=pltpu.VMEM((rows, inner), BF16),
            drows=pltpu.VMEM((rows, 3 * half), BF16),
        )
    else:
        outs.update(
            branch=shape_of((rows, width), BF16),
            dpre=shape_of((rows, inner), BF16),
            drows=shape_of((rows, 3 * half), BF16),
        )
    return Part(body, ins=ins, given=given, sums=sums, outs=outs, scratch=scratch)


def end_part(small, mods):
    width = mods.shape[1]

    def body(r, crew, pipe):
        r.d_small.part[...] = r.packed[...]
        pipe.begin(r.d_small)
        copy = crew.send(r.mods, r.held.at[0], crew.core)
        copy.wait_recv()
        r.held[1] = r.mods[...] + r.held[0]
        copy = crew.send(r.held.at[1], r.held.at[2], crew.row)
        pipe.pump()
        copy.wait_recv()
        r.held[3] = r.held[1] + r.held[2]
        r.everyone[crew.wide] = r.held[3]
        copies = [
            crew.send(r.held.at[3], r.everyone.at[crew.wide], target) for target in crew.line
        ]
        pipe.pump()
        for copy in copies:
            copy.wait_recv()
        yield

    return Part(
        body,
        ins=dict(packed=small, mods=mods),
        outs=dict(everyone=shape_of((4, 1, width), F32)),
        sums=dict(small=(small.shape[2], small.shape[3], None, F32)),
        scratch=dict(held=pltpu.VMEM((4, 1, width), F32)),
    )


def plain_grad(x, grad):
    term = to_bf16(dot_left(x, grad))
    return lax.psum_scatter(term, BLOCKS, scatter_dimension=0, tiled=True)


def take(value, index, axis):
    return lax.dynamic_index_in_dim(value, index, axis, False)


def ray_loss(final_rows, head_weight, target_rgb, foreground, valid_rays):
    predicted = jnp.dot(final_rows, head_weight, precision=PRECISE)
    colour = jax.nn.sigmoid(predicted[:, :3])
    residue = colour - jnp.swapaxes(target_rgb, 0, 1)
    opacity = predicted[:, 3]
    per_ray = jnp.sum(residue * residue, -1) + jax.nn.softplus(opacity) - foreground * opacity
    return jnp.sum(valid_rays * per_ray)


def local(
    img_in,
    tri_in,
    cam,
    targets,
    fg_mask,
    counts,
    ln1_gain,
    ln1_bias,
    enc_qkv,
    enc_qv_bias,
    enc_proj,
    enc_proj_bias,
    ln2_gain,
    ln2_bias,
    enc_fc1,
    enc_fc1_bias,
    enc_fc2,
    enc_fc2_bias,
    dec_mod,
    dec_qkv,
    dec_proj,
    dec_cross_q,
    dec_cross_kv,
    dec_cross_proj,
    dec_fc1,
    dec_fc1_bias,
    dec_fc2,
    dec_fc2_bias,
    dec_head,
):
    group = lax.axis_index("grp")
    wide = lax.axis_index("wide")
    narrow = lax.axis_index("narrow")
    wides = lax.axis_size("wide")
    blocks = wides * lax.axis_size("narrow")
    block = wide * lax.axis_size("narrow") + narrow
    moving = wides == 4
    enc_width = img_in.shape[2]
    plane_rows, dec_width = tri_in.shape[1:]
    enc_half, dec_half = enc_width // 2, dec_width // 2
    enc_ff, dec_ff = enc_fc1.shape[1], dec_fc1.shape[1]
    enc_inner, dec_inner = enc_ff // blocks // 2, dec_ff // blocks // 2
    mod_rows = dec_mod.shape[0]

    def columns(shard, parts, width):
        cut = take(shard.reshape(shard.shape[0], parts, 2, width), group, 2)
        return cut.reshape(shard.shape[0], parts * width)

    def half_rows(shard):
        return take(shard.reshape(2, shard.shape[0] // 2, shard.shape[1]), group, 0)

    small_parts = (
        ln1_gain,
        ln1_bias,
        enc_qv_bias,
        enc_proj_bias,
        ln2_gain,
        ln2_bias,
        enc_fc1_bias,
        enc_fc2_bias,
        dec_fc1_bias,
        dec_fc2_bias,
        dec_head.reshape(-1),
    )
    small = jnp.concatenate(small_parts)
    piece = types.SimpleNamespace(
        enc_qkv=columns(enc_qkv, 3, enc_half),
        dec_qkv=columns(dec_qkv, 3, dec_half),
        enc_proj=enc_proj,
        enc_fc1=columns(enc_fc1, blocks, enc_inner),
        enc_fc2=half_rows(enc_fc2),
        dec_proj=dec_proj,
        cross_q=columns(dec_cross_q, 1, dec_half),
        cross_kv=columns(dec_cross_kv, 2, dec_half),
        cross_proj=dec_cross_proj,
        dec_fc1=columns(dec_fc1, blocks, dec_inner),
        dec_fc2=half_rows(dec_fc2),
    )

    if moving:
        length = small.shape[0]
        padded = jnp.pad(small, (0, 16 * 128 - length)).reshape(16, 128)
        cam_blocks = jnp.pad(cam.reshape(blocks, 1, mod_rows), ((0, 0), (0, 0), (0, 128 - mod_rows)))
        (first,) = run(
            [begin_part(cam_blocks, dec_mod, padded, piece.enc_qkv, piece.dec_qkv)],
            1,
            True,
            links=64,
        )
        small_all = first.small.reshape(blocks, 16 * 128)[:, :length]
        modulation = first.modulation.reshape(6, dec_width)
        cam_cut = first.cams.reshape(4, 128)[:, :mod_rows]
        full = types.SimpleNamespace(enc_qkv=first.enc_qkv, dec_qkv=first.dec_qkv)
    else:
        small_all = lax.all_gather(small, BLOCKS, axis=0)
        cam_all = lax.all_gather(cam, "wide", axis=0, tiled=True)
        cam_cut = lax.dynamic_slice_in_dim(cam_all, block * mod_rows, mod_rows, 1)
        term = jnp.dot(cam_cut, dec_mod.astype(F32), precision=PRECISE)
        term = lax.psum(term, "narrow")
        modulation = lax.psum_scatter(term, "wide", scatter_dimension=0, tiled=True)
        modulation = modulation.reshape(6, dec_width)
        full = types.SimpleNamespace(
            **{
                name: lax.all_gather(value, BLOCKS, axis=0, tiled=True)
                for name, value in vars(piece).items()
            }
        )
    unpacked, offset = [], 0
    for part in small_parts:
        length = part.shape[0]
        unpacked.append(small_all[:, offset : offset + length].reshape(1, -1).astype(F32))
        offset += length
    (
        gain_one,
        shift_one,
        bias_qv,
        bias_proj,
        gain_two,
        shift_two,
        bias_fc1,
        bias_fc2,
        bias_dfc1,
        bias_dfc2,
        head_flat,
    ) = unpacked
    head = head_flat.reshape(dec_width, 4)
    qv_half = take(bias_qv.reshape(2, 2, enc_half), group, 1)
    bias_qkv = jnp.concatenate([qv_half[0], jnp.zeros((enc_half,), F32), qv_half[1]])
    bias_qkv = bias_qkv.reshape(1, -1)
    fc1_half = take(bias_fc1.reshape(blocks, 2, enc_inner), group, 1).reshape(1, -1)
    dfc1_half = take(bias_dfc1.reshape(blocks, 2, dec_inner), group, 1).reshape(1, -1)

    ray_slots = plane_rows * lax.axis_size("narrow") // VIEWS
    row_index = narrow * plane_rows + jnp.arange(plane_rows, dtype=jnp.int32)
    view_index, slot_index = row_index // ray_slots, row_index % ray_slots
    view_ids = jnp.arange(VIEWS, dtype=jnp.int32)
    limits = jnp.sum(jnp.where(view_index[:, None] == view_ids[None, :], counts, 0), -1)
    valid_rays = (slot_index < limits).astype(F32)
    foreground = fg_mask[0].astype(F32)

    every = [slice(None)]

    def split(given, moved):
        if moving:
            return given, moved
        for name, (_, value, _, _) in moved.items():
            given[name] = full_of(value)
        return given, {}

    def full_of(value):
        for name, known in vars(piece).items():
            if known is value:
                return getattr(full, name)
        raise KeyError

    enc_given, enc_moved = split(
        dict(qkv=full.enc_qkv),
        dict(
            proj=(0, piece.enc_proj, every, True),
            fc1=(1, piece.enc_fc1, every, True),
            fc2=(2, piece.enc_fc2, every, True),
            cross_kv=(5, piece.cross_kv, every, True),
        ),
    )
    self_given, self_moved = split(
        dict(qkv=full.dec_qkv),
        dict(proj=(3, piece.dec_proj, every, True), cross_q=(4, piece.cross_q, every, True)),
    )
    enc, own = run(
        [
            encoder_part(
                img_in[0],
                dict(
                    gain_one=gain_one,
                    shift_one=shift_one,
                    bias_qkv=bias_qkv,
                    bias_proj=bias_proj,
                    gain_two=gain_two,
                    shift_two=shift_two,
                    bias_fc1=fc1_half,
                    bias_fc2=bias_fc2,
                ),
                enc_given,
                enc_moved,
                dec_half,
            ),
            self_part(tri_in[0], modulation, self_given, self_moved),
        ],
        2,
        moving,
        links=64,
    )
    if moving:
        full.enc_proj, full.enc_fc1, full.enc_fc2 = enc.proj, enc.fc1, enc.fc2
        full.cross_kv, full.dec_proj, full.cross_q = enc.cross_kv, own.proj, own.cross_q
    pair_cuts = [pl.ds(0, dec_ff // 4), pl.ds(dec_ff // 4, dec_ff // 4)]
    cross_given, cross_moved = split(
        dict(),
        dict(
            proj=(0, piece.cross_proj, every, True),
            fc1=(1, piece.dec_fc1, pair_cuts, True),
            fc2=(2, piece.dec_fc2, [pl.ds(0, dec_half), pl.ds(dec_half, dec_half)], True),
        ),
    )
    (cross,) = run(
        [
            cross_part(
                own.cross_queries,
                enc.cross_keyvals,
                own.after_self,
                modulation,
                dfc1_half,
                bias_dfc2,
                cross_given,
                cross_moved,
            )
        ],
        3,
        moving,
        links=64,
    )
    if moving:
        full.cross_proj, full.dec_fc1, full.dec_fc2 = cross.proj, cross.fc1, cross.fc2

    def ray_total(rows_in, head_in):
        return ray_loss(rows_in, head_in, targets[0], foreground, valid_rays)

    total, ray_pull = jax.vjp(ray_total, cross.final, head)
    grad_final, grad_head = ray_pull(jnp.ones((), F32))

    def sums_of(**named):
        return named if moving else {}

    (late,) = run(
        [
            cross_back_part(
                dict(
                    grad=grad_final,
                    pre=cross.pre,
                    act=cross.act,
                    normed_three=cross.normed_three,
                    after_cross=cross.after_cross,
                    modulation=modulation,
                    queries=own.cross_queries,
                    keyvals=enc.cross_keyvals,
                    sums=cross.sums,
                    after_self=own.after_self,
                    image=enc.image,
                ),
                dict(
                    fc2=full.dec_fc2,
                    fc1=full.dec_fc1,
                    proj=full.cross_proj,
                    cross_q=full.cross_q,
                    cross_kv=full.cross_kv,
                ),
                sums_of(
                    fc2=(piece.dec_fc2.shape[0], dec_width, "fc2", BF16),
                    fc1=(piece.dec_fc1.shape[0], dec_ff // 2, "fc1", BF16),
                ),
            )
        ],
        4,
        moving,
        links=64,
    )
    self_rows, enc_rows = dec_qkv.shape[0], enc_qkv.shape[0]
    (front,) = run(
        [
            self_back_part(
                dict(
                    grad_self=late.grad_self,
                    attended=own.attended,
                    queries=own.queries,
                    keyvals=own.keyvals,
                    sums=own.sums,
                    normed_one=own.normed_one,
                    x=tri_in[0],
                    modulation=modulation,
                    cross_attended=cross.attended,
                    cross_branch=late.cross_branch,
                    normed_two=own.normed_two,
                    cross_dq=late.cross_dq,
                    image=enc.image,
                    cross_dkv=late.cross_dkv,
                ),
                dict(proj=full.dec_proj, qkv=full.dec_qkv),
                sums_of(
                    cross_proj=(self_rows, dec_half, None, BF16),
                    cross_q=(self_rows, dec_half, None, BF16),
                    cross_kv=(enc_rows, dec_width, None, BF16),
                    proj=(self_rows, dec_half, None, BF16),
                    qkv=(self_rows, 3 * dec_half, "qkv", BF16),
                ),
            )
        ],
        5,
        moving,
        links=96,
    )
    (back,) = run(
        [
            encoder_back_part(
                dict(
                    image_grad=late.image_grad,
                    pre=enc.pre,
                    act=enc.act,
                    hidden=enc.hidden,
                    normed_one=enc.normed_one,
                    normed_two=enc.normed_two,
                    x=img_in[0],
                    attended=enc.attended,
                    queries=enc.queries,
                    keyvals=enc.keyvals,
                    sums=enc.sums,
                    gain_one=gain_one,
                    gain_two=gain_two,
                ),
                dict(
                    fc2=full.enc_fc2, fc1=full.enc_fc1, proj=full.enc_proj, qkv=full.enc_qkv
                ),
                sums_of(
                    fc2=(piece.enc_fc2.shape[0], enc_width, "fc2", BF16),
                    fc1=(enc_rows, enc_ff // 2, "fc1", BF16),
                    proj=(enc_rows, enc_half, None, BF16),
                    qkv=(enc_rows, 3 * enc_half, "qkv", BF16),
                ),
            )
        ],
        6,
        moving,
        links=96,
    )

    def placed(half, count, width):
        cut = half.reshape(count, 1, width)
        zero = jnp.zeros_like(cut)
        low = jnp.where(group == 0, cut, zero)
        high = jnp.where(group == 0, zero, cut)
        return jnp.concatenate([low, high], 1).reshape(-1)

    row_sums = back.row_sums[0]
    qv_sums = jnp.concatenate([row_sums[:enc_half], row_sums[2 * enc_half :]])
    loss_terms = jnp.stack([total, jnp.sum(valid_rays)])
    small_grads = (
        0.5 * back.gain_one_grad,
        0.5 * back.shift_one_grad,
        placed(qv_sums, 2, enc_half),
        0.5 * back.branch_sums,
        0.5 * back.gain_two_grad,
        0.5 * back.shift_two_grad,
        placed(back.pre_sums, blocks, enc_inner),
        0.5 * column_sums(late.image_grad),
        placed(late.pre_sums, blocks, dec_inner),
        0.5 * column_sums(to_bf16(grad_final)),
        0.5 * grad_head,
        jnp.tile(0.5 * loss_terms, blocks),
    )
    packed = jnp.concatenate([part.reshape(blocks, -1) for part in small_grads], 1)
    grad_mod = jnp.concatenate(
        [
            front.gamma_one,
            front.beta_one,
            late.gamma_two,
            late.beta_two,
            late.gamma_three,
            late.beta_three,
        ],
        1,
    )
    length = packed.shape[1]
    if moving:
        packed = jnp.pad(packed, ((0, 0), (0, 16 * 128 - length))).reshape(4, 4, 16, 128)
        (last,) = run([end_part(packed, grad_mod)], 7, True, links=32)
        small_sum = (last.d_small[0] + last.d_small[1]).reshape(-1)[:length]
        mod_all = last.everyone.reshape(4, -1)
    else:
        small_sum = take(lax.psum(packed, ("grp", "wide", "narrow")), block, 0)
        mod_all = lax.all_gather(lax.psum(grad_mod, "narrow"), "wide", axis=0, tiled=True)
    small_out, offset = [], 0
    for part in small_grads:
        count = part.size // blocks
        small_out.append(small_sum[offset : offset + count])
        offset += count
    loss = small_out[11][0] / small_out[11][1]
    grad_wmod = jnp.dot(jnp.transpose(cam_cut), mod_all, precision=PRECISE)

    def own_half(value):
        return take(value.reshape(value.shape[0], 2, -1), group, 1)

    def halves_of(reduced, x, grad):
        if not moving:
            half = plain_grad(x, grad)
            reduced = jnp.stack([half, lax.ppermute(half, "grp", [(0, 1), (1, 0)])])
        return jnp.where(group == 0, reduced, reduced[::-1]).astype(F32)

    def full_columns(halves, parts):
        cut = halves.reshape(2, halves.shape[1], parts, -1)
        return jnp.transpose(cut, (1, 2, 0, 3)).reshape(halves.shape[1], -1)

    def full_rows(halves):
        return halves.reshape(-1, halves.shape[2])

    def reduced_of(space, name):
        return getattr(space, name, None)

    if moving:
        self_branch = enc_branch = enc_dpre = dec_dpre = enc_drows = dec_drows = None
    else:
        self_branch, enc_branch = own_half(front.branch), own_half(back.branch)
        enc_dpre, dec_dpre, enc_drows, dec_drows = back.dpre, late.dpre, back.drows, front.drows
    cross_branch = own_half(late.cross_branch)
    get = reduced_of
    out_qkv = halves_of(get(back, "d_qkv"), enc.normed_one, enc_drows)
    out_proj = halves_of(get(back, "d_proj"), enc.attended, enc_branch)
    out_fc1 = halves_of(get(back, "d_fc1"), enc.normed_two, enc_dpre)
    out_fc2 = halves_of(get(back, "d_fc2"), enc.act, late.image_grad)
    out_dqkv = halves_of(get(front, "d_qkv"), own.normed_one, dec_drows)
    out_dproj = halves_of(get(front, "d_proj"), own.attended, self_branch)
    out_cq = halves_of(get(front, "d_cross_q"), own.normed_two, late.cross_dq)
    out_ckv = halves_of(get(front, "d_cross_kv"), enc.image, late.cross_dkv)
    out_cproj = halves_of(get(front, "d_cross_proj"), cross.attended, cross_branch)
    out_dfc1 = halves_of(get(late, "d_fc1"), cross.normed_three, dec_dpre)
    out_dfc2 = halves_of(get(late, "d_fc2"), cross.act, to_bf16(grad_final))

    return (
        loss,
        back.x_grad[None],
        front.x_grad[None],
        small_out[0],
        small_out[1],
        full_columns(out_qkv, 3),
        small_out[2],
        full_columns(out_proj, 1),
        small_out[3],
        small_out[4],
        small_out[5],
        full_columns(out_fc1, blocks),
        small_out[6],
        full_rows(out_fc2),
        small_out[7],
        grad_wmod,
        full_columns(out_dqkv, 3),
        full_columns(out_dproj, 1),
        full_columns(out_cq, 1),
        full_columns(out_ckv, 2),
        full_columns(out_cproj, 1),
        full_columns(out_dfc1, blocks),
        small_out[8],
        full_rows(out_dfc2),
        small_out[9],
        small_out[10].reshape(-1, 4),
    )


def solution(mesh):
    tokens = P("wide", "narrow", None)
    matrix = P(BLOCKS, None)
    vector = P(BLOCKS)
    objects = P("wide", None)
    rays = (P("wide", None, "narrow"), P("wide", "narrow"))
    encoder = (vector, vector, matrix, vector, matrix, vector, vector, vector, matrix, vector)
    encoder = encoder + (matrix, vector)
    decoder = (matrix,) * 7 + (vector, matrix, vector, matrix)
    return jax.shard_map(
        local,
        mesh=mesh,
        in_specs=(tokens, tokens, objects) + rays + (objects,) + encoder + decoder,
        out_specs=(P(), tokens, tokens) + encoder + decoder,
        check_vma=False,
    )
```

```python
import functools
import types

import jax
import jax.numpy as jnp
from jax import lax
from jax.experimental import pallas as pl
from jax.experimental.pallas import tpu as pltpu
from jax.sharding import PartitionSpec as P

HEAD = 64
VIEWS = 4
NORM_EPS = 1e-06
PRECISE = lax.Precision.HIGHEST
F32 = jnp.float32
BF16 = jnp.bfloat16
MIB = 1 << 20
VMEM = pl.BlockSpec(memory_space=pltpu.VMEM)
HBM = pl.BlockSpec(memory_space=pl.ANY)
MESH = pl.DeviceIdType.MESH
BLOCKS = ("wide", "narrow")


def shape_of(shape, dtype):
    return jax.ShapeDtypeStruct(shape, dtype)


def to_bf16(value):
    return value.astype(BF16)


def dot_plain(a, b):
    return jnp.dot(a, b, preferred_element_type=F32)


def dot_right(a, b):
    return lax.dot_general(a, b, (((1,), (1,)), ((), ())), preferred_element_type=F32)


def dot_left(a, b):
    return lax.dot_general(a, b, (((0,), (0,)), ((), ())), preferred_element_type=F32)


class Crew:
    def __init__(self, send, recv, here, lines):
        self.send_sems, self.recv_sems, self.here_sems = send, recv, here
        self.used = self.kept = self.slotted = self.given = 0
        self.credit = None
        self.sent = []
        self.group = lax.axis_index("grp")
        self.wide = lax.axis_index("wide")
        self.narrow = lax.axis_index("narrow")
        self.at_core = self.narrow + 1 - 2 * lax.rem(self.narrow, 2)
        self.at_row = lax.rem(self.narrow + 2, 4)
        self.at_cross = lax.rem(self.at_core + 2, 4)
        self.grp = {"grp": 1 - self.group}
        self.core = {"narrow": self.at_core}
        self.row = {"narrow": self.at_row}
        self.places = [lax.rem(self.wide + d, 4) for d in (1, 2, 3)] if lines else []
        self.line = [{"wide": place} for place in self.places]

    def greet(self):
        barrier = pltpu.get_barrier_semaphore()
        targets = [self.grp, self.core, self.row] + self.line
        for target in targets:
            pl.semaphore_signal(barrier, inc=1, device_id=target, device_id_type=MESH)
        pl.semaphore_wait(barrier, len(targets))

    def send(self, source, landing, target):
        copy = pltpu.make_async_remote_copy(
            src_ref=source,
            dst_ref=landing,
            send_sem=self.send_sems.at[self.used],
            recv_sem=self.recv_sems.at[self.used],
            device_id=target,
            device_id_type=MESH,
        )
        self.used += 1
        self.sent.append(copy)
        copy.start()
        return copy

    def keep(self, source, landing):
        copy = pltpu.make_async_copy(source, landing, self.here_sems.at[self.kept])
        self.kept += 1
        copy.start()
        return copy

    def close(self):
        for copy in self.sent:
            copy.wait_send()


class Gather:
    def __init__(self, crew, piece, full, cut, buf):
        self.crew, self.piece, self.full, self.cut, self.buf = crew, piece, full, cut, buf
        self.steps = [self.start, self.turn, self.cross, self.finish]
        self.load, self.late = None, False

    def start(self):
        crew = self.crew
        source = self.piece.at[:, self.cut]
        own = self.full.at[crew.wide, crew.narrow, :, self.cut]
        self.own = crew.keep(source, own)
        self.lines = [crew.send(source, own, target) for target in crew.line]

    def turn(self):
        crew = self.crew
        self.own.wait()
        for copy in self.lines:
            copy.wait_recv()
        mine = self.full.at[:, crew.narrow, :, self.cut]
        self.row = crew.send(mine, mine, crew.row)
        self.core = crew.send(mine, mine, crew.core)

    def cross(self):
        crew = self.crew
        self.row.wait_recv()
        other = self.full.at[:, crew.at_row, :, self.cut]
        self.far = crew.send(other, other, crew.core)

    def finish(self):
        self.core.wait_recv()
        self.far.wait_recv()
        if self.buf is not None and not self.late:
            self.fetch()

    def fetch(self):
        if self.load is None:
            self.load = self.crew.keep(
                self.full.at[:, :, :, self.cut], self.buf.at[:, :, :, self.cut]
            )


class GatherRow(Gather):
    def start(self):
        crew = self.crew
        source = self.piece.at[:, self.cut]
        own = self.full.at[crew.wide, crew.narrow, :, self.cut]
        self.row = crew.send(source, own, crew.row)
        self.own = crew.keep(source, own)
        self.lines = [crew.send(source, own, target) for target in crew.line]

    def turn(self):
        crew = self.crew
        self.row.wait_recv()
        other = self.full.at[crew.wide, crew.at_row, :, self.cut]
        self.lines += [crew.send(other, other, target) for target in crew.line]

    def cross(self):
        crew = self.crew
        self.own.wait()
        for copy in self.lines:
            copy.wait_recv()
        mine = self.full.at[:, crew.narrow, :, self.cut]
        other = self.full.at[:, crew.at_row, :, self.cut]
        self.core = crew.send(mine, mine, crew.core)
        self.far = crew.send(other, other, crew.core)


class GatherShared(Gather):
    def __init__(self, crew, piece, full, cut, buf):
        half = piece.shape[1] // 2
        mine = pl.ds(pl.multiple_of(crew.group * half, half), half)
        super().__init__(crew, piece, full, mine, buf)
        self.steps = [self.start, self.turn, self.over, self.cross, self.finish]

    def turn(self):
        crew = self.crew
        self.own.wait()
        for copy in self.lines:
            copy.wait_recv()
        mine = self.full.at[:, crew.narrow, :, self.cut]
        self.row = crew.send(mine, mine, crew.row)
        self.others = [crew.send(mine, mine, crew.grp)]

    def over(self):
        crew = self.crew
        self.row.wait_recv()
        other = self.full.at[:, crew.at_row, :, self.cut]
        self.others.append(crew.send(other, other, crew.grp))

    def cross(self):
        crew = self.crew
        for copy in self.others:
            copy.wait_recv()
        mine, other = self.full.at[:, crew.narrow], self.full.at[:, crew.at_row]
        self.core = crew.send(mine, mine, crew.core)
        self.far = crew.send(other, other, crew.core)
        self.cut = slice(None)


class Scatter:
    def __init__(self, crew, whole, cut, index):
        rows = whole.part.shape[2]
        self.crew, self.part, self.cut, self.index = crew, whole.part, cut, index
        self.pair = whole.slots.at[index % 2, :, :, pl.ds(0, rows), pl.ds(0, cut.size)]
        self.single = whole.single.at[:, :, cut]
        self.lines = whole.lines.at[:, :, cut]
        self.out = whole.out.at[:, :, cut]
        self.steps = [self.start, self.turn, self.along, self.over, self.finish]

    def start(self):
        crew, part = self.crew, self.part
        if self.index >= 2:
            pl.semaphore_wait(crew.credit, 1)
        self.core = crew.send(part.at[:, crew.at_core, :, self.cut], self.pair.at[0], crew.core)
        self.far = crew.send(part.at[:, crew.at_cross, :, self.cut], self.pair.at[1], crew.core)

    def add(self, place, landing):
        part, cut = self.part, self.cut

        def one(i, carry):
            total = part[i, place, :, cut].astype(F32) + landing[i].astype(F32)
            part[i, place, :, cut] = total.astype(part.dtype)
            return carry

        lax.fori_loop(0, part.shape[0], one, 0)

    def turn(self):
        crew = self.crew
        self.far.wait_recv()
        self.add(crew.at_row, self.pair.at[1])
        self.row = crew.send(self.part.at[:, crew.at_row, :, self.cut], self.single, crew.row)
        self.core.wait_recv()
        self.add(crew.narrow, self.pair.at[0])
        if self.index < crew.slotted - 2:
            pl.semaphore_signal(crew.credit, inc=1, device_id=crew.core, device_id_type=MESH)

    def along(self):
        crew, part = self.crew, self.part
        self.row.wait_recv()
        self.add(crew.narrow, self.single)
        self.copies = [
            crew.send(part.at[place, crew.narrow, :, self.cut], self.lines.at[i], target)
            for i, (place, target) in enumerate(zip(crew.places, crew.line))
        ]

    def over(self):
        crew, part = self.crew, self.part
        for copy in self.copies:
            copy.wait_recv()
        total = part[crew.wide, crew.narrow, :, self.cut].astype(F32)
        for i in range(3):
            total = total + self.lines[i].astype(F32)
        own = self.out.at[crew.group]
        own[...] = total.astype(part.dtype)
        self.other = crew.send(own, own, crew.grp)

    def finish(self):
        self.other.wait_recv()


class ScatterLine(Scatter):
    def __init__(self, crew, whole, cut, index):
        super().__init__(crew, whole, cut, index)
        self.steps = [self.start, self.turn, self.along, self.over, self.finish]

    def turn(self):
        crew, part = self.crew, self.part
        self.far.wait_recv()
        self.add(crew.at_row, self.pair.at[1])
        self.core.wait_recv()
        self.add(crew.narrow, self.pair.at[0])
        if self.index < crew.slotted - 2:
            pl.semaphore_signal(crew.credit, inc=1, device_id=crew.core, device_id_type=MESH)
        self.copies = [
            [
                crew.send(part.at[place, narrow, :, self.cut], landing.at[i], target)
                for i, (place, target) in enumerate(zip(crew.places, crew.line))
            ]
            for narrow, landing in ((crew.at_row, self.single), (crew.narrow, self.lines))
        ]

    def total(self, copies, narrow, landing):
        crew = self.crew
        for copy in copies:
            copy.wait_recv()
        total = self.part[crew.wide, narrow, :, self.cut].astype(F32)
        for i in range(3):
            total = total + landing[i].astype(F32)
        return total.astype(self.part.dtype)

    def along(self):
        crew, part = self.crew, self.part
        own = part.at[crew.wide, crew.at_row, :, self.cut]
        own[...] = self.total(self.copies[0], crew.at_row, self.single)
        self.row = crew.send(own, self.single.at[3], crew.row)

    def over(self):
        crew = self.crew
        total = self.total(self.copies[1], crew.narrow, self.lines)
        self.row.wait_recv()
        own = self.out.at[crew.group]
        total = total.astype(F32) + self.single[3].astype(F32)
        own[...] = total.astype(self.part.dtype)
        self.other = crew.send(own, own, crew.grp)


class Summed:
    def __init__(self, part, single, lines, out, slots, kind):
        self.part, self.single, self.lines, self.out, self.slots = part, single, lines, out, slots
        self.kind = kind


class Pipe:
    def __init__(self, ahead):
        self.ahead, self.queue, self.jobs, self.pending = ahead, [], [], None

    def plan(self, job):
        job.at = 0
        self.queue.append(job)

    def begin(self, job):
        job.steps[0]()
        job.at = 1
        self.jobs.append(job)

    def fill(self):
        while self.queue and sum(job.at == 1 for job in self.jobs) < self.ahead:
            self.begin(self.queue.pop(0))

    def settle(self):
        if self.pending is not None:
            self.pending.turn()
            self.pending.at = 2
            self.jobs.append(self.pending)
            self.pending = None

    def add(self, job):
        job.start()
        self.settle()
        self.pending = job

    def go(self, job):
        job.steps[job.at]()
        job.at += 1
        if job.at == len(job.steps):
            self.jobs.remove(job)

    def pump(self, lag=1):
        before = self.pending
        self.settle()
        waiting = {}
        for job in self.jobs:
            if job is not before:
                waiting.setdefault(job.at, []).append(job)
        for at in sorted(waiting, reverse=True):
            if at == 1 or len(waiting[at]) > lag:
                self.go(waiting[at][0])
        self.fill()

    def need(self, job):
        while job.at < len(job.steps):
            self.pump()
            if job.at and job.at < len(job.steps):
                self.go(job)

    def drain(self):
        while self.jobs or self.queue or self.pending is not None:
            self.pump(0)


class Matrix:
    def __init__(self, buf, pipe):
        self.buf, self.pipe, self.jobs, self.load = buf, pipe, [], None
        self.loaded = []

    def need(self, index=None):
        wanted = [job for i, job in enumerate(self.jobs) if index is None or index == i]
        for job in wanted:
            self.pipe.need(job)
        for job in self.jobs:
            if job.at == len(job.steps):
                job.fetch()
        for job in wanted:
            if job not in self.loaded:
                job.load.wait()
                self.loaded.append(job)
        if self.load is not None:
            self.load.wait()
            self.load = None

    def cols(self, cut):
        value = self.buf[..., cut]
        return value.reshape(-1, value.shape[-1])

    def rows(self, i):
        if len(self.buf.shape) == 4:
            return self.buf[i].reshape(-1, self.buf.shape[3])
        height = self.buf.shape[0] // 4
        return self.buf[pl.ds(i * height, height), :]

    def all(self):
        return self.cols(slice(None))


class Part:
    def __init__(self, body, **named):
        self.body = body
        self.ins = named.get("ins", {})
        self.far = named.get("far", {})
        self.outs = named.get("outs", {})
        self.scratch = named.get("scratch", {})
        self.given = named.get("given", {})
        self.links = named.get("links", {})
        self.late = named.get("late", {})
        self.halves = named.get("halves", {})
        self.moved = named.get("moved", {})
        self.sums = named.get("sums", {})


def cuts_of(piece):
    cols = piece.shape[1]
    width = width_of(cols)
    return [pl.ds(first, width) for first in range(0, cols, width)]


def width_of(cols):
    for width in (512, 384):
        if cols % width == 0:
            return width
    return cols


def grad_scratch(rows, cols, dtype):
    return pltpu.VMEM((4, rows, cols), dtype), pltpu.VMEM((3, rows, cols), dtype)


def run(parts, collective, lines, order=(), ahead=4, links=0, flops=0, moved=0, limit=63):
    arrays, in_specs, out_shapes, out_specs, scratch = [], [], [], [], []
    layout = []
    for part in parts:
        named = []
        for name, value in part.ins.items():
            arrays.append(value)
            in_specs.append(VMEM)
        for name, value in part.far.items():
            arrays.append(value)
            in_specs.append(HBM)
        for name, value in part.given.items():
            arrays.append(value)
            in_specs.append(HBM)
            scratch.append(pltpu.VMEM(value.shape, BF16))
        for name, value in part.halves.items():
            arrays.append(value)
            in_specs.append(HBM)
            scratch.append(pltpu.VMEM((value.shape[0] // 2,) + value.shape[1:], BF16))
        for name, (_, _, piece, _, loaded) in part.moved.items():
            arrays.append(piece)
            in_specs.append(HBM)
            shape = (4, 4) + piece.shape
            out_shapes.append(shape_of(shape, piece.dtype))
            out_specs.append(HBM)
            if loaded and name not in part.late:
                scratch.append(pltpu.VMEM(shape, piece.dtype))
        for name, value in part.outs.items():
            out_shapes.append(value)
            out_specs.append(VMEM)
        for name, (kind, rows, cols, weight, dtype) in part.sums.items():
            out_shapes.append(shape_of((2, rows, cols), dtype))
            out_specs.append(VMEM)
            scratch.extend(grad_scratch(rows, cols, dtype))
            if weight is None:
                scratch.append(pltpu.VMEM((4, 4, rows, cols), dtype))
        for name, value in part.scratch.items():
            scratch.append(value)
    n_in, n_out = len(arrays), len(out_shapes)
    count = max(links, 1)
    summed = [entry for part in parts for entry in part.sums.values()]
    slotted = sum(cols // width_of(cols) for _, _, cols, _, _ in summed)
    if summed:
        depth = max(rows for _, rows, _, _, _ in summed)
        span = max(width_of(cols) for _, _, cols, _, _ in summed)
        scratch.append(pltpu.VMEM((2, 2, 4, depth, span), summed[0][4]))
        scratch.append(pltpu.SemaphoreType.REGULAR)
    scratch = scratch + [pltpu.SemaphoreType.DMA((count,))] * 3

    def kernel(*refs):
        ins, outs = iter(refs[:n_in]), iter(refs[n_in : n_in + n_out])
        rest = iter(refs[n_in + n_out : -3])
        crew = Crew(*refs[-3:], lines)
        slots = None
        if summed:
            slots, crew.credit = refs[-5:-3]
            crew.slotted = slotted
        pipe = Pipe(ahead)
        crew.greet()
        planned, spaces, loads = [], [], []
        for part in parts:
            space = types.SimpleNamespace()
            for name in part.ins:
                setattr(space, name, next(ins))
            for name in part.far:
                setattr(space, name, next(ins))
            for name in part.given:
                matrix = Matrix(next(rest), pipe)
                loads.append((matrix, next(ins)))
                setattr(space, name, matrix)
            for name in part.halves:
                matrix = Matrix(next(rest), pipe)
                height = matrix.buf.shape[0]
                first = pl.multiple_of(crew.group * height, height)
                loads.append((matrix, next(ins).at[pl.ds(first, height)]))
                setattr(space, name, matrix)
            for name, (kind, rank, piece, cuts, loaded) in part.moved.items():
                source, full = next(ins), next(outs)
                buf = next(rest) if loaded and name not in part.late else None
                matrix = Matrix(buf, pipe)
                setattr(space, name, matrix)
                for i, cut in enumerate(cuts):
                    job = kind(crew, source, full, cut, buf)
                    matrix.jobs.append(job)
                    planned.append((rank + 0.01 * i, job))
            for name in part.outs:
                setattr(space, name, next(outs))
            for name, (kind, rows, cols, weight, dtype) in part.sums.items():
                out = next(outs)
                single, lines_in = next(rest), next(rest)
                own = next(rest) if weight is None else getattr(space, weight).buf
                setattr(space, "d_" + name, Summed(own, single, lines_in, out, slots, kind))
            for name in part.scratch:
                setattr(space, name, next(rest))
            spaces.append(space)
        for part, space in zip(parts, spaces):
            for name, (other, known) in part.links.items():
                setattr(space, name, getattr(spaces[parts.index(other)], known))
        for part, space in zip(parts, spaces):
            for name, (held, _) in part.late.items():
                cols = part.moved[name][2].shape[1]
                rows_in = part.moved[name][2].shape[0]
                matrix = getattr(space, name)
                matrix.buf = getattr(space, held).at[:, :, pl.ds(0, rows_in), pl.ds(0, cols)]
                for job in matrix.jobs:
                    job.buf, job.late = matrix.buf, part.late[name][1]
        for _, job in sorted(planned, key=lambda entry: entry[0]):
            pipe.plan(job)
        pipe.fill()
        for matrix, source in loads:
            matrix.load = crew.keep(source, matrix.buf)
        strands = [part.body(space, crew, pipe) for part, space in zip(parts, spaces)]
        for i in order:
            next(strands[i], None)
        while strands:
            for strand in list(strands):
                if next(strand, True):
                    strands.remove(strand)
        pipe.drain()
        for matrix, _ in loads:
            matrix.need()
        crew.close()

    results = pl.pallas_call(
        kernel,
        out_shape=out_shapes,
        in_specs=in_specs,
        out_specs=out_specs,
        scratch_shapes=scratch,
        compiler_params=pltpu.CompilerParams(
            vmem_limit_bytes=limit * MIB, collective_id=collective, has_side_effects=True
        ),
        cost_estimate=pl.CostEstimate(
            flops=int(flops), bytes_accessed=int(moved), transcendentals=0
        ),
    )(*arrays)
    results = iter(results)
    given = []
    for part in parts:
        space = types.SimpleNamespace()
        for name in part.moved:
            setattr(space, name, next(results))
        for name in part.outs:
            setattr(space, name, next(results))
        for name in part.sums:
            setattr(space, "d_" + name, next(results))
        given.append(space)
    return given


def normalise(x):
    centered = x - jnp.mean(x, -1, keepdims=True)
    scale = lax.rsqrt(jnp.mean(centered * centered, -1, keepdims=True) + NORM_EPS)
    return centered * scale, scale


def norm_back(values, gain, grad):
    xhat, scale = normalise(values)
    inner = grad * gain
    term = inner - jnp.mean(inner, -1, keepdims=True)
    term = term - xhat * jnp.mean(inner * xhat, -1, keepdims=True)
    return (
        term * scale,
        jnp.sum(grad * xhat, 0, keepdims=True),
        jnp.sum(grad, 0, keepdims=True),
    )


def column_sums(value):
    return jnp.sum(value.astype(F32), 0, keepdims=True)


def gelu_pair(pre):
    cdf = 0.5 * (1.0 + lax.erf(pre * 0.7071067811865476))
    return cdf, pre * cdf


def gelu_both(pre):
    cdf, act = gelu_pair(pre)
    return act, cdf + pre * (0.3989422804014327 * jnp.exp(-0.5 * pre * pre))


def head_masks(rows):
    lane = lax.broadcasted_iota(jnp.int32, (rows, 2 * HEAD), 1)
    return [lane < HEAD, lane >= HEAD]


class Spread:
    def __init__(self, crew, keyvals):
        self.crew, self.keyvals, self.copies = crew, keyvals, []

    def give(self, slot):
        copy = self.crew.send(
            self.keyvals.at[slot], self.keyvals.at[slot + 1], self.crew.core
        )
        self.copies.append(copy)

    def finish(self):
        for copy in self.copies:
            copy.wait_recv()


class Fold:
    def __init__(self, crew, dkeyvals, landing):
        self.crew, self.dkeyvals, self.landing = crew, dkeyvals, landing
        self.core = crew.send(dkeyvals.at[1], landing.at[0], crew.core)
        self.far = crew.send(dkeyvals.at[3], landing.at[1], crew.core)

    def turn(self):
        dkeyvals, landing = self.dkeyvals, self.landing
        self.far.wait_recv()
        dkeyvals[2] = (dkeyvals[2].astype(F32) + landing[1].astype(F32)).astype(BF16)
        self.row = self.crew.send(dkeyvals.at[2], landing.at[2], self.crew.row)

    def finish(self):
        landing = self.landing
        self.core.wait_recv()
        own = self.dkeyvals[0].astype(F32) + landing[0].astype(F32)
        self.row.wait_recv()
        return (own + landing[2].astype(F32)).astype(BF16)


def attend(q_ref, keyvals, out_ref, out_first, sums_ref, half, first, last):
    rows = q_ref.shape[0]
    masks = head_masks(rows)

    def pair(i, carry):
        cut = pl.ds(pl.multiple_of(i * 2 * HEAD, 2 * HEAD), 2 * HEAD)
        cut_v = pl.ds(pl.multiple_of(half + i * 2 * HEAD, 2 * HEAD), 2 * HEAD)
        q_now = q_ref[:, cut] * BF16(HEAD**-0.5)
        parts = []
        for a in range(2):
            q_head = jnp.where(masks[a], q_now, BF16(0))
            scores = [dot_right(keyvals[j, :, cut], q_head) for j in range(4)]
            top = functools.reduce(jnp.maximum, [jnp.max(s, 0, keepdims=True) for s in scores])
            total, mixed = 0.0, 0.0
            for j in range(4):
                e = jnp.exp(scores[j] - top)
                total = total + jnp.sum(e, 0, keepdims=True)
                mixed = mixed + dot_left(keyvals[j, :, cut_v], e.astype(BF16))
            parts.append(mixed[a * HEAD : (a + 1) * HEAD] * (1.0 / total))
            sums_ref[i, a : a + 1, :] = top + jnp.log(total)
        place = pl.ds(pl.multiple_of(out_first + i * 2 * HEAD, 2 * HEAD), 2 * HEAD)
        out_ref[:, place] = jnp.concatenate(parts, 0).T.astype(BF16)
        return carry

    lax.fori_loop(first, last, pair, 0)


def attend_back(q_ref, keyvals, sums_ref, g_ref, dq_ref, dkeyvals, half, first, last):
    rows = q_ref.shape[0]
    masks = head_masks(rows)

    def pair(i, carry):
        cut = pl.ds(pl.multiple_of(i * 2 * HEAD, 2 * HEAD), 2 * HEAD)
        cut_v = pl.ds(pl.multiple_of(half + i * 2 * HEAD, 2 * HEAD), 2 * HEAD)
        q_now = q_ref[:, cut] * BF16(HEAD**-0.5)
        parts, dk_first, dv_first = [], [], []
        for a in range(2):
            q_head = jnp.where(masks[a], q_now, BF16(0))
            g_head = jnp.where(masks[a], g_ref[:, cut], BF16(0))
            log_sum = sums_ref[i, a : a + 1, :]
            weights, dweights, delta = [], [], 0.0
            for j in range(4):
                p = jnp.exp(dot_right(keyvals[j, :, cut], q_head) - log_sum)
                dp = dot_right(keyvals[j, :, cut_v], g_head)
                delta = delta + jnp.sum(p * dp, 0, keepdims=True)
                weights.append(p)
                dweights.append(dp)
            mixed = 0.0
            for j in range(4):
                ds = (weights[j] * (dweights[j] - delta)).astype(BF16)
                dk = dot_plain(ds, q_head)
                dv = dot_plain(weights[j].astype(BF16), g_head)
                mixed = mixed + dot_left(keyvals[j, :, cut], ds)
                if a == 0:
                    dk_first.append(dk)
                    dv_first.append(dv)
                else:
                    dkeyvals[j, :, cut] = (dk_first[j] + dk).astype(BF16)
                    dkeyvals[j, :, cut_v] = (dv_first[j] + dv).astype(BF16)
            parts.append(mixed[a * HEAD : (a + 1) * HEAD] * HEAD**-0.5)
        dq_ref[:, cut] = jnp.concatenate(parts, 0).T.astype(BF16)
        return carry

    lax.fori_loop(first, last, pair, 0)


def own_cut(crew, half):
    return pl.ds(pl.multiple_of(crew.group * half, half), half)


def send_half(crew, buffer, half):
    cut = own_cut(crew, half)
    return crew.send(buffer.at[:, cut], buffer.at[:, cut], crew.grp)


def grad_into(crew, whole, pipe, x, grad):
    part = whole.part
    wide, narrow, rows, cols = part.shape
    width = width_of(cols)
    turned = x[...].T
    for first in range(0, cols, width):
        cut = pl.ds(first, width)
        term = dot_plain(turned, grad[:, first : first + width])
        part[:, :, :, cut] = term.astype(part.dtype).reshape(wide, narrow, rows, width)
        scatter(crew, whole, pipe, cut)


def scatter(crew, whole, pipe, cut):
    pipe.add(whole.kind(crew, whole, cut, crew.given))
    crew.given += 1


def laid(rows, count, first):
    span, cols = rows.shape[1], 16 * count

    def place_of(shape):
        col = lax.broadcasted_iota(jnp.int32, shape, 1)
        owner = jnp.floor((col.astype(F32) + 0.5) * (1.0 / count)).astype(jnp.int32)
        return owner, col - owner * count

    lane = lax.broadcasted_iota(jnp.int32, (span, cols), 0)
    pick = jnp.where(lane == place_of((span, cols))[1] + first, 1.0, 0.0)
    out = dot_plain(to_bf16(rows), to_bf16(pick))
    block = lax.broadcasted_iota(jnp.int32, (16, cols), 0)
    kept = jnp.where(block == place_of((16, cols))[0], out, 0.0)
    return jnp.sum(kept, 0, keepdims=True)


def begin_part(cam, mod, small, enc_width, dec_width, enc_inner, dec_inner):
    depth, width = mod.shape
    half = enc_width // 2

    def body(r, crew, pipe):
        cams = r.cams
        copies = [
            crew.send(r.cam.at[place * 4 + crew.narrow], cams.at[crew.wide], target)
            for place, target in zip(crew.places, crew.line)
        ]
        cams[crew.wide] = r.cam[crew.wide * 4 + crew.narrow]
        yield
        for copy in copies:
            copy.wait_recv()
        rows = cams[...].reshape(4, cams.shape[2])[:, :depth]
        high = to_bf16(rows)
        left = rows - high.astype(F32)
        middle = to_bf16(left)
        low = to_bf16(left - middle.astype(F32))
        terms = [dot_plain(part, r.mod[...]) for part in (high, middle, low)]
        r.terms[...] = (terms[0] + (terms[1] + terms[2])).reshape(4, 1, width)
        copies = [
            crew.send(r.terms.at[place], r.landed.at[i], target)
            for i, (place, target) in enumerate(zip(crew.places, crew.line))
        ]
        r.small.need()
        rows = r.small.buf[...].astype(F32).reshape(16, 16, 128)
        for i, name in enumerate(
            (r.gain_one, r.shift_one, r.bias_proj, r.gain_two, r.shift_two, r.bias_fc2)
        ):
            name[...] = laid(rows[:, i], enc_width // 16, 0)
        r.bias_qv[...] = laid(rows[:, 6], enc_width // 8, 0)
        for i in range(2):
            source = pl.ds(pl.multiple_of(i * enc_width + crew.group * half, half), half)
            r.bias_qkv[:, pl.ds(2 * i * half, half)] = r.bias_qv[:, source]
        r.bias_qkv[:, pl.ds(half, half)] = jnp.zeros((1, half), F32)
        for copy in copies:
            copy.wait_recv()
        r.held[0] = r.terms[crew.wide] + (r.landed[0] + r.landed[1] + r.landed[2])
        copy = crew.send(r.held.at[0], r.held.at[1], crew.core)
        two = jnp.concatenate([rows[:, 7], rows[:, 8]], 1)
        r.bias_fc1[...] = laid(two, enc_inner, crew.group * enc_inner)
        copy.wait_recv()
        r.held[2] = r.held[0] + r.held[1]
        copy = crew.send(r.held.at[2], r.held.at[3], crew.row)
        two = jnp.concatenate([rows[:, 9], rows[:, 10]], 1)
        r.bias_dfc1[...] = laid(two, dec_inner, crew.group * dec_inner)
        r.bias_dfc2[...] = laid(rows[:, 11], dec_width // 16, 0)
        copy.wait_recv()
        for i in range(6):
            cut = pl.ds(i * dec_width, dec_width)
            r.modulation[pl.ds(i, 1), :] = r.held[2, :, cut] + r.held[3, :, cut]

    vector = shape_of((1, enc_width), F32)
    return Part(
        body,
        ins=dict(cam=cam, mod=mod),
        moved=dict(small=(Gather, 0, small, [slice(None)], True)),
        outs=dict(
            modulation=shape_of((6, dec_width), F32),
            cams=shape_of((4, 1, 128), F32),
            gain_one=vector,
            gain_two=vector,
        ),
        scratch=dict(
            terms=pltpu.VMEM((4, 1, width), F32),
            landed=pltpu.VMEM((3, 1, width), F32),
            held=pltpu.VMEM((4, 1, width), F32),
            shift_one=pltpu.VMEM((1, enc_width), F32),
            shift_two=pltpu.VMEM((1, enc_width), F32),
            bias_proj=pltpu.VMEM((1, enc_width), F32),
            bias_fc2=pltpu.VMEM((1, enc_width), F32),
            bias_qv=pltpu.VMEM((1, 2 * enc_width), F32),
            bias_qkv=pltpu.VMEM((1, 3 * half), F32),
            bias_fc1=pltpu.VMEM((1, 16 * enc_inner), F32),
            bias_dfc1=pltpu.VMEM((1, 16 * dec_inner), F32),
            bias_dfc2=pltpu.VMEM((1, dec_width), F32),
        ),
    )


def encoder_part(x, params, links, given, moved, late, inner, cross_half):
    rows, width = x.shape
    half = width // 2
    pairs = half // (2 * HEAD)

    def body(r, crew, pipe):
        copy = crew.send(r.x, r.x_row, crew.row)
        yield
        x_now = r.x[...].astype(F32)
        normed = to_bf16(normalise(x_now)[0] * r.gain_one[...] + r.shift_one[...])
        r.normed_one[...] = normed
        copy.wait_recv()
        x_now = r.x_row[...].astype(F32)
        other = to_bf16(normalise(x_now)[0] * r.gain_one[...] + r.shift_one[...])
        r.qkv.need()
        weight = r.qkv.all()
        bias = r.bias_qkv[...]
        out = dot_plain(normed, weight) + bias
        r.queries[...] = to_bf16(out[:, :half])
        r.keyvals[0] = to_bf16(out[:, half:])
        spread = Spread(crew, r.keyvals)
        spread.give(0)
        r.keyvals[2] = to_bf16(dot_plain(other, weight[:, half:]) + bias[:, half:])
        spread.give(2)
        pipe.pump()
        yield
        spread.finish()
        attend(r.queries, r.keyvals, r.attended, crew.group * half, r.sums, half, 0, pairs)
        copy = send_half(crew, r.attended, half)
        pipe.pump()
        yield
        r.proj.need()
        copy.wait_recv()
        hidden = r.x[...].astype(F32) + dot_plain(r.attended[...], r.proj.all())
        hidden = hidden + r.bias_proj[...]
        r.hidden[...] = hidden
        normed = normalise(hidden)[0] * r.gain_two[...] + r.shift_two[...]
        r.normed_two[...] = to_bf16(normed)
        step = inner // 4
        total = 0.0
        for i in range(4):
            if i == 0:
                r.fc1.need()
            cut = pl.ds(i * step, step)
            pre = dot_plain(r.normed_two[...], r.fc1.cols(cut)) + r.bias_fc1[:, cut]
            r.pre[:, cut] = pre
            act = to_bf16(gelu_pair(pre)[1])
            if i == 0:
                r.fc2.need()
            total = total + dot_plain(act, r.fc2.rows(i))
        r.term[...] = to_bf16(total)
        copy = crew.send(r.term, r.landed, crew.grp)
        pipe.pump()
        yield
        copy.wait_recv()
        both = r.term[...].astype(F32) + r.landed[...].astype(F32)
        r.image[...] = to_bf16(r.hidden[...] + both + r.bias_fc2[...])
        copy = crew.send(r.image, r.x_row, crew.row)
        r.cross_kv.need()
        spread = Spread(crew, r.cross_keyvals)
        r.cross_keyvals[0] = to_bf16(dot_plain(r.image[...], r.cross_kv.all()))
        spread.give(0)
        yield
        copy.wait_recv()
        r.cross_keyvals[2] = to_bf16(dot_plain(r.x_row[...], r.cross_kv.all()))
        spread.give(2)
        yield
        spread.finish()

    ins = dict(x=x)
    ins.update(params)
    return Part(
        body,
        ins=ins,
        links=links,
        given=given,
        moved=moved,
        late=late,
        outs=dict(
            normed_one=shape_of((rows, width), BF16),
            queries=shape_of((rows, half), BF16),
            keyvals=shape_of((4, rows, width), BF16),
            attended=shape_of((rows, width), BF16),
            sums=shape_of((pairs, 2, rows), F32),
            hidden=shape_of((rows, width), F32),
            normed_two=shape_of((rows, width), BF16),
            pre=shape_of((rows, inner), F32),
            image=shape_of((rows, width), BF16),
            cross_keyvals=shape_of((4, rows, 2 * cross_half), BF16),
        ),
        scratch=dict(
            x_row=pltpu.VMEM((rows, width), BF16),
            term=pltpu.VMEM((rows, width), BF16),
            landed=pltpu.VMEM((rows, width), BF16),
        ),
    )


def self_part(x, params, links, given, moved, late, scratch):
    rows, width = x.shape
    half = width // 2
    pairs = half // (2 * HEAD)

    def body(r, crew, pipe):
        copy = crew.send(r.x, r.x_row, crew.row)
        yield
        gain, shift = 1.0 + r.modulation[0:1], r.modulation[1:2]
        r.normed_one[...] = to_bf16(normalise(r.x[...].astype(F32))[0] * gain + shift)
        copy.wait_recv()
        r.x_row[...] = to_bf16(normalise(r.x_row[...].astype(F32))[0] * gain + shift)
        spread = Spread(crew, r.keyvals)
        for i in (1, 2, 0):
            cut = pl.ds(i * half, half)
            r.qkv.need(i)
            if i == 0:
                r.queries[...] = to_bf16(dot_plain(r.normed_one[...], r.qkv.cols(cut)))
            else:
                place = pl.ds((i - 1) * half, half)
                r.keyvals[0, :, place] = to_bf16(
                    dot_plain(r.normed_one[...], r.qkv.cols(cut))
                )
                r.keyvals[2, :, place] = to_bf16(dot_plain(r.x_row[...], r.qkv.cols(cut)))
            if i == 2:
                spread.give(0)
                spread.give(2)
        pipe.pump()
        yield
        spread.finish()
        first = crew.group * half
        attend(r.queries, r.keyvals, r.attended, first, r.sums, half, 0, pairs // 2)
        pipe.pump()
        attend(r.queries, r.keyvals, r.attended, first, r.sums, half, pairs // 2, pairs)
        copy = send_half(crew, r.attended, half)
        pipe.pump()
        yield
        r.proj.need()
        copy.wait_recv()
        after = r.x[...].astype(F32) + dot_plain(r.attended[...], r.proj.all())
        r.after_self[...] = after
        normed = normalise(after)[0] * (1.0 + r.modulation[2:3]) + r.modulation[3:4]
        r.normed_two[...] = to_bf16(normed)
        r.cross_q.need()
        r.cross_queries[...] = to_bf16(dot_plain(r.normed_two[...], r.cross_q.all()))
        pipe.pump()

    ins = dict(x=x)
    ins.update(params)
    scratch = dict(scratch)
    scratch.update(x_row=pltpu.VMEM((rows, width), BF16))
    return Part(
        body,
        ins=ins,
        links=links,
        given=given,
        moved=moved,
        late=late,
        outs=dict(
            normed_one=shape_of((rows, width), BF16),
            queries=shape_of((rows, half), BF16),
            keyvals=shape_of((4, rows, width), BF16),
            attended=shape_of((rows, width), BF16),
            sums=shape_of((pairs, 2, rows), F32),
            after_self=shape_of((rows, width), F32),
            normed_two=shape_of((rows, width), BF16),
            cross_queries=shape_of((rows, half), BF16),
        ),
        scratch=scratch,
    )


def cross_part(rows, width, inner, ins, links, given, moved, late):
    half = width // 2
    pairs = half // (2 * HEAD)

    def body(r, crew, pipe):
        first = crew.group * half
        attend(r.queries, r.keyvals, r.attended, first, r.sums, half, 0, pairs // 2)
        pipe.pump()
        attend(r.queries, r.keyvals, r.attended, first, r.sums, half, pairs // 2, pairs)
        copy = send_half(crew, r.attended, half)
        pipe.pump()
        r.proj.need()
        copy.wait_recv()
        after = r.after_self[...] + dot_plain(r.attended[...], r.proj.all())
        r.after_cross[...] = after
        normed = normalise(after)[0] * (1.0 + r.modulation[4:5]) + r.modulation[5:6]
        r.normed_three[...] = to_bf16(normed)
        step = inner // 4
        for i in range(4):
            r.fc1.need(i)
            cut = pl.ds(i * step, step)
            pre = dot_plain(r.normed_three[...], r.fc1.cols(cut)) + r.bias_fc1[:, cut]
            r.pre[:, cut] = pre
            r.act[:, cut] = to_bf16(gelu_pair(pre)[1])
        copies = []
        for i in range(2):
            r.fc2.need(i)
            cut = pl.ds(i * half, half)
            r.term[:, cut] = to_bf16(dot_plain(r.act[...], r.fc2.cols(cut)))
            copies.append(crew.send(r.term.at[:, cut], r.landed.at[:, cut], crew.grp))
        for i, copy in enumerate(copies):
            cut = pl.ds(i * half, half)
            copy.wait_recv()
            both = r.term[:, cut].astype(F32) + r.landed[:, cut].astype(F32)
            r.final[:, cut] = r.after_cross[:, cut] + both + r.bias_fc2[:, cut]
        yield

    return Part(
        body,
        ins=ins,
        links=links,
        given=given,
        moved=moved,
        late=late,
        outs=dict(
            attended=shape_of((rows, width), BF16),
            sums=shape_of((pairs, 2, rows), F32),
            after_cross=shape_of((rows, width), F32),
            normed_three=shape_of((rows, width), BF16),
            pre=shape_of((rows, inner), F32),
            final=shape_of((rows, width), F32),
        ),
        scratch=dict(
            act=pltpu.VMEM((rows, inner), BF16),
            term=pltpu.VMEM((rows, width), BF16),
            landed=pltpu.VMEM((rows, width), BF16),
        ),
    )


def feed_back(r, grad):
    inner = r.pre.shape[1]
    step = inner // 4
    total = 0.0
    r.fc2.need()
    for i in range(4):
        cut = pl.ds(i * step, step)
        dact = dot_right(grad, r.fc2.rows(i))
        act, slope = gelu_both(r.pre[:, cut])
        r.act[:, cut] = to_bf16(act)
        dpre = to_bf16(slope * dact)
        r.dpre[:, cut] = dpre
        r.pre_sums[:, cut] = column_sums(dpre)
        if i == 0:
            r.fc1.need()
        total = total + dot_right(dpre, r.fc1.cols(cut))
    return to_bf16(total)


def both_of(r):
    return r.term[...].astype(F32) + r.landed[...].astype(F32)


def cross_back_part(ins, given, halves, sums):
    rows, width = ins["after_cross"].shape
    inner = ins["pre"].shape[1]
    held, image_width = ins["image"].shape
    half = width // 2
    pairs = half // (2 * HEAD)
    moving = bool(sums)

    def body(r, crew, pipe):
        r.branch[...] = to_bf16(r.grad[...])
        r.term[...] = feed_back(r, r.branch[...])
        copy = crew.send(r.term, r.landed, crew.grp)
        if moving:
            grad_into(crew, r.d_fc2, pipe, r.act, r.branch)
            grad_into(crew, r.d_fc1, pipe, r.normed_three, r.dpre)
        copy.wait_recv()
        gain = 1.0 + r.modulation[4:5]
        grad_in, r.gamma_three[...], r.beta_three[...] = norm_back(
            r.after_cross[...], gain, both_of(r)
        )
        after = r.grad[...] + grad_in
        r.grad_after[...] = after
        r.cross_branch[...] = to_bf16(after)
        r.proj.need()
        r.dattended[...] = to_bf16(dot_right(r.cross_branch[...], r.proj.all()))
        if moving:
            branch = r.cross_branch[:, own_cut(crew, half)]
            grad_into(crew, r.d_proj, pipe, r.attended, branch)
        pipe.pump()
        args = (r.queries, r.keyvals, r.sums, r.dattended, r.cross_dq, r.dkeyvals, half)
        attend_back(*args, 0, pairs // 2)
        pipe.pump()
        attend_back(*args, pairs // 2, pairs)
        fold = Fold(crew, r.dkeyvals, r.landing)
        r.cross_q.need()
        r.term_two[...] = to_bf16(dot_right(r.cross_dq[...], r.cross_q.all()))
        copy = crew.send(r.term_two, r.landed_two, crew.grp)
        fold.turn()
        if moving:
            grad_into(crew, r.d_cross_q, pipe, r.normed_two, r.cross_dq)
        pipe.pump()
        copy.wait_recv()
        gain = 1.0 + r.modulation[2:3]
        both = r.term_two[...].astype(F32) + r.landed_two[...].astype(F32)
        grad_in, r.gamma_two[...], r.beta_two[...] = norm_back(r.after_self[...], gain, both)
        r.cross_dkv[...] = fold.finish()
        r.cross_kv.need()
        r.term_image[...] = to_bf16(dot_right(r.cross_dkv[...], r.cross_kv.all()))
        copy = crew.send(r.term_image, r.landed_image, crew.grp)
        r.grad_self[...] = r.grad_after[...] + grad_in
        pipe.pump()
        copy.wait_recv()
        both = r.term_image[...].astype(F32) + r.landed_image[...].astype(F32)
        r.image_grad[...] = to_bf16(both)
        yield

    outs = dict(
        pre_sums=shape_of((1, inner), F32),
        gamma_three=shape_of((1, width), F32),
        beta_three=shape_of((1, width), F32),
        gamma_two=shape_of((1, width), F32),
        beta_two=shape_of((1, width), F32),
        cross_branch=shape_of((rows, width), BF16),
        cross_dq=shape_of((rows, half), BF16),
        cross_dkv=shape_of((held, width), BF16),
        grad_self=shape_of((rows, width), F32),
        image_grad=shape_of((held, image_width), BF16),
    )
    wide_row = pltpu.VMEM((rows, width), BF16)
    scratch = dict(
        branch=wide_row,
        term=wide_row,
        landed=wide_row,
        term_two=wide_row,
        landed_two=wide_row,
        grad_after=pltpu.VMEM((rows, width), F32),
        dattended=pltpu.VMEM((rows, half), BF16),
        dkeyvals=pltpu.VMEM((4, held, width), BF16),
        landing=pltpu.VMEM((3, held, width), BF16),
        term_image=pltpu.VMEM((held, image_width), BF16),
        landed_image=pltpu.VMEM((held, image_width), BF16),
    )
    if moving:
        scratch.update(
            act=pltpu.VMEM((rows, inner), BF16), dpre=pltpu.VMEM((rows, inner), BF16)
        )
    else:
        outs.update(act=shape_of((rows, inner), BF16), dpre=shape_of((rows, inner), BF16))
    return Part(
        body, ins=ins, given=given, halves=halves, sums=sums, outs=outs, scratch=scratch
    )


def self_back_part(ins, far, given, halves, sums):
    rows, width = far["x"].shape
    half = width // 2
    pairs = half // (2 * HEAD)
    moving = bool(sums)

    def body(r, crew, pipe):
        crew.keep(r.grad_self, r.x_grad).wait()
        branch = r.drows if moving else r.branch
        whole = pl.ds(0, width)
        branch[:, whole] = to_bf16(r.x_grad[...])
        r.proj.need()
        r.term[:, pl.ds(0, half)] = to_bf16(dot_right(branch[:, whole], r.proj.all()))
        if moving:
            grad_into(crew, r.d_proj, pipe, r.attended, branch[:, own_cut(crew, half)])
        if moving:
            grad_into(crew, r.d_cross_kv, pipe, r.image, r.cross_dkv)
        yield
        args = (r.queries, r.keyvals, r.sums, r.term, r.drows, r.dkeyvals, half)
        attend_back(*args, 0, pairs // 2)
        pipe.pump()
        attend_back(*args, pairs // 2, pairs)
        fold = Fold(crew, r.dkeyvals, r.landing)
        yield
        fold.turn()
        pipe.pump()
        yield
        r.drows[:, pl.ds(half, 2 * half)] = fold.finish()
        r.qkv.need()
        r.term[...] = to_bf16(dot_right(r.drows[...], r.qkv.all()))
        copy = crew.send(r.term, r.landed, crew.grp)
        if moving:
            grad_into(crew, r.d_qkv, pipe, r.normed_one, r.drows)
        held = (r.drows if moving else r.held).at[:, pl.ds(0, width)]
        fetch = crew.keep(r.x, held)
        yield
        fetch.wait()
        copy.wait_recv()
        gain = 1.0 + r.modulation[0:1]
        grad_in, r.gamma_one[...], r.beta_one[...] = norm_back(
            held[...].astype(F32), gain, both_of(r)
        )
        r.x_grad[...] += grad_in

    outs = dict(
        gamma_one=shape_of((1, width), F32),
        beta_one=shape_of((1, width), F32),
        x_grad=shape_of((rows, width), F32),
    )
    wide_row = pltpu.VMEM((rows, width), BF16)
    scratch = dict(
        term=wide_row,
        landed=wide_row,
        dkeyvals=pltpu.VMEM((4, rows, width), BF16),
        landing=pltpu.VMEM((3, rows, width), BF16),
    )
    if moving:
        scratch.update(drows=pltpu.VMEM((rows, 3 * half), BF16))
    else:
        scratch.update(held=wide_row)
        outs.update(
            branch=shape_of((rows, width), BF16), drows=shape_of((rows, 3 * half), BF16)
        )
    return Part(
        body, ins=ins, far=far, given=given, halves=halves, sums=sums, outs=outs, scratch=scratch
    )


def encoder_back_part(ins, far, given, halves, sums):
    rows, width = far["x"].shape
    half = width // 2
    pairs = half // (2 * HEAD)
    inner = ins["pre"].shape[1]
    moving = bool(sums)

    def body(r, crew, pipe):
        r.term[...] = feed_back(r, r.image_grad[...])
        copy = crew.send(r.term, r.landed, crew.grp)
        if moving:
            grad_into(crew, r.d_fc2, pipe, r.act, r.image_grad)
            grad_into(crew, r.d_fc1, pipe, r.normed_two, r.dpre)
        yield
        copy.wait_recv()
        grad_in, r.gain_two_grad[...], r.shift_two_grad[...] = norm_back(
            r.hidden[...], r.gain_two[...], both_of(r)
        )
        grad_hidden = r.image_grad[...].astype(F32) + grad_in
        r.x_grad[...] = grad_hidden
        branch = r.drows if moving else r.branch
        whole = pl.ds(0, width)
        branch[:, whole] = to_bf16(grad_hidden)
        r.branch_sums[...] = column_sums(branch[:, whole])
        r.proj.need()
        r.term_two[:, pl.ds(0, half)] = to_bf16(dot_right(branch[:, whole], r.proj.all()))
        if moving:
            grad_into(crew, r.d_proj, pipe, r.attended, branch[:, own_cut(crew, half)])
        pipe.pump()
        attend_back(
            r.queries, r.keyvals, r.sums, r.term_two, r.drows, r.dkeyvals, half, 0, pairs
        )
        fold = Fold(crew, r.dkeyvals, r.landing)
        yield
        fold.turn()
        pipe.pump()
        yield
        r.drows[:, pl.ds(half, 2 * half)] = fold.finish()
        r.row_sums[...] = column_sums(r.drows[...])
        r.qkv.need()
        r.term_two[...] = to_bf16(dot_right(r.drows[...], r.qkv.all()))
        copy = crew.send(r.term_two, r.landed_two, crew.grp)
        if moving:
            grad_into(crew, r.d_qkv, pipe, r.normed_one, r.drows)
        held = (r.drows if moving else r.held).at[:, pl.ds(0, width)]
        fetch = crew.keep(r.x, held)
        yield
        fetch.wait()
        copy.wait_recv()
        both = r.term_two[...].astype(F32) + r.landed_two[...].astype(F32)
        grad_in, r.gain_one_grad[...], r.shift_one_grad[...] = norm_back(
            held[...].astype(F32), r.gain_one[...], both
        )
        r.x_grad[...] += grad_in

    vector = shape_of((1, width), F32)
    outs = dict(
        pre_sums=shape_of((1, inner), F32),
        gain_two_grad=vector,
        shift_two_grad=vector,
        branch_sums=vector,
        row_sums=shape_of((1, 3 * half), F32),
        gain_one_grad=vector,
        shift_one_grad=vector,
        x_grad=shape_of((rows, width), F32),
    )
    wide_row = pltpu.VMEM((rows, width), BF16)
    scratch = dict(
        term=wide_row,
        landed=wide_row,
        term_two=wide_row,
        landed_two=wide_row,
        dkeyvals=pltpu.VMEM((4, rows, width), BF16),
        landing=pltpu.VMEM((3, rows, width), BF16),
    )
    if moving:
        scratch.update(
            act=pltpu.VMEM((rows, inner), BF16),
            dpre=pltpu.VMEM((rows, inner), BF16),
            drows=pltpu.VMEM((rows, 3 * half), BF16),
        )
    else:
        scratch.update(held=wide_row)
        outs.update(
            branch=shape_of((rows, width), BF16),
            act=shape_of((rows, inner), BF16),
            dpre=shape_of((rows, inner), BF16),
            drows=shape_of((rows, 3 * half), BF16),
        )
    return Part(
        body, ins=ins, far=far, given=given, halves=halves, sums=sums, outs=outs, scratch=scratch
    )


def end_part(small, mods):
    width = mods.shape[1]

    def body(r, crew, pipe):
        r.d_small.part[...] = r.packed[...]
        scatter(crew, r.d_small, pipe, pl.ds(0, 128))
        copy = crew.send(r.mods, r.held.at[0], crew.core)
        copy.wait_recv()
        r.held[1] = r.mods[...] + r.held[0]
        copy = crew.send(r.held.at[1], r.held.at[2], crew.row)
        pipe.pump()
        copy.wait_recv()
        r.held[3] = r.held[1] + r.held[2]
        r.everyone[crew.wide] = r.held[3]
        copies = [
            crew.send(r.held.at[3], r.everyone.at[crew.wide], target) for target in crew.line
        ]
        pipe.pump()
        for copy in copies:
            copy.wait_recv()
        yield

    return Part(
        body,
        ins=dict(packed=small, mods=mods),
        outs=dict(everyone=shape_of((4, 1, width), F32)),
        sums=dict(small=(Scatter, small.shape[2], small.shape[3], None, F32)),
        scratch=dict(held=pltpu.VMEM((4, 1, width), F32)),
    )


def plain_grad(x, grad):
    term = to_bf16(dot_left(x, grad))
    return lax.psum_scatter(term, BLOCKS, scatter_dimension=0, tiled=True)


def take(value, index, axis):
    return lax.dynamic_index_in_dim(value, index, axis, False)


def ray_loss(final_rows, head_weight, target_rgb, foreground, valid_rays):
    predicted = jnp.dot(final_rows, head_weight, precision=PRECISE)
    colour = jax.nn.sigmoid(predicted[:, :3])
    residue = colour - jnp.swapaxes(target_rgb, 0, 1)
    opacity = predicted[:, 3]
    per_ray = jnp.sum(residue * residue, -1) + jax.nn.softplus(opacity) - foreground * opacity
    return jnp.sum(valid_rays * per_ray)


def local(
    img_in,
    tri_in,
    cam,
    targets,
    fg_mask,
    counts,
    ln1_gain,
    ln1_bias,
    enc_qkv,
    enc_qv_bias,
    enc_proj,
    enc_proj_bias,
    ln2_gain,
    ln2_bias,
    enc_fc1,
    enc_fc1_bias,
    enc_fc2,
    enc_fc2_bias,
    dec_mod,
    dec_qkv,
    dec_proj,
    dec_cross_q,
    dec_cross_kv,
    dec_cross_proj,
    dec_fc1,
    dec_fc1_bias,
    dec_fc2,
    dec_fc2_bias,
    dec_head,
):
    group = lax.axis_index("grp")
    wide = lax.axis_index("wide")
    narrow = lax.axis_index("narrow")
    wides = lax.axis_size("wide")
    blocks = wides * lax.axis_size("narrow")
    block = wide * lax.axis_size("narrow") + narrow
    moving = wides == 4
    enc_width = img_in.shape[2]
    plane_rows, dec_width = tri_in.shape[1:]
    enc_half, dec_half = enc_width // 2, dec_width // 2
    enc_ff, dec_ff = enc_fc1.shape[1], dec_fc1.shape[1]
    enc_inner, dec_inner = enc_ff // blocks // 2, dec_ff // blocks // 2
    mod_rows = dec_mod.shape[0]

    def columns(shard, parts, width):
        cut = take(shard.reshape(shard.shape[0], parts, 2, width), group, 2)
        return cut.reshape(shard.shape[0], parts * width)

    def half_rows(shard):
        return take(shard.reshape(2, shard.shape[0] // 2, shard.shape[1]), group, 0)

    small_parts = (
        ln1_gain,
        ln1_bias,
        enc_proj_bias,
        ln2_gain,
        ln2_bias,
        enc_fc2_bias,
        enc_qv_bias,
        enc_fc1_bias,
        dec_fc1_bias,
        dec_fc2_bias,
        dec_head.reshape(-1),
    )
    piece = types.SimpleNamespace(
        enc_qkv=columns(enc_qkv, 3, enc_half),
        dec_qkv=columns(dec_qkv, 3, dec_half),
        enc_proj=enc_proj,
        enc_fc1=columns(enc_fc1, blocks, enc_inner),
        enc_fc2=half_rows(enc_fc2),
        dec_proj=dec_proj,
        cross_q=columns(dec_cross_q, 1, dec_half),
        cross_kv=columns(dec_cross_kv, 2, dec_half),
        cross_proj=dec_cross_proj,
        dec_fc1=columns(dec_fc1, blocks, dec_inner),
        dec_fc2=half_rows(dec_fc2),
    )

    ray_slots = plane_rows * lax.axis_size("narrow") // VIEWS
    row_index = narrow * plane_rows + jnp.arange(plane_rows, dtype=jnp.int32)
    view_index, slot_index = row_index // ray_slots, row_index % ray_slots
    view_ids = jnp.arange(VIEWS, dtype=jnp.int32)
    limits = jnp.sum(jnp.where(view_index[:, None] == view_ids[None, :], counts, 0), -1)
    valid_rays = (slot_index < limits).astype(F32)
    foreground = fg_mask[0].astype(F32)

    if moving:
        rows_of = []
        for part in small_parts:
            short = -part.shape[0] % 128
            rows_of.append(jnp.pad(part, (0, short)))
        small = jnp.concatenate(rows_of)
        small = jnp.pad(small, (0, 16 * 128 - small.shape[0])).reshape(16, 128)
        cam_blocks = jnp.pad(cam.reshape(blocks, 1, mod_rows), ((0, 0), (0, 0), (0, 128 - mod_rows)))
        begin = begin_part(cam_blocks, dec_mod, small, enc_width, dec_width, enc_inner, dec_inner)
        wide_buffer = pltpu.VMEM((4, 4, dec_fc1.shape[0], dec_ff // 2), BF16)
        tall_buffer = pltpu.VMEM((4, 4, dec_fc2.shape[0] // 2, dec_width), BF16)
        square_buffer = pltpu.VMEM((4, 4, dec_proj.shape[0], dec_width), BF16)
        own_part = self_part(
            tri_in[0],
            dict(),
            dict(modulation=(begin, "modulation")),
            dict(),
            dict(
                qkv=(GatherRow, 2, piece.dec_qkv, cuts_of(piece.dec_qkv), True),
                proj=(GatherShared, 6, piece.dec_proj, [None], True),
                cross_q=(Gather, 7, piece.cross_q, cuts_of(piece.cross_q), True),
            ),
            dict(qkv=("broad", False), proj=("square", False)),
            dict(broad=wide_buffer, tall=tall_buffer, square=square_buffer),
        )
        enc_part = encoder_part(
            img_in[0],
            dict(),
            dict(
                gain_one=(begin, "gain_one"),
                shift_one=(begin, "shift_one"),
                bias_qkv=(begin, "bias_qkv"),
                bias_proj=(begin, "bias_proj"),
                gain_two=(begin, "gain_two"),
                shift_two=(begin, "shift_two"),
                bias_fc1=(begin, "bias_fc1"),
                bias_fc2=(begin, "bias_fc2"),
                tall=(own_part, "tall"),
            ),
            dict(),
            dict(
                qkv=(Gather, 1, piece.enc_qkv, cuts_of(piece.enc_qkv), True),
                proj=(GatherShared, 3, piece.enc_proj, [None], True),
                fc1=(GatherRow, 4, piece.enc_fc1, cuts_of(piece.enc_fc1), True),
                fc2=(Gather, 5, piece.enc_fc2, cuts_of(piece.enc_fc2), True),
                cross_kv=(Gather, 8, piece.cross_kv, cuts_of(piece.cross_kv), True),
            ),
            dict(fc2=("tall", False)),
            enc_ff // 2,
            dec_half,
        )
        last_part = cross_part(
            plane_rows,
            dec_width,
            dec_ff // 2,
            dict(),
            dict(
                queries=(own_part, "cross_queries"),
                keyvals=(enc_part, "cross_keyvals"),
                after_self=(own_part, "after_self"),
                modulation=(begin, "modulation"),
                bias_fc1=(begin, "bias_dfc1"),
                bias_fc2=(begin, "bias_dfc2"),
                broad=(own_part, "broad"),
                tall=(own_part, "tall"),
                square=(own_part, "square"),
            ),
            dict(),
            dict(
                proj=(GatherShared, 9, piece.cross_proj, [None], True),
                fc1=(Gather, 10, piece.dec_fc1, cuts_of(piece.dec_fc1), True),
                fc2=(Gather, 11, piece.dec_fc2, cuts_of(piece.dec_fc2), True),
            ),
            dict(fc1=("broad", True), fc2=("tall", True), proj=("square", True)),
        )
        first, enc, own, cross = run(
            [begin, enc_part, own_part, last_part],
            2,
            True,
            order=(1, 0, 2, 0, 1, 2, 1, 2, 1, 2, 1, 1, 1),
            links=320,
        )
        modulation, cam_cut = first.modulation, first.cams.reshape(4, 128)[:, :mod_rows]
        gain_one, gain_two = first.gain_one, first.gain_two
        head = first.small.reshape(blocks, 16, 128)[:, 12:14]
        head = head.reshape(dec_width, 4).astype(F32)
        full = types.SimpleNamespace(
            enc_qkv=enc.qkv,
            enc_proj=enc.proj,
            enc_fc1=enc.fc1,
            enc_fc2=enc.fc2,
            cross_kv=enc.cross_kv,
            dec_qkv=own.qkv,
            dec_proj=own.proj,
            cross_q=own.cross_q,
            cross_proj=cross.proj,
            dec_fc1=cross.fc1,
            dec_fc2=cross.fc2,
        )
    else:
        small_all = lax.all_gather(jnp.concatenate(small_parts), BLOCKS, axis=0)
        unpacked, offset = [], 0
        for part in small_parts:
            length = part.shape[0]
            unpacked.append(small_all[:, offset : offset + length].reshape(1, -1).astype(F32))
            offset += length
        (
            gain_one,
            shift_one,
            bias_proj,
            gain_two,
            shift_two,
            bias_fc2,
            bias_qv,
            bias_fc1,
            bias_dfc1,
            bias_dfc2,
            head_flat,
        ) = unpacked
        head = head_flat.reshape(dec_width, 4)
        qv_half = take(bias_qv.reshape(2, 2, enc_half), group, 1)
        bias_qkv = jnp.concatenate([qv_half[0], jnp.zeros((enc_half,), F32), qv_half[1]])
        bias_qkv = bias_qkv.reshape(1, -1)
        fc1_half = take(bias_fc1.reshape(blocks, 2, enc_inner), group, 1).reshape(1, -1)
        dfc1_half = take(bias_dfc1.reshape(blocks, 2, dec_inner), group, 1).reshape(1, -1)
        cam_all = lax.all_gather(cam, "wide", axis=0, tiled=True)
        cam_cut = lax.dynamic_slice_in_dim(cam_all, block * mod_rows, mod_rows, 1)
        term = jnp.dot(cam_cut, dec_mod.astype(F32), precision=PRECISE)
        term = lax.psum(term, "narrow")
        modulation = lax.psum_scatter(term, "wide", scatter_dimension=0, tiled=True)
        modulation = modulation.reshape(6, dec_width)
        full = types.SimpleNamespace(
            **{
                name: lax.all_gather(value, BLOCKS, axis=0, tiled=True)
                for name, value in vars(piece).items()
            }
        )
        enc, own = run(
            [
                encoder_part(
                    img_in[0],
                    dict(
                        gain_one=gain_one,
                        shift_one=shift_one,
                        bias_qkv=bias_qkv,
                        bias_proj=bias_proj,
                        gain_two=gain_two,
                        shift_two=shift_two,
                        bias_fc1=fc1_half,
                        bias_fc2=bias_fc2,
                    ),
                    dict(),
                    dict(
                        qkv=full.enc_qkv,
                        proj=full.enc_proj,
                        fc1=full.enc_fc1,
                        fc2=full.enc_fc2,
                        cross_kv=full.cross_kv,
                    ),
                    dict(),
                    dict(),
                    enc_ff // 2,
                    dec_half,
                ),
                self_part(
                    tri_in[0],
                    dict(modulation=modulation),
                    dict(),
                    dict(qkv=full.dec_qkv, proj=full.dec_proj, cross_q=full.cross_q),
                    dict(),
                    dict(),
                    dict(),
                ),
            ],
            2,
            False,
            links=32,
        )
        (cross,) = run(
            [
                cross_part(
                    plane_rows,
                    dec_width,
                    dec_ff // 2,
                    dict(
                        queries=own.cross_queries,
                        keyvals=enc.cross_keyvals,
                        after_self=own.after_self,
                        modulation=modulation,
                        bias_fc1=dfc1_half,
                        bias_fc2=bias_dfc2,
                    ),
                    dict(),
                    dict(proj=full.cross_proj, fc1=full.dec_fc1, fc2=full.dec_fc2),
                    dict(),
                    dict(),
                )
            ],
            3,
            False,
            links=32,
        )

    def ray_total(rows_in, head_in):
        return ray_loss(rows_in, head_in, targets[0], foreground, valid_rays)

    total, ray_pull = jax.vjp(ray_total, cross.final, head)
    grad_final, grad_head = ray_pull(jnp.ones((), F32))

    def sums_of(**named):
        return named if moving else {}

    (late,) = run(
        [
            cross_back_part(
                dict(
                    grad=grad_final,
                    pre=cross.pre,
                    normed_three=cross.normed_three,
                    after_cross=cross.after_cross,
                    modulation=modulation,
                    queries=own.cross_queries,
                    keyvals=enc.cross_keyvals,
                    sums=cross.sums,
                    after_self=own.after_self,
                    image=enc.image,
                    attended=cross.attended,
                    normed_two=own.normed_two,
                ),
                dict(
                    fc2=full.dec_fc2,
                    fc1=full.dec_fc1,
                    cross_q=full.cross_q,
                    cross_kv=full.cross_kv,
                ),
                dict(proj=full.cross_proj),
                sums_of(
                    fc2=(Scatter, piece.dec_fc2.shape[0], dec_width, "fc2", BF16),
                    fc1=(Scatter, piece.dec_fc1.shape[0], dec_ff // 2, "fc1", BF16),
                    proj=(ScatterLine, dec_cross_proj.shape[0], dec_half, None, BF16),
                    cross_q=(ScatterLine, dec_cross_q.shape[0], dec_half, "cross_q", BF16),
                ),
            )
        ],
        4,
        moving,
        links=128,
    )
    self_rows, enc_rows = dec_qkv.shape[0], enc_qkv.shape[0]
    front, back = run(
        [
            self_back_part(
                dict(
                    attended=own.attended,
                    queries=own.queries,
                    keyvals=own.keyvals,
                    sums=own.sums,
                    normed_one=own.normed_one,
                    modulation=modulation,
                    image=enc.image,
                    cross_dkv=late.cross_dkv,
                ),
                dict(grad_self=late.grad_self, x=tri_in[0]),
                dict(qkv=full.dec_qkv),
                dict(proj=full.dec_proj),
                sums_of(
                    cross_kv=(ScatterLine, enc_rows, dec_width, None, BF16),
                    proj=(Scatter, self_rows, dec_half, None, BF16),
                    qkv=(Scatter, self_rows, 3 * dec_half, "qkv", BF16),
                ),
            ),
            encoder_back_part(
                dict(
                    image_grad=late.image_grad,
                    pre=enc.pre,
                    hidden=enc.hidden,
                    normed_one=enc.normed_one,
                    normed_two=enc.normed_two,
                    attended=enc.attended,
                    queries=enc.queries,
                    keyvals=enc.keyvals,
                    sums=enc.sums,
                    gain_one=gain_one,
                    gain_two=gain_two,
                ),
                dict(x=img_in[0]),
                dict(fc2=full.enc_fc2, fc1=full.enc_fc1, qkv=full.enc_qkv),
                dict(proj=full.enc_proj),
                sums_of(
                    fc2=(Scatter, piece.enc_fc2.shape[0], enc_width, "fc2", BF16),
                    fc1=(ScatterLine, enc_rows, enc_ff // 2, "fc1", BF16),
                    proj=(Scatter, enc_rows, enc_half, None, BF16),
                    qkv=(Scatter, enc_rows, 3 * enc_half, "qkv", BF16),
                ),
            )
        ],
        5,
        moving,
        links=200,
    )

    def placed(half, count, width):
        cut = half.reshape(count, 1, width)
        zero = jnp.zeros_like(cut)
        low = jnp.where(group == 0, cut, zero)
        high = jnp.where(group == 0, zero, cut)
        return jnp.concatenate([low, high], 1).reshape(-1)

    row_sums = back.row_sums[0]
    qv_sums = jnp.concatenate([row_sums[:enc_half], row_sums[2 * enc_half :]])
    loss_terms = jnp.stack([total, jnp.sum(valid_rays)])
    small_grads = (
        0.5 * back.gain_one_grad,
        0.5 * back.shift_one_grad,
        placed(qv_sums, 2, enc_half),
        0.5 * back.branch_sums,
        0.5 * back.gain_two_grad,
        0.5 * back.shift_two_grad,
        placed(back.pre_sums, blocks, enc_inner),
        0.5 * column_sums(late.image_grad),
        placed(late.pre_sums, blocks, dec_inner),
        0.5 * column_sums(to_bf16(grad_final)),
        0.5 * grad_head,
        jnp.tile(0.5 * loss_terms, blocks),
    )
    packed = jnp.concatenate([part.reshape(blocks, -1) for part in small_grads], 1)
    grad_mod = jnp.concatenate(
        [
            front.gamma_one,
            front.beta_one,
            late.gamma_two,
            late.beta_two,
            late.gamma_three,
            late.beta_three,
        ],
        1,
    )
    length = packed.shape[1]
    if moving:
        packed = jnp.pad(packed, ((0, 0), (0, 16 * 128 - length))).reshape(4, 4, 16, 128)
        (last,) = run([end_part(packed, grad_mod)], 7, True, links=32)
        small_sum = (last.d_small[0] + last.d_small[1]).reshape(-1)[:length]
        mod_all = last.everyone.reshape(4, -1)
    else:
        small_sum = take(lax.psum(packed, ("grp", "wide", "narrow")), block, 0)
        mod_all = lax.all_gather(lax.psum(grad_mod, "narrow"), "wide", axis=0, tiled=True)
    small_out, offset = [], 0
    for part in small_grads:
        count = part.size // blocks
        small_out.append(small_sum[offset : offset + count])
        offset += count
    loss = small_out[11][0] / small_out[11][1]
    grad_wmod = jnp.dot(jnp.transpose(cam_cut), mod_all, precision=PRECISE)

    def own_half(value):
        return take(value.reshape(value.shape[0], 2, -1), group, 1)

    def halves_of(reduced, x, grad):
        if not moving:
            half = plain_grad(x, grad)
            other = lax.ppermute(half, "grp", [(0, 1), (1, 0)])
            pair = jnp.stack([half, other])
            reduced = jnp.where(group == 0, pair, pair[::-1])
        return reduced.astype(F32)

    def full_columns(halves, parts):
        cut = halves.reshape(2, halves.shape[1], parts, -1)
        return jnp.transpose(cut, (1, 2, 0, 3)).reshape(halves.shape[1], -1)

    def full_rows(halves):
        return halves.reshape(-1, halves.shape[2])

    def reduced_of(space, name):
        return getattr(space, name, None)

    if moving:
        self_branch = enc_branch = enc_dpre = dec_dpre = enc_drows = dec_drows = None
        enc_act = dec_act = None
    else:
        self_branch, enc_branch = own_half(front.branch), own_half(back.branch)
        enc_act, dec_act = back.act, late.act
        enc_dpre, dec_dpre, enc_drows, dec_drows = back.dpre, late.dpre, back.drows, front.drows
    cross_branch = own_half(late.cross_branch)
    get = reduced_of
    out_qkv = halves_of(get(back, "d_qkv"), enc.normed_one, enc_drows)
    out_proj = halves_of(get(back, "d_proj"), enc.attended, enc_branch)
    out_fc1 = halves_of(get(back, "d_fc1"), enc.normed_two, enc_dpre)
    out_fc2 = halves_of(get(back, "d_fc2"), enc_act, late.image_grad)
    out_dqkv = halves_of(get(front, "d_qkv"), own.normed_one, dec_drows)
    out_dproj = halves_of(get(front, "d_proj"), own.attended, self_branch)
    out_cq = halves_of(get(late, "d_cross_q"), own.normed_two, late.cross_dq)
    out_ckv = halves_of(get(front, "d_cross_kv"), enc.image, late.cross_dkv)
    out_cproj = halves_of(get(late, "d_proj"), cross.attended, cross_branch)
    out_dfc1 = halves_of(get(late, "d_fc1"), cross.normed_three, dec_dpre)
    out_dfc2 = halves_of(get(late, "d_fc2"), dec_act, to_bf16(grad_final))

    return (
        loss,
        back.x_grad[None],
        front.x_grad[None],
        small_out[0],
        small_out[1],
        full_columns(out_qkv, 3),
        small_out[2],
        full_columns(out_proj, 1),
        small_out[3],
        small_out[4],
        small_out[5],
        full_columns(out_fc1, blocks),
        small_out[6],
        full_rows(out_fc2),
        small_out[7],
        grad_wmod,
        full_columns(out_dqkv, 3),
        full_columns(out_dproj, 1),
        full_columns(out_cq, 1),
        full_columns(out_ckv, 2),
        full_columns(out_cproj, 1),
        full_columns(out_dfc1, blocks),
        small_out[8],
        full_rows(out_dfc2),
        small_out[9],
        small_out[10].reshape(-1, 4),
    )


def solution(mesh):
    tokens = P("wide", "narrow", None)
    matrix = P(BLOCKS, None)
    vector = P(BLOCKS)
    objects = P("wide", None)
    rays = (P("wide", None, "narrow"), P("wide", "narrow"))
    encoder = (vector, vector, matrix, vector, matrix, vector, vector, vector, matrix, vector)
    encoder = encoder + (matrix, vector)
    decoder = (matrix,) * 7 + (vector, matrix, vector, matrix)
    return jax.shard_map(
        local,
        mesh=mesh,
        in_specs=(tokens, tokens, objects) + rays + (objects,) + encoder + decoder,
        out_specs=(P(), tokens, tokens) + encoder + decoder,
        check_vma=False,
    )
```

```python
import functools
import types

import jax
import jax.numpy as jnp
from jax import lax
from jax.experimental import pallas as pl
from jax.experimental.pallas import tpu as pltpu
from jax.sharding import PartitionSpec as P

HEAD = 64
VIEWS = 4
NORM_EPS = 1e-06
PRECISE = lax.Precision.HIGHEST
F32 = jnp.float32
BF16 = jnp.bfloat16
MIB = 1 << 20
VMEM = pl.BlockSpec(memory_space=pltpu.VMEM)
HBM = pl.BlockSpec(memory_space=pl.ANY)
MESH = pl.DeviceIdType.MESH
BLOCKS = ("wide", "narrow")


def shape_of(shape, dtype):
    return jax.ShapeDtypeStruct(shape, dtype)


def to_bf16(value):
    return value.astype(BF16)


def dot_plain(a, b):
    return jnp.dot(a, b, preferred_element_type=F32)


def dot_right(a, b):
    return lax.dot_general(a, b, (((1,), (1,)), ((), ())), preferred_element_type=F32)


def dot_left(a, b):
    return lax.dot_general(a, b, (((0,), (0,)), ((), ())), preferred_element_type=F32)


class Crew:
    def __init__(self, send, recv, here, lines):
        self.send_sems, self.recv_sems, self.here_sems = send, recv, here
        self.used = self.kept = self.slotted = self.given = 0
        self.credit = None
        self.sent = []
        self.group = lax.axis_index("grp")
        self.wide = lax.axis_index("wide")
        self.narrow = lax.axis_index("narrow")
        self.at_core = self.narrow + 1 - 2 * lax.rem(self.narrow, 2)
        self.at_row = lax.rem(self.narrow + 2, 4)
        self.at_cross = lax.rem(self.at_core + 2, 4)
        self.grp = {"grp": 1 - self.group}
        self.core = {"narrow": self.at_core}
        self.row = {"narrow": self.at_row}
        self.places = [lax.rem(self.wide + d, 4) for d in (1, 2, 3)] if lines else []
        self.line = [{"wide": place} for place in self.places]

    def greet(self):
        barrier = pltpu.get_barrier_semaphore()
        targets = [self.grp, self.core, self.row] + self.line
        for target in targets:
            pl.semaphore_signal(barrier, inc=1, device_id=target, device_id_type=MESH)
        pl.semaphore_wait(barrier, len(targets))

    def send(self, source, landing, target):
        copy = pltpu.make_async_remote_copy(
            src_ref=source,
            dst_ref=landing,
            send_sem=self.send_sems.at[self.used],
            recv_sem=self.recv_sems.at[self.used],
            device_id=target,
            device_id_type=MESH,
        )
        self.used += 1
        self.sent.append(copy)
        copy.start()
        return copy

    def keep(self, source, landing):
        copy = pltpu.make_async_copy(source, landing, self.here_sems.at[self.kept])
        self.kept += 1
        copy.start()
        return copy

    def close(self):
        for copy in self.sent:
            copy.wait_send()


class Gather:
    def __init__(self, crew, piece, full, cut, buf):
        self.crew, self.piece, self.full, self.cut, self.buf = crew, piece, full, cut, buf
        rows, cols = full.shape[2:]
        self.source = piece
        if piece.shape[0] == 2 * rows:
            self.source = piece.at[pl.ds(pl.multiple_of(crew.group * rows, rows), rows), cut]
        elif piece.shape[1] == 2 * cols:
            first = pl.multiple_of(2 * cut.start + crew.group * cut.size, 128)
            self.source = piece.at[:, pl.ds(first, cut.size)]
        else:
            self.source = piece.at[:, cut]
        self.steps = [self.start, self.turn, self.cross, self.finish]
        self.load, self.late = None, False

    def start(self):
        crew = self.crew
        source = self.source
        own = self.full.at[crew.wide, crew.narrow, :, self.cut]
        self.own = crew.keep(source, own)
        self.lines = [crew.send(source, own, target) for target in crew.line]

    def turn(self):
        crew = self.crew
        self.own.wait()
        for copy in self.lines:
            copy.wait_recv()
        mine = self.full.at[:, crew.narrow, :, self.cut]
        self.row = crew.send(mine, mine, crew.row)
        self.core = crew.send(mine, mine, crew.core)

    def cross(self):
        crew = self.crew
        self.row.wait_recv()
        other = self.full.at[:, crew.at_row, :, self.cut]
        self.far = crew.send(other, other, crew.core)

    def finish(self):
        self.core.wait_recv()
        self.far.wait_recv()
        if self.buf is not None and not self.late:
            self.fetch()

    def fetch(self):
        if self.load is None:
            self.load = self.crew.keep(
                self.full.at[:, :, :, self.cut], self.buf.at[:, :, :, self.cut]
            )


class GatherRow(Gather):
    def start(self):
        crew = self.crew
        source = self.source
        own = self.full.at[crew.wide, crew.narrow, :, self.cut]
        self.row = crew.send(source, own, crew.row)
        self.own = crew.keep(source, own)
        self.lines = [crew.send(source, own, target) for target in crew.line]

    def turn(self):
        crew = self.crew
        self.row.wait_recv()
        other = self.full.at[crew.wide, crew.at_row, :, self.cut]
        self.lines += [crew.send(other, other, target) for target in crew.line]

    def cross(self):
        crew = self.crew
        self.own.wait()
        for copy in self.lines:
            copy.wait_recv()
        mine = self.full.at[:, crew.narrow, :, self.cut]
        other = self.full.at[:, crew.at_row, :, self.cut]
        self.core = crew.send(mine, mine, crew.core)
        self.far = crew.send(other, other, crew.core)


class GatherShared(Gather):
    def __init__(self, crew, piece, full, cut, buf):
        half = piece.shape[1] // 2
        mine = pl.ds(pl.multiple_of(crew.group * half, half), half)
        super().__init__(crew, piece, full, mine, buf)
        self.steps = [self.start, self.turn, self.over, self.cross, self.finish]

    def turn(self):
        crew = self.crew
        self.own.wait()
        for copy in self.lines:
            copy.wait_recv()
        mine = self.full.at[:, crew.narrow, :, self.cut]
        self.row = crew.send(mine, mine, crew.row)
        self.others = [crew.send(mine, mine, crew.grp)]

    def over(self):
        crew = self.crew
        self.row.wait_recv()
        other = self.full.at[:, crew.at_row, :, self.cut]
        self.others.append(crew.send(other, other, crew.grp))

    def cross(self):
        crew = self.crew
        for copy in self.others:
            copy.wait_recv()
        mine, other = self.full.at[:, crew.narrow], self.full.at[:, crew.at_row]
        self.core = crew.send(mine, mine, crew.core)
        self.far = crew.send(other, other, crew.core)
        self.cut = slice(None)


class Scatter:
    def __init__(self, crew, whole, cut, index):
        rows = whole.part.shape[2]
        self.crew, self.part, self.cut, self.index = crew, whole.part, cut, index
        self.pair = whole.slots.at[index % 2, :, :, pl.ds(0, rows), pl.ds(0, cut.size)]
        self.single = whole.single.at[:, :, cut]
        self.lines = whole.lines.at[:, :, cut]
        self.out = whole.out.at[:, :, cut]
        self.steps = [self.start, self.turn, self.along, self.over, self.finish]

    def start(self):
        crew, part = self.crew, self.part
        if self.index >= 2:
            pl.semaphore_wait(crew.credit, 1)
        self.core = crew.send(part.at[:, crew.at_core, :, self.cut], self.pair.at[0], crew.core)
        self.far = crew.send(part.at[:, crew.at_cross, :, self.cut], self.pair.at[1], crew.core)

    def add(self, place, landing):
        part, cut = self.part, self.cut

        def one(i, carry):
            total = part[i, place, :, cut].astype(F32) + landing[i].astype(F32)
            part[i, place, :, cut] = total.astype(part.dtype)
            return carry

        lax.fori_loop(0, part.shape[0], one, 0)

    def turn(self):
        crew = self.crew
        self.far.wait_recv()
        self.add(crew.at_row, self.pair.at[1])
        self.row = crew.send(self.part.at[:, crew.at_row, :, self.cut], self.single, crew.row)
        self.core.wait_recv()
        self.add(crew.narrow, self.pair.at[0])
        if self.index < crew.slotted - 2:
            pl.semaphore_signal(crew.credit, inc=1, device_id=crew.core, device_id_type=MESH)

    def along(self):
        crew, part = self.crew, self.part
        self.row.wait_recv()
        self.add(crew.narrow, self.single)
        self.copies = [
            crew.send(part.at[place, crew.narrow, :, self.cut], self.lines.at[i], target)
            for i, (place, target) in enumerate(zip(crew.places, crew.line))
        ]

    def over(self):
        crew, part = self.crew, self.part
        for copy in self.copies:
            copy.wait_recv()
        total = part[crew.wide, crew.narrow, :, self.cut].astype(F32)
        for i in range(3):
            total = total + self.lines[i].astype(F32)
        own = self.out.at[crew.group]
        own[...] = total.astype(part.dtype)
        self.other = crew.send(own, own, crew.grp)

    def finish(self):
        self.other.wait_recv()


class ScatterLine(Scatter):
    def __init__(self, crew, whole, cut, index):
        super().__init__(crew, whole, cut, index)
        self.steps = [self.start, self.turn, self.along, self.over, self.finish]

    def turn(self):
        crew, part = self.crew, self.part
        self.far.wait_recv()
        self.add(crew.at_row, self.pair.at[1])
        self.core.wait_recv()
        self.add(crew.narrow, self.pair.at[0])
        if self.index < crew.slotted - 2:
            pl.semaphore_signal(crew.credit, inc=1, device_id=crew.core, device_id_type=MESH)
        self.copies = [
            [
                crew.send(part.at[place, narrow, :, self.cut], landing.at[i], target)
                for i, (place, target) in enumerate(zip(crew.places, crew.line))
            ]
            for narrow, landing in ((crew.at_row, self.single), (crew.narrow, self.lines))
        ]

    def total(self, copies, narrow, landing):
        crew = self.crew
        for copy in copies:
            copy.wait_recv()
        total = self.part[crew.wide, narrow, :, self.cut].astype(F32)
        for i in range(3):
            total = total + landing[i].astype(F32)
        return total.astype(self.part.dtype)

    def along(self):
        crew, part = self.crew, self.part
        own = part.at[crew.wide, crew.at_row, :, self.cut]
        own[...] = self.total(self.copies[0], crew.at_row, self.single)
        self.row = crew.send(own, self.single.at[3], crew.row)

    def over(self):
        crew = self.crew
        total = self.total(self.copies[1], crew.narrow, self.lines)
        self.row.wait_recv()
        own = self.out.at[crew.group]
        total = total.astype(F32) + self.single[3].astype(F32)
        own[...] = total.astype(self.part.dtype)
        self.other = crew.send(own, own, crew.grp)


class Summed:
    def __init__(self, part, single, lines, out, slots, kind):
        self.part, self.single, self.lines, self.out, self.slots = part, single, lines, out, slots
        self.kind = kind


class Pipe:
    def __init__(self, ahead):
        self.ahead, self.queue, self.jobs, self.pending = ahead, [], [], None

    def plan(self, job):
        job.at = 0
        self.queue.append(job)

    def begin(self, job):
        job.steps[0]()
        job.at = 1
        self.jobs.append(job)

    def fill(self):
        while self.queue and sum(job.at == 1 for job in self.jobs) < self.ahead:
            self.begin(self.queue.pop(0))

    def settle(self):
        if self.pending is not None:
            self.pending.turn()
            self.pending.at = 2
            self.jobs.append(self.pending)
            self.pending = None

    def add(self, job):
        job.start()
        self.settle()
        self.pending = job

    def go(self, job):
        job.steps[job.at]()
        job.at += 1
        if job.at == len(job.steps):
            self.jobs.remove(job)

    def pump(self, lag=1):
        before = self.pending
        self.settle()
        waiting = {}
        for job in self.jobs:
            if job is not before:
                waiting.setdefault(job.at, []).append(job)
        for at in sorted(waiting, reverse=True):
            if at == 1 or len(waiting[at]) > lag:
                self.go(waiting[at][0])
        self.fill()

    def need(self, job):
        while job.at < len(job.steps):
            self.pump()
            if job.at and job.at < len(job.steps):
                self.go(job)

    def drain(self):
        while self.jobs or self.queue or self.pending is not None:
            self.pump(0)


class Matrix:
    def __init__(self, buf, pipe):
        self.buf, self.pipe, self.jobs, self.load = buf, pipe, [], None
        self.loaded = []

    def need(self, index=None):
        wanted = [job for i, job in enumerate(self.jobs) if index is None or index == i]
        for job in wanted:
            self.pipe.need(job)
        for job in self.jobs:
            if job.at == len(job.steps):
                job.fetch()
        for job in wanted:
            if job not in self.loaded:
                job.load.wait()
                self.loaded.append(job)
        if self.load is not None:
            self.load.wait()
            self.load = None

    def cols(self, cut):
        value = self.buf[..., cut]
        return value.reshape(-1, value.shape[-1])

    def rows(self, i):
        if len(self.buf.shape) == 4:
            return self.buf[i].reshape(-1, self.buf.shape[3])
        height = self.buf.shape[0] // 4
        return self.buf[pl.ds(i * height, height), :]

    def all(self):
        return self.cols(slice(None))


class Part:
    def __init__(self, body, **named):
        self.body = body
        self.ins = named.get("ins", {})
        self.far = named.get("far", {})
        self.outs = named.get("outs", {})
        self.scratch = named.get("scratch", {})
        self.given = named.get("given", {})
        self.links = named.get("links", {})
        self.packs = named.get("packs", {})
        self.late = named.get("late", {})
        self.halves = named.get("halves", {})
        self.shapes = named.get("shapes", {})
        self.moved = named.get("moved", {})
        self.sums = named.get("sums", {})


def cuts_of(piece):
    cols = piece.shape[1]
    width = width_of(cols)
    return [pl.ds(first, width) for first in range(0, cols, width)]


def width_of(cols):
    for width in (512, 384):
        if cols % width == 0:
            return width
    return cols


def grad_scratch(rows, cols, dtype):
    return pltpu.VMEM((4, rows, cols), dtype), pltpu.VMEM((3, rows, cols), dtype)


def run(parts, collective, lines, order=(), ahead=4, links=0, flops=0, moved=0, limit=63):
    arrays, in_specs, out_shapes, out_specs, scratch = [], [], [], [], []
    layout = []
    for part in parts:
        named = []
        for name, value in part.ins.items():
            arrays.append(value)
            in_specs.append(VMEM)
        for name, value in part.far.items():
            arrays.append(value)
            in_specs.append(HBM)
        for name, value in part.given.items():
            arrays.append(value)
            in_specs.append(HBM)
            scratch.append(pltpu.VMEM(value.shape, BF16))
        for name, value in part.halves.items():
            arrays.append(value)
            in_specs.append(HBM)
            scratch.append(pltpu.VMEM((value.shape[0] // 2,) + value.shape[1:], BF16))
        for name, (_, _, piece, cuts, loaded) in part.moved.items():
            arrays.append(piece)
            in_specs.append(HBM)
            shape = (4, 4) + part.shapes.get(name, piece.shape)
            out_shapes.append(shape_of(shape, piece.dtype))
            out_specs.append(HBM)
            if loaded and name not in part.late:
                scratch.append(pltpu.VMEM(shape, piece.dtype))
        for name, shape in part.packs.items():
            out_shapes.append(shape_of((4, 4) + shape, F32))
            out_specs.append(HBM)
            scratch.append(pltpu.VMEM((4, 4) + shape, F32))
            scratch.append(pltpu.VMEM(shape, F32))
        for name, value in part.outs.items():
            out_shapes.append(value)
            out_specs.append(VMEM)
        for name, (kind, rows, cols, weight, dtype) in part.sums.items():
            out_shapes.append(shape_of((2, rows, cols), dtype))
            out_specs.append(VMEM)
            scratch.extend(grad_scratch(rows, cols, dtype))
            if weight is None:
                scratch.append(pltpu.VMEM((4, 4, rows, cols), dtype))
        for name, value in part.scratch.items():
            scratch.append(value)
    n_in, n_out = len(arrays), len(out_shapes)
    count = max(links, 1)
    summed = [entry for part in parts for entry in part.sums.values()]
    slotted = sum(cols // width_of(cols) for _, _, cols, _, _ in summed)
    if summed:
        depth = max(rows for _, rows, _, _, _ in summed)
        span = max(width_of(cols) for _, _, cols, _, _ in summed)
        scratch.append(pltpu.VMEM((2, 2, 4, depth, span), summed[0][4]))
        scratch.append(pltpu.SemaphoreType.REGULAR)
    scratch = scratch + [pltpu.SemaphoreType.DMA((count,))] * 3

    def kernel(*refs):
        ins, outs = iter(refs[:n_in]), iter(refs[n_in : n_in + n_out])
        rest = iter(refs[n_in + n_out : -3])
        crew = Crew(*refs[-3:], lines)
        slots = None
        if summed:
            slots, crew.credit = refs[-5:-3]
            crew.slotted = slotted
        pipe = Pipe(ahead)
        crew.greet()
        planned, spaces, loads = [], [], []
        for part in parts:
            space = types.SimpleNamespace()
            for name in part.ins:
                setattr(space, name, next(ins))
            for name in part.far:
                setattr(space, name, next(ins))
            for name in part.given:
                matrix = Matrix(next(rest), pipe)
                loads.append((matrix, next(ins)))
                setattr(space, name, matrix)
            for name in part.halves:
                matrix = Matrix(next(rest), pipe)
                height = matrix.buf.shape[0]
                first = pl.multiple_of(crew.group * height, height)
                loads.append((matrix, next(ins).at[pl.ds(first, height)]))
                setattr(space, name, matrix)
            for name, (kind, rank, piece, cuts, loaded) in part.moved.items():
                source, full = next(ins), next(outs)
                buf = next(rest) if loaded and name not in part.late else None
                matrix = Matrix(buf, pipe)
                setattr(space, name, matrix)
                for i, cut in enumerate(cuts):
                    job = kind(crew, source, full, cut, buf)
                    matrix.jobs.append(job)
                    planned.append((rank + 0.01 * i, job))
            for name in part.packs:
                matrix = Matrix(next(rest), pipe)
                matrix.piece = next(rest)
                matrix.jobs.append(Gather(crew, matrix.piece, next(outs), slice(None), matrix.buf))
                setattr(space, name, matrix)
            for name in part.outs:
                setattr(space, name, next(outs))
            for name, (kind, rows, cols, weight, dtype) in part.sums.items():
                out = next(outs)
                single, lines_in = next(rest), next(rest)
                own = next(rest) if weight is None else getattr(space, weight).buf
                setattr(space, "d_" + name, Summed(own, single, lines_in, out, slots, kind))
            for name in part.scratch:
                setattr(space, name, next(rest))
            spaces.append(space)
        for part, space in zip(parts, spaces):
            for name, (other, known) in part.links.items():
                setattr(space, name, getattr(spaces[parts.index(other)], known))
        for part, space in zip(parts, spaces):
            for name, (held, _) in part.late.items():
                rows_in, cols = part.shapes.get(name, part.moved[name][2].shape)
                matrix = getattr(space, name)
                matrix.buf = getattr(space, held).at[:, :, pl.ds(0, rows_in), pl.ds(0, cols)]
                for job in matrix.jobs:
                    job.buf, job.late = matrix.buf, part.late[name][1]
        for _, job in sorted(planned, key=lambda entry: entry[0]):
            pipe.plan(job)
        pipe.fill()
        for matrix, source in loads:
            matrix.load = crew.keep(source, matrix.buf)
        strands = [part.body(space, crew, pipe) for part, space in zip(parts, spaces)]
        for i in order:
            next(strands[i], None)
        while strands:
            for strand in list(strands):
                if next(strand, True):
                    strands.remove(strand)
        pipe.drain()
        for matrix, _ in loads:
            matrix.need()
        crew.close()

    results = pl.pallas_call(
        kernel,
        out_shape=out_shapes,
        in_specs=in_specs,
        out_specs=out_specs,
        scratch_shapes=scratch,
        compiler_params=pltpu.CompilerParams(
            vmem_limit_bytes=limit * MIB, collective_id=collective, has_side_effects=True
        ),
        cost_estimate=pl.CostEstimate(
            flops=int(flops), bytes_accessed=int(moved), transcendentals=0
        ),
    )(*arrays)
    results = iter(results)
    given = []
    for part in parts:
        space = types.SimpleNamespace()
        for name in part.moved:
            setattr(space, name, next(results))
        for name in part.packs:
            setattr(space, name, next(results))
        for name in part.outs:
            setattr(space, name, next(results))
        for name in part.sums:
            setattr(space, "d_" + name, next(results))
        given.append(space)
    return given


def normalise(x):
    centered = x - jnp.mean(x, -1, keepdims=True)
    scale = lax.rsqrt(jnp.mean(centered * centered, -1, keepdims=True) + NORM_EPS)
    return centered * scale, scale


def norm_back(values, gain, grad):
    xhat, scale = normalise(values)
    inner = grad * gain
    term = inner - jnp.mean(inner, -1, keepdims=True)
    term = term - xhat * jnp.mean(inner * xhat, -1, keepdims=True)
    return (
        term * scale,
        jnp.sum(grad * xhat, 0, keepdims=True),
        jnp.sum(grad, 0, keepdims=True),
    )


def column_sums(value):
    return jnp.sum(value.astype(F32), 0, keepdims=True)


def gelu_pair(pre):
    cdf = 0.5 * (1.0 + lax.erf(pre * 0.7071067811865476))
    return cdf, pre * cdf


def gelu_both(pre):
    cdf, act = gelu_pair(pre)
    return act, cdf + pre * (0.3989422804014327 * jnp.exp(-0.5 * pre * pre))


def head_masks(rows):
    lane = lax.broadcasted_iota(jnp.int32, (rows, 2 * HEAD), 1)
    return [lane < HEAD, lane >= HEAD]


class Spread:
    def __init__(self, crew, keyvals):
        self.crew, self.keyvals, self.copies = crew, keyvals, []

    def give(self, slot):
        copy = self.crew.send(
            self.keyvals.at[slot], self.keyvals.at[slot + 1], self.crew.core
        )
        self.copies.append(copy)

    def finish(self):
        for copy in self.copies:
            copy.wait_recv()


class Fold:
    def __init__(self, crew, dkeyvals, landing):
        self.crew, self.dkeyvals, self.landing = crew, dkeyvals, landing
        self.core = crew.send(dkeyvals.at[1], landing.at[0], crew.core)
        self.far = crew.send(dkeyvals.at[3], landing.at[1], crew.core)

    def turn(self):
        dkeyvals, landing = self.dkeyvals, self.landing
        self.far.wait_recv()
        dkeyvals[2] = (dkeyvals[2].astype(F32) + landing[1].astype(F32)).astype(BF16)
        self.row = self.crew.send(dkeyvals.at[2], landing.at[2], self.crew.row)

    def finish(self):
        landing = self.landing
        self.core.wait_recv()
        own = self.dkeyvals[0].astype(F32) + landing[0].astype(F32)
        self.row.wait_recv()
        return (own + landing[2].astype(F32)).astype(BF16)


def attend(q_ref, keyvals, out_ref, out_first, sums_ref, half, first, last):
    rows = q_ref.shape[0]
    masks = head_masks(rows)

    def pair(i, carry):
        cut = pl.ds(pl.multiple_of(i * 2 * HEAD, 2 * HEAD), 2 * HEAD)
        cut_v = pl.ds(pl.multiple_of(half + i * 2 * HEAD, 2 * HEAD), 2 * HEAD)
        q_now = q_ref[:, cut] * BF16(HEAD**-0.5)
        parts = []
        for a in range(2):
            q_head = jnp.where(masks[a], q_now, BF16(0))
            scores = [dot_right(keyvals[j, :, cut], q_head) for j in range(4)]
            top = functools.reduce(jnp.maximum, [jnp.max(s, 0, keepdims=True) for s in scores])
            total, mixed = 0.0, 0.0
            for j in range(4):
                e = jnp.exp(scores[j] - top)
                total = total + jnp.sum(e, 0, keepdims=True)
                mixed = mixed + dot_left(keyvals[j, :, cut_v], e.astype(BF16))
            parts.append(mixed[a * HEAD : (a + 1) * HEAD] * (1.0 / total))
            sums_ref[i, a : a + 1, :] = top + jnp.log(total)
        place = pl.ds(pl.multiple_of(out_first + i * 2 * HEAD, 2 * HEAD), 2 * HEAD)
        out_ref[:, place] = jnp.concatenate(parts, 0).T.astype(BF16)
        return carry

    lax.fori_loop(first, last, pair, 0)


def attend_back(q_ref, keyvals, sums_ref, g_ref, dq_ref, dkeyvals, half, first, last):
    rows = q_ref.shape[0]
    masks = head_masks(rows)

    def pair(i, carry):
        cut = pl.ds(pl.multiple_of(i * 2 * HEAD, 2 * HEAD), 2 * HEAD)
        cut_v = pl.ds(pl.multiple_of(half + i * 2 * HEAD, 2 * HEAD), 2 * HEAD)
        q_now = q_ref[:, cut] * BF16(HEAD**-0.5)
        parts, dk_first, dv_first = [], [], []
        for a in range(2):
            q_head = jnp.where(masks[a], q_now, BF16(0))
            g_head = jnp.where(masks[a], g_ref[:, cut], BF16(0))
            log_sum = sums_ref[i, a : a + 1, :]
            weights, dweights, delta = [], [], 0.0
            for j in range(4):
                p = jnp.exp(dot_right(keyvals[j, :, cut], q_head) - log_sum)
                dp = dot_right(keyvals[j, :, cut_v], g_head)
                delta = delta + jnp.sum(p * dp, 0, keepdims=True)
                weights.append(p)
                dweights.append(dp)
            mixed = 0.0
            for j in range(4):
                ds = (weights[j] * (dweights[j] - delta)).astype(BF16)
                dk = dot_plain(ds, q_head)
                dv = dot_plain(weights[j].astype(BF16), g_head)
                mixed = mixed + dot_left(keyvals[j, :, cut], ds)
                if a == 0:
                    dk_first.append(dk)
                    dv_first.append(dv)
                else:
                    dkeyvals[j, :, cut] = (dk_first[j] + dk).astype(BF16)
                    dkeyvals[j, :, cut_v] = (dv_first[j] + dv).astype(BF16)
            parts.append(mixed[a * HEAD : (a + 1) * HEAD] * HEAD**-0.5)
        dq_ref[:, cut] = jnp.concatenate(parts, 0).T.astype(BF16)
        return carry

    lax.fori_loop(first, last, pair, 0)


def own_cut(crew, half):
    return pl.ds(pl.multiple_of(crew.group * half, half), half)


def send_half(crew, buffer, half):
    cut = own_cut(crew, half)
    return crew.send(buffer.at[:, cut], buffer.at[:, cut], crew.grp)


def grad_into(crew, whole, pipe, x, grad, begin=0, end=None):
    part = whole.part
    wide, narrow, rows, cols = part.shape
    width = width_of(cols)
    turned = x[...].T
    for first in range(begin, cols if end is None else end, width):
        cut = pl.ds(first, width)
        term = dot_plain(turned, grad[:, first : first + width])
        part[:, :, :, cut] = term.astype(part.dtype).reshape(wide, narrow, rows, width)
        scatter(crew, whole, pipe, cut)


def scatter(crew, whole, pipe, cut):
    pipe.add(whole.kind(crew, whole, cut, crew.given))
    crew.given += 1


def laid(rows, count, first):
    span, cols = rows.shape[1], 16 * count

    def place_of(shape):
        col = lax.broadcasted_iota(jnp.int32, shape, 1)
        owner = jnp.floor((col.astype(F32) + 0.5) * (1.0 / count)).astype(jnp.int32)
        return owner, col - owner * count

    lane = lax.broadcasted_iota(jnp.int32, (span, cols), 0)
    pick = jnp.where(lane == place_of((span, cols))[1] + first, 1.0, 0.0)
    out = dot_plain(to_bf16(rows), to_bf16(pick))
    block = lax.broadcasted_iota(jnp.int32, (16, cols), 0)
    kept = block == place_of((16, cols))[0]
    return [
        jnp.sum(jnp.where(kept, out[16 * k : 16 * k + 16], 0.0), 0, keepdims=True)
        for k in range(rows.shape[0] // 16)
    ]


SMALL = [chr(97 + i) + "_in" for i in range(11)]


def begin_part(cam, mod, small, enc_width, dec_width, enc_inner, dec_inner):
    depth, width = mod.shape
    half = enc_width // 2

    def body(r, crew, pipe):
        cams = r.cams
        copies = [
            crew.send(r.cam.at[place * 4 + crew.narrow], cams.at[crew.wide], target)
            for place, target in zip(crew.places, crew.line)
        ]
        cams[crew.wide] = r.cam[crew.wide * 4 + crew.narrow]
        row = 0
        r.small.piece[...] = jnp.zeros((16, 128), F32)
        for name in SMALL:
            value = getattr(r, name)[...].astype(F32)
            for first in range(0, value.shape[1], 128):
                cut = value[:, first : first + 128]
                r.small.piece[row : row + 1, 0 : cut.shape[1]] = cut
                row += 1
        pipe.begin(r.small.jobs[0])
        yield
        for copy in copies:
            copy.wait_recv()
        rows = cams[...].reshape(4, cams.shape[2])[:, :depth]
        high = to_bf16(rows)
        left = rows - high.astype(F32)
        middle = to_bf16(left)
        low = to_bf16(left - middle.astype(F32))
        rows = jnp.concatenate([high.astype(F32), middle.astype(F32), low.astype(F32)], 0)
        terms = dot_plain(to_bf16(rows), r.mod[...])
        r.terms[...] = (terms[0:4] + (terms[4:8] + terms[8:12])).reshape(4, 1, width)
        copies = [
            crew.send(r.terms.at[place], r.landed.at[i], target)
            for i, (place, target) in enumerate(zip(crew.places, crew.line))
        ]
        r.small.need()
        rows = r.small.buf[...].reshape(16, 16, 128)
        names = (r.gain_one, r.shift_one, r.bias_proj, r.gain_two, r.shift_two, r.bias_fc2)
        six = jnp.concatenate([rows[:, i] for i in range(6)], 0)
        for name, vector in zip(names, laid(six, enc_width // 16, 0)):
            name[...] = vector
        (r.bias_qv[...],) = laid(rows[:, 6], enc_width // 8, 0)
        for i in range(2):
            source = pl.ds(pl.multiple_of(i * enc_width + crew.group * half, half), half)
            r.bias_qkv[:, pl.ds(2 * i * half, half)] = r.bias_qv[:, source]
        r.bias_qkv[:, pl.ds(half, half)] = jnp.zeros((1, half), F32)
        for copy in copies:
            copy.wait_recv()
        r.held[0] = r.terms[crew.wide] + (r.landed[0] + r.landed[1] + r.landed[2])
        copy = crew.send(r.held.at[0], r.held.at[1], crew.core)
        two = jnp.concatenate([rows[:, 7], rows[:, 8]], 1)
        (r.bias_fc1[...],) = laid(two, enc_inner, crew.group * enc_inner)
        copy.wait_recv()
        r.held[2] = r.held[0] + r.held[1]
        copy = crew.send(r.held.at[2], r.held.at[3], crew.row)
        two = jnp.concatenate([rows[:, 9], rows[:, 10]], 1)
        (r.bias_dfc1[...],) = laid(two, dec_inner, crew.group * dec_inner)
        (r.bias_dfc2[...],) = laid(rows[:, 11], dec_width // 16, 0)
        pipe.pump()
        copy.wait_recv()
        pipe.pump()
        for i in range(6):
            cut = pl.ds(i * dec_width, dec_width)
            r.modulation[pl.ds(i, 1), :] = r.held[2, :, cut] + r.held[3, :, cut]

    vector = shape_of((1, enc_width), F32)
    ins = dict(cam=cam, mod=mod)
    ins.update({SMALL[i]: value for i, value in enumerate(small)})
    return Part(
        body,
        ins=ins,
        packs=dict(small=(16, 128)),
        outs=dict(
            modulation=shape_of((6, dec_width), F32),
            cams=shape_of((4, 1, 128), F32),
            gain_one=vector,
            gain_two=vector,
        ),
        scratch=dict(
            terms=pltpu.VMEM((4, 1, width), F32),
            landed=pltpu.VMEM((3, 1, width), F32),
            held=pltpu.VMEM((4, 1, width), F32),
            shift_one=pltpu.VMEM((1, enc_width), F32),
            shift_two=pltpu.VMEM((1, enc_width), F32),
            bias_proj=pltpu.VMEM((1, enc_width), F32),
            bias_fc2=pltpu.VMEM((1, enc_width), F32),
            bias_qv=pltpu.VMEM((1, 2 * enc_width), F32),
            bias_qkv=pltpu.VMEM((1, 3 * half), F32),
            bias_fc1=pltpu.VMEM((1, 16 * enc_inner), F32),
            bias_dfc1=pltpu.VMEM((1, 16 * dec_inner), F32),
            bias_dfc2=pltpu.VMEM((1, dec_width), F32),
        ),
    )


def encoder_part(x, params, links, given, moved, late, shapes, inner, cross_half):
    rows, width = x.shape
    half = width // 2
    pairs = half // (2 * HEAD)

    def body(r, crew, pipe):
        copy = crew.send(r.x, r.x_row, crew.row)
        yield
        x_now = r.x[...].astype(F32)
        normed = to_bf16(normalise(x_now)[0] * r.gain_one[...] + r.shift_one[...])
        r.normed_one[...] = normed
        copy.wait_recv()
        x_now = r.x_row[...].astype(F32)
        other = to_bf16(normalise(x_now)[0] * r.gain_one[...] + r.shift_one[...])
        r.qkv.need()
        weight = r.qkv.all()
        bias = r.bias_qkv[...]
        out = dot_plain(normed, weight) + bias
        r.queries[...] = to_bf16(out[:, :half])
        r.keyvals[0] = to_bf16(out[:, half:])
        spread = Spread(crew, r.keyvals)
        spread.give(0)
        r.keyvals[2] = to_bf16(dot_plain(other, weight[:, half:]) + bias[:, half:])
        spread.give(2)
        pipe.pump()
        yield
        spread.finish()
        attend(r.queries, r.keyvals, r.attended, crew.group * half, r.sums, half, 0, pairs)
        copy = send_half(crew, r.attended, half)
        pipe.pump()
        yield
        r.proj.need()
        copy.wait_recv()
        hidden = r.x[...].astype(F32) + dot_plain(r.attended[...], r.proj.all())
        hidden = hidden + r.bias_proj[...]
        r.hidden[...] = hidden
        normed = normalise(hidden)[0] * r.gain_two[...] + r.shift_two[...]
        r.normed_two[...] = to_bf16(normed)
        step = inner // 4
        total = 0.0
        for i in range(4):
            if i == 0:
                r.fc1.need()
            cut = pl.ds(i * step, step)
            pre = dot_plain(r.normed_two[...], r.fc1.cols(cut)) + r.bias_fc1[:, cut]
            r.pre[:, cut] = pre
            act = to_bf16(gelu_pair(pre)[1])
            if i == 0:
                r.fc2.need()
            total = total + dot_plain(act, r.fc2.rows(i))
        r.term[...] = to_bf16(total)
        copy = crew.send(r.term, r.landed, crew.grp)
        pipe.pump()
        yield
        copy.wait_recv()
        both = r.term[...].astype(F32) + r.landed[...].astype(F32)
        r.image[...] = to_bf16(r.hidden[...] + both + r.bias_fc2[...])
        copy = crew.send(r.image, r.x_row, crew.row)
        r.cross_kv.need()
        spread = Spread(crew, r.cross_keyvals)
        r.cross_keyvals[0] = to_bf16(dot_plain(r.image[...], r.cross_kv.all()))
        spread.give(0)
        yield
        copy.wait_recv()
        r.cross_keyvals[2] = to_bf16(dot_plain(r.x_row[...], r.cross_kv.all()))
        spread.give(2)
        yield
        spread.finish()

    ins = dict(x=x)
    ins.update(params)
    return Part(
        body,
        ins=ins,
        links=links,
        given=given,
        moved=moved,
        late=late,
        shapes=shapes,
        outs=dict(
            normed_one=shape_of((rows, width), BF16),
            queries=shape_of((rows, half), BF16),
            keyvals=shape_of((4, rows, width), BF16),
            attended=shape_of((rows, width), BF16),
            sums=shape_of((pairs, 2, rows), F32),
            hidden=shape_of((rows, width), F32),
            normed_two=shape_of((rows, width), BF16),
            pre=shape_of((rows, inner), F32),
            image=shape_of((rows, width), BF16),
            cross_keyvals=shape_of((4, rows, 2 * cross_half), BF16),
        ),
        scratch=dict(
            x_row=pltpu.VMEM((rows, width), BF16),
            term=pltpu.VMEM((rows, width), BF16),
            landed=pltpu.VMEM((rows, width), BF16),
        ),
    )


def self_part(x, params, links, given, moved, late, shapes, scratch):
    rows, width = x.shape
    half = width // 2
    pairs = half // (2 * HEAD)

    def body(r, crew, pipe):
        copy = crew.send(r.x, r.x_row, crew.row)
        yield
        gain, shift = 1.0 + r.modulation[0:1], r.modulation[1:2]
        r.normed_one[...] = to_bf16(normalise(r.x[...].astype(F32))[0] * gain + shift)
        copy.wait_recv()
        r.x_row[...] = to_bf16(normalise(r.x_row[...].astype(F32))[0] * gain + shift)
        spread = Spread(crew, r.keyvals)
        for i in (1, 2, 0):
            cut = pl.ds(i * half, half)
            r.qkv.need(i)
            if i == 0:
                r.queries[...] = to_bf16(dot_plain(r.normed_one[...], r.qkv.cols(cut)))
            else:
                place = pl.ds((i - 1) * half, half)
                r.keyvals[0, :, place] = to_bf16(
                    dot_plain(r.normed_one[...], r.qkv.cols(cut))
                )
                r.keyvals[2, :, place] = to_bf16(dot_plain(r.x_row[...], r.qkv.cols(cut)))
            if i == 2:
                spread.give(0)
                spread.give(2)
        pipe.pump()
        yield
        spread.finish()
        first = crew.group * half
        attend(r.queries, r.keyvals, r.attended, first, r.sums, half, 0, pairs // 2)
        pipe.pump()
        attend(r.queries, r.keyvals, r.attended, first, r.sums, half, pairs // 2, pairs)
        copy = send_half(crew, r.attended, half)
        pipe.pump()
        yield
        r.proj.need()
        copy.wait_recv()
        after = r.x[...].astype(F32) + dot_plain(r.attended[...], r.proj.all())
        r.after_self[...] = after
        normed = normalise(after)[0] * (1.0 + r.modulation[2:3]) + r.modulation[3:4]
        r.normed_two[...] = to_bf16(normed)
        r.cross_q.need()
        r.cross_queries[...] = to_bf16(dot_plain(r.normed_two[...], r.cross_q.all()))
        pipe.pump()

    ins = dict(x=x)
    ins.update(params)
    scratch = dict(scratch)
    scratch.update(x_row=pltpu.VMEM((rows, width), BF16))
    return Part(
        body,
        ins=ins,
        links=links,
        given=given,
        moved=moved,
        late=late,
        shapes=shapes,
        outs=dict(
            normed_one=shape_of((rows, width), BF16),
            queries=shape_of((rows, half), BF16),
            keyvals=shape_of((4, rows, width), BF16),
            attended=shape_of((rows, width), BF16),
            sums=shape_of((pairs, 2, rows), F32),
            after_self=shape_of((rows, width), F32),
            normed_two=shape_of((rows, width), BF16),
            cross_queries=shape_of((rows, half), BF16),
        ),
        scratch=scratch,
    )


def cross_part(rows, width, inner, ins, links, given, moved, late, shapes):
    half = width // 2
    pairs = half // (2 * HEAD)

    def body(r, crew, pipe):
        first = crew.group * half
        attend(r.queries, r.keyvals, r.attended, first, r.sums, half, 0, pairs // 2)
        pipe.pump()
        attend(r.queries, r.keyvals, r.attended, first, r.sums, half, pairs // 2, pairs)
        copy = send_half(crew, r.attended, half)
        pipe.pump()
        r.proj.need()
        copy.wait_recv()
        after = r.after_self[...] + dot_plain(r.attended[...], r.proj.all())
        r.after_cross[...] = after
        normed = normalise(after)[0] * (1.0 + r.modulation[4:5]) + r.modulation[5:6]
        r.normed_three[...] = to_bf16(normed)
        step = inner // 4
        for i in range(4):
            r.fc1.need(i)
            cut = pl.ds(i * step, step)
            pre = dot_plain(r.normed_three[...], r.fc1.cols(cut)) + r.bias_fc1[:, cut]
            r.pre[:, cut] = pre
            r.act[:, cut] = to_bf16(gelu_pair(pre)[1])
        copies = []
        for i in range(2):
            r.fc2.need(i)
            cut = pl.ds(i * half, half)
            r.term[:, cut] = to_bf16(dot_plain(r.act[...], r.fc2.cols(cut)))
            copies.append(crew.send(r.term.at[:, cut], r.landed.at[:, cut], crew.grp))
        for i, copy in enumerate(copies):
            cut = pl.ds(i * half, half)
            copy.wait_recv()
            both = r.term[:, cut].astype(F32) + r.landed[:, cut].astype(F32)
            r.final[:, cut] = r.after_cross[:, cut] + both + r.bias_fc2[:, cut]
        yield

    return Part(
        body,
        ins=ins,
        links=links,
        given=given,
        moved=moved,
        late=late,
        shapes=shapes,
        outs=dict(
            attended=shape_of((rows, width), BF16),
            sums=shape_of((pairs, 2, rows), F32),
            after_cross=shape_of((rows, width), F32),
            normed_three=shape_of((rows, width), BF16),
            pre=shape_of((rows, inner), F32),
            final=shape_of((rows, width), F32),
        ),
        scratch=dict(
            act=pltpu.VMEM((rows, inner), BF16),
            term=pltpu.VMEM((rows, width), BF16),
            landed=pltpu.VMEM((rows, width), BF16),
        ),
    )


def feed_back(r, grad):
    inner = r.pre.shape[1]
    step = inner // 4
    total = 0.0
    r.fc2.need()
    for i in range(4):
        cut = pl.ds(i * step, step)
        dact = dot_right(grad, r.fc2.rows(i))
        act, slope = gelu_both(r.pre[:, cut])
        r.act[:, cut] = to_bf16(act)
        dpre = to_bf16(slope * dact)
        r.dpre[:, cut] = dpre
        r.pre_sums[:, cut] = column_sums(dpre)
        if i == 0:
            r.fc1.need()
        total = total + dot_right(dpre, r.fc1.cols(cut))
    return to_bf16(total)


def both_of(r):
    return r.term[...].astype(F32) + r.landed[...].astype(F32)


def cross_back_part(ins, given, halves, sums):
    rows, width = ins["after_cross"].shape
    inner = ins["pre"].shape[1]
    held, image_width = ins["image"].shape
    half = width // 2
    pairs = half // (2 * HEAD)
    moving = bool(sums)

    def body(r, crew, pipe):
        r.branch[...] = to_bf16(r.grad[...])
        r.term[...] = feed_back(r, r.branch[...])
        copy = crew.send(r.term, r.landed, crew.grp)
        if moving:
            grad_into(crew, r.d_fc2, pipe, r.act, r.branch)
            grad_into(crew, r.d_fc1, pipe, r.normed_three, r.dpre)
        copy.wait_recv()
        gain = 1.0 + r.modulation[4:5]
        grad_in, r.gamma_three[...], r.beta_three[...] = norm_back(
            r.after_cross[...], gain, both_of(r)
        )
        after = r.grad[...] + grad_in
        r.grad_after[...] = after
        r.cross_branch[...] = to_bf16(after)
        r.proj.need()
        r.dattended[...] = to_bf16(dot_right(r.cross_branch[...], r.proj.all()))
        if moving:
            branch = r.cross_branch[:, own_cut(crew, half)]
            grad_into(crew, r.d_proj, pipe, r.attended, branch)
        pipe.pump()
        args = (r.queries, r.keyvals, r.sums, r.dattended, r.cross_dq, r.dkeyvals, half)
        attend_back(*args, 0, pairs // 2)
        pipe.pump()
        attend_back(*args, pairs // 2, pairs)
        fold = Fold(crew, r.dkeyvals, r.landing)
        r.cross_q.need()
        r.term_two[...] = to_bf16(dot_right(r.cross_dq[...], r.cross_q.all()))
        copy = crew.send(r.term_two, r.landed_two, crew.grp)
        fold.turn()
        if moving:
            grad_into(crew, r.d_cross_q, pipe, r.normed_two, r.cross_dq)
        pipe.pump()
        copy.wait_recv()
        gain = 1.0 + r.modulation[2:3]
        both = r.term_two[...].astype(F32) + r.landed_two[...].astype(F32)
        grad_in, r.gamma_two[...], r.beta_two[...] = norm_back(r.after_self[...], gain, both)
        r.cross_dkv[...] = fold.finish()
        r.cross_kv.need()
        r.term_image[...] = to_bf16(dot_right(r.cross_dkv[...], r.cross_kv.all()))
        copy = crew.send(r.term_image, r.landed_image, crew.grp)
        r.grad_self[...] = r.grad_after[...] + grad_in
        pipe.pump()
        copy.wait_recv()
        both = r.term_image[...].astype(F32) + r.landed_image[...].astype(F32)
        r.image_grad[...] = to_bf16(both)
        yield

    outs = dict(
        pre_sums=shape_of((1, inner), F32),
        gamma_three=shape_of((1, width), F32),
        beta_three=shape_of((1, width), F32),
        gamma_two=shape_of((1, width), F32),
        beta_two=shape_of((1, width), F32),
        cross_branch=shape_of((rows, width), BF16),
        cross_dq=shape_of((rows, half), BF16),
        cross_dkv=shape_of((held, width), BF16),
        grad_self=shape_of((rows, width), F32),
        image_grad=shape_of((held, image_width), BF16),
    )
    wide_row = pltpu.VMEM((rows, width), BF16)
    scratch = dict(
        branch=wide_row,
        term=wide_row,
        landed=wide_row,
        term_two=wide_row,
        landed_two=wide_row,
        grad_after=pltpu.VMEM((rows, width), F32),
        dattended=pltpu.VMEM((rows, half), BF16),
        dkeyvals=pltpu.VMEM((4, held, width), BF16),
        landing=pltpu.VMEM((3, held, width), BF16),
        term_image=pltpu.VMEM((held, image_width), BF16),
        landed_image=pltpu.VMEM((held, image_width), BF16),
    )
    if moving:
        scratch.update(
            act=pltpu.VMEM((rows, inner), BF16), dpre=pltpu.VMEM((rows, inner), BF16)
        )
    else:
        outs.update(act=shape_of((rows, inner), BF16), dpre=shape_of((rows, inner), BF16))
    return Part(
        body, ins=ins, given=given, halves=halves, sums=sums, outs=outs, scratch=scratch
    )


def self_back_part(ins, far, given, halves, sums):
    rows, width = far["x"].shape
    half = width // 2
    pairs = half // (2 * HEAD)
    moving = bool(sums)

    def body(r, crew, pipe):
        crew.keep(r.grad_self, r.x_grad).wait()
        branch = r.drows if moving else r.branch
        whole = pl.ds(0, width)
        branch[:, whole] = to_bf16(r.x_grad[...])
        r.proj.need()
        r.term[:, pl.ds(0, half)] = to_bf16(dot_right(branch[:, whole], r.proj.all()))
        if moving:
            grad_into(crew, r.d_proj, pipe, r.attended, branch[:, own_cut(crew, half)])
        args = (r.queries, r.keyvals, r.sums, r.term, r.drows, r.dkeyvals, half)
        attend_back(*args, 0, pairs // 2)
        pipe.pump(2)
        attend_back(*args, pairs // 2, pairs)
        fold = Fold(crew, r.dkeyvals, r.landing)
        first, rest = pl.ds(0, half), pl.ds(half, 2 * half)
        r.qkv.need()
        r.term[...] = to_bf16(dot_right(r.drows[:, first], r.qkv.cols(first)))
        fold.turn()
        if moving:
            grad_into(crew, r.d_qkv, pipe, r.normed_one, r.drows, 0, half)
            grad_into(crew, r.d_cross_kv, pipe, r.image, r.cross_dkv)
        pipe.pump(2)
        yield
        r.drows[:, rest] = fold.finish()
        term = r.term[...].astype(F32) + dot_right(r.drows[:, rest], r.qkv.cols(rest))
        r.term[...] = to_bf16(term)
        copy = crew.send(r.term, r.landed, crew.grp)
        if moving:
            grad_into(crew, r.d_qkv, pipe, r.normed_one, r.drows, half)
        held = (r.drows if moving else r.held).at[:, pl.ds(0, width)]
        fetch = crew.keep(r.x, held)
        yield
        fetch.wait()
        copy.wait_recv()
        gain = 1.0 + r.modulation[0:1]
        grad_in, r.gamma_one[...], r.beta_one[...] = norm_back(
            held[...].astype(F32), gain, both_of(r)
        )
        r.x_grad[...] += grad_in

    outs = dict(
        gamma_one=shape_of((1, width), F32),
        beta_one=shape_of((1, width), F32),
        x_grad=shape_of((rows, width), F32),
    )
    wide_row = pltpu.VMEM((rows, width), BF16)
    scratch = dict(
        term=wide_row,
        landed=wide_row,
        dkeyvals=pltpu.VMEM((4, rows, width), BF16),
        landing=pltpu.VMEM((3, rows, width), BF16),
    )
    if moving:
        scratch.update(drows=pltpu.VMEM((rows, 3 * half), BF16))
    else:
        scratch.update(held=wide_row)
        outs.update(
            branch=shape_of((rows, width), BF16), drows=shape_of((rows, 3 * half), BF16)
        )
    return Part(
        body, ins=ins, far=far, given=given, halves=halves, sums=sums, outs=outs, scratch=scratch
    )


def encoder_back_part(ins, far, given, halves, sums):
    rows, width = far["x"].shape
    half = width // 2
    pairs = half // (2 * HEAD)
    inner = ins["pre"].shape[1]
    moving = bool(sums)

    def body(r, crew, pipe):
        r.term[...] = feed_back(r, r.image_grad[...])
        copy = crew.send(r.term, r.landed, crew.grp)
        if moving:
            grad_into(crew, r.d_fc2, pipe, r.act, r.image_grad)
            grad_into(crew, r.d_fc1, pipe, r.normed_two, r.dpre)
        yield
        copy.wait_recv()
        grad_in, r.gain_two_grad[...], r.shift_two_grad[...] = norm_back(
            r.hidden[...], r.gain_two[...], both_of(r)
        )
        grad_hidden = r.image_grad[...].astype(F32) + grad_in
        r.x_grad[...] = grad_hidden
        branch = r.drows if moving else r.branch
        whole = pl.ds(0, width)
        branch[:, whole] = to_bf16(grad_hidden)
        r.branch_sums[...] = column_sums(branch[:, whole])
        r.proj.need()
        r.term_two[:, pl.ds(0, half)] = to_bf16(dot_right(branch[:, whole], r.proj.all()))
        if moving:
            grad_into(crew, r.d_proj, pipe, r.attended, branch[:, own_cut(crew, half)])
        pipe.pump(2)
        args = (r.queries, r.keyvals, r.sums, r.term_two, r.drows, r.dkeyvals, half)
        attend_back(*args, 0, pairs)
        fold = Fold(crew, r.dkeyvals, r.landing)
        first, rest = pl.ds(0, half), pl.ds(half, 2 * half)
        r.qkv.need()
        r.term_two[...] = to_bf16(dot_right(r.drows[:, first], r.qkv.cols(first)))
        fold.turn()
        r.row_sums[:, first] = column_sums(r.drows[:, first])
        if moving:
            grad_into(crew, r.d_qkv, pipe, r.normed_one, r.drows, 0, half)
        pipe.pump(2)
        yield
        r.drows[:, rest] = fold.finish()
        r.row_sums[:, rest] = column_sums(r.drows[:, rest])
        term = r.term_two[...].astype(F32) + dot_right(r.drows[:, rest], r.qkv.cols(rest))
        r.term_two[...] = to_bf16(term)
        copy = crew.send(r.term_two, r.landed_two, crew.grp)
        if moving:
            grad_into(crew, r.d_qkv, pipe, r.normed_one, r.drows, half)
        held = (r.drows if moving else r.held).at[:, pl.ds(0, width)]
        fetch = crew.keep(r.x, held)
        yield
        fetch.wait()
        copy.wait_recv()
        both = r.term_two[...].astype(F32) + r.landed_two[...].astype(F32)
        grad_in, r.gain_one_grad[...], r.shift_one_grad[...] = norm_back(
            held[...].astype(F32), r.gain_one[...], both
        )
        r.x_grad[...] += grad_in

    vector = shape_of((1, width), F32)
    outs = dict(
        pre_sums=shape_of((1, inner), F32),
        gain_two_grad=vector,
        shift_two_grad=vector,
        branch_sums=vector,
        row_sums=shape_of((1, 3 * half), F32),
        gain_one_grad=vector,
        shift_one_grad=vector,
        x_grad=shape_of((rows, width), F32),
    )
    wide_row = pltpu.VMEM((rows, width), BF16)
    scratch = dict(
        term=wide_row,
        landed=wide_row,
        term_two=wide_row,
        landed_two=wide_row,
        dkeyvals=pltpu.VMEM((4, rows, width), BF16),
        landing=pltpu.VMEM((3, rows, width), BF16),
    )
    if moving:
        scratch.update(
            act=pltpu.VMEM((rows, inner), BF16),
            dpre=pltpu.VMEM((rows, inner), BF16),
            drows=pltpu.VMEM((rows, 3 * half), BF16),
        )
    else:
        scratch.update(held=wide_row)
        outs.update(
            branch=shape_of((rows, width), BF16),
            act=shape_of((rows, inner), BF16),
            dpre=shape_of((rows, inner), BF16),
            drows=shape_of((rows, 3 * half), BF16),
        )
    return Part(
        body, ins=ins, far=far, given=given, halves=halves, sums=sums, outs=outs, scratch=scratch
    )


def end_part(small, mods):
    width = mods.shape[1]

    def body(r, crew, pipe):
        r.d_small.part[...] = r.packed[...]
        scatter(crew, r.d_small, pipe, pl.ds(0, 128))
        copy = crew.send(r.mods, r.held.at[0], crew.core)
        copy.wait_recv()
        r.held[1] = r.mods[...] + r.held[0]
        copy = crew.send(r.held.at[1], r.held.at[2], crew.row)
        pipe.pump()
        copy.wait_recv()
        r.held[3] = r.held[1] + r.held[2]
        r.everyone[crew.wide] = r.held[3]
        copies = [
            crew.send(r.held.at[3], r.everyone.at[crew.wide], target) for target in crew.line
        ]
        pipe.pump()
        for copy in copies:
            copy.wait_recv()
        yield

    return Part(
        body,
        ins=dict(packed=small, mods=mods),
        outs=dict(everyone=shape_of((4, 1, width), F32)),
        sums=dict(small=(Scatter, small.shape[2], small.shape[3], None, F32)),
        scratch=dict(held=pltpu.VMEM((4, 1, width), F32)),
    )


def plain_grad(x, grad):
    term = to_bf16(dot_left(x, grad))
    return lax.psum_scatter(term, BLOCKS, scatter_dimension=0, tiled=True)


def take(value, index, axis):
    return lax.dynamic_index_in_dim(value, index, axis, False)


def ray_loss(final_rows, head_weight, target_rgb, foreground, valid_rays):
    predicted = jnp.dot(final_rows, head_weight, precision=PRECISE)
    colour = jax.nn.sigmoid(predicted[:, :3])
    residue = colour - jnp.swapaxes(target_rgb, 0, 1)
    opacity = predicted[:, 3]
    per_ray = jnp.sum(residue * residue, -1) + jax.nn.softplus(opacity) - foreground * opacity
    return jnp.sum(valid_rays * per_ray)


def local(
    img_in,
    tri_in,
    cam,
    targets,
    fg_mask,
    counts,
    ln1_gain,
    ln1_bias,
    enc_qkv,
    enc_qv_bias,
    enc_proj,
    enc_proj_bias,
    ln2_gain,
    ln2_bias,
    enc_fc1,
    enc_fc1_bias,
    enc_fc2,
    enc_fc2_bias,
    dec_mod,
    dec_qkv,
    dec_proj,
    dec_cross_q,
    dec_cross_kv,
    dec_cross_proj,
    dec_fc1,
    dec_fc1_bias,
    dec_fc2,
    dec_fc2_bias,
    dec_head,
):
    group = lax.axis_index("grp")
    wide = lax.axis_index("wide")
    narrow = lax.axis_index("narrow")
    wides = lax.axis_size("wide")
    blocks = wides * lax.axis_size("narrow")
    block = wide * lax.axis_size("narrow") + narrow
    moving = wides == 4
    enc_width = img_in.shape[2]
    plane_rows, dec_width = tri_in.shape[1:]
    enc_half, dec_half = enc_width // 2, dec_width // 2
    enc_ff, dec_ff = enc_fc1.shape[1], dec_fc1.shape[1]
    enc_inner, dec_inner = enc_ff // blocks // 2, dec_ff // blocks // 2
    mod_rows = dec_mod.shape[0]

    def columns(shard, parts, width):
        cut = take(shard.reshape(shard.shape[0], parts, 2, width), group, 2)
        return cut.reshape(shard.shape[0], parts * width)

    def half_rows(shard):
        return take(shard.reshape(2, shard.shape[0] // 2, shard.shape[1]), group, 0)

    small_parts = (
        ln1_gain,
        ln1_bias,
        enc_proj_bias,
        ln2_gain,
        ln2_bias,
        enc_fc2_bias,
        enc_qv_bias,
        enc_fc1_bias,
        dec_fc1_bias,
        dec_fc2_bias,
        dec_head.reshape(-1),
    )
    piece = types.SimpleNamespace(
        enc_qkv=columns(enc_qkv, 3, enc_half),
        dec_qkv=columns(dec_qkv, 3, dec_half),
        enc_proj=enc_proj,
        enc_fc1=columns(enc_fc1, blocks, enc_inner),
        enc_fc2=half_rows(enc_fc2),
        dec_proj=dec_proj,
        cross_q=columns(dec_cross_q, 1, dec_half),
        cross_kv=columns(dec_cross_kv, 2, dec_half),
        cross_proj=dec_cross_proj,
        dec_fc1=columns(dec_fc1, blocks, dec_inner),
        dec_fc2=half_rows(dec_fc2),
    )
    shape = types.SimpleNamespace(**{name: value.shape for name, value in vars(piece).items()})
    raw = types.SimpleNamespace(
        enc_qkv=enc_qkv,
        dec_qkv=dec_qkv,
        enc_fc2=enc_fc2,
        cross_q=dec_cross_q,
        cross_kv=dec_cross_kv,
        dec_fc2=dec_fc2,
    )

    ray_slots = plane_rows * lax.axis_size("narrow") // VIEWS
    row_index = narrow * plane_rows + jnp.arange(plane_rows, dtype=jnp.int32)
    view_index, slot_index = row_index // ray_slots, row_index % ray_slots
    view_ids = jnp.arange(VIEWS, dtype=jnp.int32)
    limits = jnp.sum(jnp.where(view_index[:, None] == view_ids[None, :], counts, 0), -1)
    valid_rays = (slot_index < limits).astype(F32)
    foreground = fg_mask[0].astype(F32)

    if moving:
        small = [part.reshape(1, -1) for part in small_parts]
        cam_blocks = jnp.pad(cam.reshape(blocks, 1, mod_rows), ((0, 0), (0, 0), (0, 128 - mod_rows)))
        begin = begin_part(cam_blocks, dec_mod, small, enc_width, dec_width, enc_inner, dec_inner)
        wide_buffer = pltpu.VMEM((4, 4, dec_fc1.shape[0], dec_ff // 2), BF16)
        tall_buffer = pltpu.VMEM((4, 4, dec_fc2.shape[0] // 2, dec_width), BF16)
        square_buffer = pltpu.VMEM((4, 4, dec_proj.shape[0], dec_width), BF16)
        own_part = self_part(
            tri_in[0],
            dict(),
            dict(modulation=(begin, "modulation")),
            dict(),
            dict(
                qkv=(Gather, 2, raw.dec_qkv, cuts_of(piece.dec_qkv), True),
                proj=(GatherShared, 6, piece.dec_proj, [None], True),
                cross_q=(Gather, 7, raw.cross_q, cuts_of(piece.cross_q), True),
            ),
            dict(qkv=("broad", False), proj=("square", False)),
            dict(qkv=shape.dec_qkv, cross_q=shape.cross_q),
            dict(broad=wide_buffer, tall=tall_buffer, square=square_buffer),
        )
        enc_part = encoder_part(
            img_in[0],
            dict(),
            dict(
                gain_one=(begin, "gain_one"),
                shift_one=(begin, "shift_one"),
                bias_qkv=(begin, "bias_qkv"),
                bias_proj=(begin, "bias_proj"),
                gain_two=(begin, "gain_two"),
                shift_two=(begin, "shift_two"),
                bias_fc1=(begin, "bias_fc1"),
                bias_fc2=(begin, "bias_fc2"),
                tall=(own_part, "tall"),
            ),
            dict(),
            dict(
                qkv=(Gather, 1, raw.enc_qkv, cuts_of(piece.enc_qkv), True),
                proj=(GatherShared, 3, piece.enc_proj, [None], True),
                fc1=(Gather, 4, piece.enc_fc1, cuts_of(piece.enc_fc1), True),
                fc2=(Gather, 5, raw.enc_fc2, cuts_of(piece.enc_fc2), True),
                cross_kv=(Gather, 8, raw.cross_kv, cuts_of(piece.cross_kv), True),
            ),
            dict(fc2=("tall", False)),
            dict(qkv=shape.enc_qkv, fc2=shape.enc_fc2, cross_kv=shape.cross_kv),
            enc_ff // 2,
            dec_half,
        )
        last_part = cross_part(
            plane_rows,
            dec_width,
            dec_ff // 2,
            dict(),
            dict(
                queries=(own_part, "cross_queries"),
                keyvals=(enc_part, "cross_keyvals"),
                after_self=(own_part, "after_self"),
                modulation=(begin, "modulation"),
                bias_fc1=(begin, "bias_dfc1"),
                bias_fc2=(begin, "bias_dfc2"),
                broad=(own_part, "broad"),
                tall=(own_part, "tall"),
                square=(own_part, "square"),
            ),
            dict(),
            dict(
                proj=(GatherShared, 9, piece.cross_proj, [None], True),
                fc1=(Gather, 10, piece.dec_fc1, cuts_of(piece.dec_fc1), True),
                fc2=(Gather, 11, raw.dec_fc2, cuts_of(piece.dec_fc2), True),
            ),
            dict(fc1=("broad", True), fc2=("tall", True), proj=("square", True)),
            dict(fc2=shape.dec_fc2),
        )
        first, enc, own, cross = run(
            [begin, enc_part, own_part, last_part],
            2,
            True,
            order=(1, 0, 0, 2, 1, 2, 1, 2, 1, 2, 1, 1, 1),
            ahead=2,
            links=320,
        )
        modulation, cam_cut = first.modulation, first.cams.reshape(4, 128)[:, :mod_rows]
        gain_one, gain_two = first.gain_one, first.gain_two
        head = first.small.reshape(blocks, 16, 128)[:, 12:14]
        head = head.reshape(dec_width, 4)
        full = types.SimpleNamespace(
            enc_qkv=enc.qkv,
            enc_proj=enc.proj,
            enc_fc1=enc.fc1,
            enc_fc2=enc.fc2,
            cross_kv=enc.cross_kv,
            dec_qkv=own.qkv,
            dec_proj=own.proj,
            cross_q=own.cross_q,
            cross_proj=cross.proj,
            dec_fc1=cross.fc1,
            dec_fc2=cross.fc2,
        )
    else:
        small_all = lax.all_gather(jnp.concatenate(small_parts), BLOCKS, axis=0)
        unpacked, offset = [], 0
        for part in small_parts:
            length = part.shape[0]
            unpacked.append(small_all[:, offset : offset + length].reshape(1, -1).astype(F32))
            offset += length
        (
            gain_one,
            shift_one,
            bias_proj,
            gain_two,
            shift_two,
            bias_fc2,
            bias_qv,
            bias_fc1,
            bias_dfc1,
            bias_dfc2,
            head_flat,
        ) = unpacked
        head = head_flat.reshape(dec_width, 4)
        qv_half = take(bias_qv.reshape(2, 2, enc_half), group, 1)
        bias_qkv = jnp.concatenate([qv_half[0], jnp.zeros((enc_half,), F32), qv_half[1]])
        bias_qkv = bias_qkv.reshape(1, -1)
        fc1_half = take(bias_fc1.reshape(blocks, 2, enc_inner), group, 1).reshape(1, -1)
        dfc1_half = take(bias_dfc1.reshape(blocks, 2, dec_inner), group, 1).reshape(1, -1)
        cam_all = lax.all_gather(cam, "wide", axis=0, tiled=True)
        cam_cut = lax.dynamic_slice_in_dim(cam_all, block * mod_rows, mod_rows, 1)
        term = jnp.dot(cam_cut, dec_mod.astype(F32), precision=PRECISE)
        term = lax.psum(term, "narrow")
        modulation = lax.psum_scatter(term, "wide", scatter_dimension=0, tiled=True)
        modulation = modulation.reshape(6, dec_width)
        full = types.SimpleNamespace(
            **{
                name: lax.all_gather(value, BLOCKS, axis=0, tiled=True)
                for name, value in vars(piece).items()
            }
        )
        enc, own = run(
            [
                encoder_part(
                    img_in[0],
                    dict(
                        gain_one=gain_one,
                        shift_one=shift_one,
                        bias_qkv=bias_qkv,
                        bias_proj=bias_proj,
                        gain_two=gain_two,
                        shift_two=shift_two,
                        bias_fc1=fc1_half,
                        bias_fc2=bias_fc2,
                    ),
                    dict(),
                    dict(
                        qkv=full.enc_qkv,
                        proj=full.enc_proj,
                        fc1=full.enc_fc1,
                        fc2=full.enc_fc2,
                        cross_kv=full.cross_kv,
                    ),
                    dict(),
                    dict(),
                    dict(),
                    enc_ff // 2,
                    dec_half,
                ),
                self_part(
                    tri_in[0],
                    dict(modulation=modulation),
                    dict(),
                    dict(qkv=full.dec_qkv, proj=full.dec_proj, cross_q=full.cross_q),
                    dict(),
                    dict(),
                    dict(),
                    dict(),
                ),
            ],
            2,
            False,
            links=32,
        )
        (cross,) = run(
            [
                cross_part(
                    plane_rows,
                    dec_width,
                    dec_ff // 2,
                    dict(
                        queries=own.cross_queries,
                        keyvals=enc.cross_keyvals,
                        after_self=own.after_self,
                        modulation=modulation,
                        bias_fc1=dfc1_half,
                        bias_fc2=bias_dfc2,
                    ),
                    dict(),
                    dict(proj=full.cross_proj, fc1=full.dec_fc1, fc2=full.dec_fc2),
                    dict(),
                    dict(),
                    dict(),
                )
            ],
            3,
            False,
            links=32,
        )

    def ray_total(rows_in, head_in):
        return ray_loss(rows_in, head_in, targets[0], foreground, valid_rays)

    total, ray_pull = jax.vjp(ray_total, cross.final, head)
    grad_final, grad_head = ray_pull(jnp.ones((), F32))

    def sums_of(**named):
        return named if moving else {}

    (late,) = run(
        [
            cross_back_part(
                dict(
                    grad=grad_final,
                    pre=cross.pre,
                    normed_three=cross.normed_three,
                    after_cross=cross.after_cross,
                    modulation=modulation,
                    queries=own.cross_queries,
                    keyvals=enc.cross_keyvals,
                    sums=cross.sums,
                    after_self=own.after_self,
                    image=enc.image,
                    attended=cross.attended,
                    normed_two=own.normed_two,
                ),
                dict(
                    fc2=full.dec_fc2,
                    fc1=full.dec_fc1,
                    cross_q=full.cross_q,
                    cross_kv=full.cross_kv,
                ),
                dict(proj=full.cross_proj),
                sums_of(
                    fc2=(Scatter, piece.dec_fc2.shape[0], dec_width, "fc2", BF16),
                    fc1=(Scatter, piece.dec_fc1.shape[0], dec_ff // 2, "fc1", BF16),
                    proj=(ScatterLine, dec_cross_proj.shape[0], dec_half, None, BF16),
                    cross_q=(ScatterLine, dec_cross_q.shape[0], dec_half, "cross_q", BF16),
                ),
            )
        ],
        4,
        moving,
        links=128,
    )
    self_rows, enc_rows = dec_qkv.shape[0], enc_qkv.shape[0]
    front, back = run(
        [
            self_back_part(
                dict(
                    attended=own.attended,
                    queries=own.queries,
                    keyvals=own.keyvals,
                    sums=own.sums,
                    normed_one=own.normed_one,
                    modulation=modulation,
                    image=enc.image,
                    cross_dkv=late.cross_dkv,
                ),
                dict(grad_self=late.grad_self, x=tri_in[0]),
                dict(qkv=full.dec_qkv),
                dict(proj=full.dec_proj),
                sums_of(
                    cross_kv=(ScatterLine, enc_rows, dec_width, None, BF16),
                    proj=(Scatter, self_rows, dec_half, None, BF16),
                    qkv=(Scatter, self_rows, 3 * dec_half, "qkv", BF16),
                ),
            ),
            encoder_back_part(
                dict(
                    image_grad=late.image_grad,
                    pre=enc.pre,
                    hidden=enc.hidden,
                    normed_one=enc.normed_one,
                    normed_two=enc.normed_two,
                    attended=enc.attended,
                    queries=enc.queries,
                    keyvals=enc.keyvals,
                    sums=enc.sums,
                    gain_one=gain_one,
                    gain_two=gain_two,
                ),
                dict(x=img_in[0]),
                dict(fc2=full.enc_fc2, fc1=full.enc_fc1, qkv=full.enc_qkv),
                dict(proj=full.enc_proj),
                sums_of(
                    fc2=(Scatter, piece.enc_fc2.shape[0], enc_width, "fc2", BF16),
                    fc1=(ScatterLine, enc_rows, enc_ff // 2, "fc1", BF16),
                    proj=(Scatter, enc_rows, enc_half, None, BF16),
                    qkv=(Scatter, enc_rows, 3 * enc_half, "qkv", BF16),
                ),
            )
        ],
        5,
        moving,
        order=(1, 0, 1, 0, 1, 0, 1),
        links=200,
    )

    def placed(half, count, width):
        cut = half.reshape(count, 1, width)
        zero = jnp.zeros_like(cut)
        low = jnp.where(group == 0, cut, zero)
        high = jnp.where(group == 0, zero, cut)
        return jnp.concatenate([low, high], 1).reshape(-1)

    row_sums = back.row_sums[0]
    qv_sums = jnp.concatenate([row_sums[:enc_half], row_sums[2 * enc_half :]])
    loss_terms = jnp.stack([total, jnp.sum(valid_rays)])
    small_grads = (
        0.5 * back.gain_one_grad,
        0.5 * back.shift_one_grad,
        placed(qv_sums, 2, enc_half),
        0.5 * back.branch_sums,
        0.5 * back.gain_two_grad,
        0.5 * back.shift_two_grad,
        placed(back.pre_sums, blocks, enc_inner),
        0.5 * column_sums(late.image_grad),
        placed(late.pre_sums, blocks, dec_inner),
        0.5 * column_sums(to_bf16(grad_final)),
        0.5 * grad_head,
        jnp.tile(0.5 * loss_terms, blocks),
    )
    packed = jnp.concatenate([part.reshape(blocks, -1) for part in small_grads], 1)
    grad_mod = jnp.concatenate(
        [
            front.gamma_one,
            front.beta_one,
            late.gamma_two,
            late.beta_two,
            late.gamma_three,
            late.beta_three,
        ],
        1,
    )
    length = packed.shape[1]
    if moving:
        packed = jnp.pad(packed, ((0, 0), (0, 16 * 128 - length))).reshape(4, 4, 16, 128)
        (last,) = run([end_part(packed, grad_mod)], 7, True, links=32)
        small_sum = (last.d_small[0] + last.d_small[1]).reshape(-1)[:length]
        mod_all = last.everyone.reshape(4, -1)
    else:
        small_sum = take(lax.psum(packed, ("grp", "wide", "narrow")), block, 0)
        mod_all = lax.all_gather(lax.psum(grad_mod, "narrow"), "wide", axis=0, tiled=True)
    small_out, offset = [], 0
    for part in small_grads:
        count = part.size // blocks
        small_out.append(small_sum[offset : offset + count])
        offset += count
    loss = small_out[11][0] / small_out[11][1]
    grad_wmod = jnp.dot(jnp.transpose(cam_cut), mod_all, precision=PRECISE)

    def own_half(value):
        return take(value.reshape(value.shape[0], 2, -1), group, 1)

    def halves_of(reduced, x, grad):
        if not moving:
            half = plain_grad(x, grad)
            other = lax.ppermute(half, "grp", [(0, 1), (1, 0)])
            pair = jnp.stack([half, other])
            reduced = jnp.where(group == 0, pair, pair[::-1])
        return reduced.astype(F32)

    def full_columns(halves, parts):
        width = halves.shape[2] // parts
        cut = [
            halves[g, :, p * width : (p + 1) * width] for p in range(parts) for g in range(2)
        ]
        return jnp.concatenate(cut, 1)

    def full_rows(halves):
        return halves.reshape(-1, halves.shape[2])

    def reduced_of(space, name):
        return getattr(space, name, None)

    if moving:
        self_branch = enc_branch = enc_dpre = dec_dpre = enc_drows = dec_drows = None
        enc_act = dec_act = None
    else:
        self_branch, enc_branch = own_half(front.branch), own_half(back.branch)
        enc_act, dec_act = back.act, late.act
        enc_dpre, dec_dpre, enc_drows, dec_drows = back.dpre, late.dpre, back.drows, front.drows
    cross_branch = own_half(late.cross_branch)
    get = reduced_of
    out_qkv = halves_of(get(back, "d_qkv"), enc.normed_one, enc_drows)
    out_proj = halves_of(get(back, "d_proj"), enc.attended, enc_branch)
    out_fc1 = halves_of(get(back, "d_fc1"), enc.normed_two, enc_dpre)
    out_fc2 = halves_of(get(back, "d_fc2"), enc_act, late.image_grad)
    out_dqkv = halves_of(get(front, "d_qkv"), own.normed_one, dec_drows)
    out_dproj = halves_of(get(front, "d_proj"), own.attended, self_branch)
    out_cq = halves_of(get(late, "d_cross_q"), own.normed_two, late.cross_dq)
    out_ckv = halves_of(get(front, "d_cross_kv"), enc.image, late.cross_dkv)
    out_cproj = halves_of(get(late, "d_proj"), cross.attended, cross_branch)
    out_dfc1 = halves_of(get(late, "d_fc1"), cross.normed_three, dec_dpre)
    out_dfc2 = halves_of(get(late, "d_fc2"), dec_act, to_bf16(grad_final))

    return (
        loss,
        back.x_grad[None],
        front.x_grad[None],
        small_out[0],
        small_out[1],
        full_columns(out_qkv, 3),
        small_out[2],
        full_columns(out_proj, 1),
        small_out[3],
        small_out[4],
        small_out[5],
        full_columns(out_fc1, blocks),
        small_out[6],
        full_rows(out_fc2),
        small_out[7],
        grad_wmod,
        full_columns(out_dqkv, 3),
        full_columns(out_dproj, 1),
        full_columns(out_cq, 1),
        full_columns(out_ckv, 2),
        full_columns(out_cproj, 1),
        full_columns(out_dfc1, blocks),
        small_out[8],
        full_rows(out_dfc2),
        small_out[9],
        small_out[10].reshape(-1, 4),
    )


def solution(mesh):
    tokens = P("wide", "narrow", None)
    matrix = P(BLOCKS, None)
    vector = P(BLOCKS)
    objects = P("wide", None)
    rays = (P("wide", None, "narrow"), P("wide", "narrow"))
    encoder = (vector, vector, matrix, vector, matrix, vector, vector, vector, matrix, vector)
    encoder = encoder + (matrix, vector)
    decoder = (matrix,) * 7 + (vector, matrix, vector, matrix)
    return jax.shard_map(
        local,
        mesh=mesh,
        in_specs=(tokens, tokens, objects) + rays + (objects,) + encoder + decoder,
        out_specs=(P(), tokens, tokens) + encoder + decoder,
        check_vma=False,
    )
```

```python
import functools
import types

import jax
import jax.numpy as jnp
from jax import lax
from jax.experimental import pallas as pl
from jax.experimental.pallas import tpu as pltpu
from jax.sharding import PartitionSpec as P

HEAD = 64
VIEWS = 4
NORM_EPS = 1e-06
PRECISE = lax.Precision.HIGHEST
F32 = jnp.float32
BF16 = jnp.bfloat16
MIB = 1 << 20
VMEM = pl.BlockSpec(memory_space=pltpu.VMEM)
HBM = pl.BlockSpec(memory_space=pl.ANY)
MESH = pl.DeviceIdType.MESH
BLOCKS = ("wide", "narrow")


def shape_of(shape, dtype):
    return jax.ShapeDtypeStruct(shape, dtype)


def to_bf16(value):
    return value.astype(BF16)


def dot_plain(a, b):
    return jnp.dot(a, b, preferred_element_type=F32)


def dot_right(a, b):
    return lax.dot_general(a, b, (((1,), (1,)), ((), ())), preferred_element_type=F32)


def dot_left(a, b):
    return lax.dot_general(a, b, (((0,), (0,)), ((), ())), preferred_element_type=F32)


class Crew:
    def __init__(self, send, recv, here, lines):
        self.send_sems, self.recv_sems, self.here_sems = send, recv, here
        self.used = self.kept = self.slotted = self.given = 0
        self.credit = None
        self.sent = []
        self.group = lax.axis_index("grp")
        self.wide = lax.axis_index("wide")
        self.narrow = lax.axis_index("narrow")
        self.at_core = self.narrow + 1 - 2 * lax.rem(self.narrow, 2)
        self.at_row = lax.rem(self.narrow + 2, 4)
        self.at_cross = lax.rem(self.at_core + 2, 4)
        self.grp = {"grp": 1 - self.group}
        self.core = {"narrow": self.at_core}
        self.row = {"narrow": self.at_row}
        self.places = [lax.rem(self.wide + d, 4) for d in (1, 2, 3)] if lines else []
        self.line = [{"wide": place} for place in self.places]

    def greet(self):
        barrier = pltpu.get_barrier_semaphore()
        targets = [self.grp, self.core, self.row] + self.line
        for target in targets:
            pl.semaphore_signal(barrier, inc=1, device_id=target, device_id_type=MESH)
        pl.semaphore_wait(barrier, len(targets))

    def send(self, source, landing, target):
        copy = pltpu.make_async_remote_copy(
            src_ref=source,
            dst_ref=landing,
            send_sem=self.send_sems.at[self.used],
            recv_sem=self.recv_sems.at[self.used],
            device_id=target,
            device_id_type=MESH,
        )
        self.used += 1
        self.sent.append(copy)
        copy.start()
        return copy

    def keep(self, source, landing):
        copy = pltpu.make_async_copy(source, landing, self.here_sems.at[self.kept])
        self.kept += 1
        copy.start()
        return copy

    def close(self):
        for copy in self.sent:
            copy.wait_send()


class Gather:
    def __init__(self, crew, piece, full, cut, buf):
        self.crew, self.piece, self.full, self.cut, self.buf = crew, piece, full, cut, buf
        rows, cols = full.shape[2:]
        self.source = piece
        if piece.shape[0] == 2 * rows:
            self.source = piece.at[pl.ds(pl.multiple_of(crew.group * rows, rows), rows), cut]
        elif piece.shape[1] == 2 * cols:
            first = pl.multiple_of(2 * cut.start + crew.group * cut.size, 128)
            self.source = piece.at[:, pl.ds(first, cut.size)]
        else:
            self.source = piece.at[:, cut]
        self.steps = [self.start, self.turn, self.cross, self.finish]
        self.load, self.late = None, False

    def start(self):
        crew = self.crew
        source = self.source
        own = self.full.at[crew.wide, crew.narrow, :, self.cut]
        self.own = crew.keep(source, own)
        self.lines = [crew.send(source, own, target) for target in crew.line]

    def turn(self):
        crew = self.crew
        self.own.wait()
        for copy in self.lines:
            copy.wait_recv()
        mine = self.full.at[:, crew.narrow, :, self.cut]
        self.row = crew.send(mine, mine, crew.row)
        self.core = crew.send(mine, mine, crew.core)

    def cross(self):
        crew = self.crew
        self.row.wait_recv()
        other = self.full.at[:, crew.at_row, :, self.cut]
        self.far = crew.send(other, other, crew.core)

    def finish(self):
        self.core.wait_recv()
        self.far.wait_recv()
        if self.buf is not None and not self.late:
            self.fetch()

    def fetch(self):
        if self.load is None:
            self.load = self.crew.keep(
                self.full.at[:, :, :, self.cut], self.buf.at[:, :, :, self.cut]
            )


class GatherRow(Gather):
    def start(self):
        crew = self.crew
        source = self.source
        own = self.full.at[crew.wide, crew.narrow, :, self.cut]
        self.row = crew.send(source, own, crew.row)
        self.own = crew.keep(source, own)
        self.lines = [crew.send(source, own, target) for target in crew.line]

    def turn(self):
        crew = self.crew
        self.row.wait_recv()
        other = self.full.at[crew.wide, crew.at_row, :, self.cut]
        self.lines += [crew.send(other, other, target) for target in crew.line]

    def cross(self):
        crew = self.crew
        self.own.wait()
        for copy in self.lines:
            copy.wait_recv()
        mine = self.full.at[:, crew.narrow, :, self.cut]
        other = self.full.at[:, crew.at_row, :, self.cut]
        self.core = crew.send(mine, mine, crew.core)
        self.far = crew.send(other, other, crew.core)


class GatherShared(Gather):
    def __init__(self, crew, piece, full, cut, buf):
        half = piece.shape[1] // 2
        mine = pl.ds(pl.multiple_of(crew.group * half, half), half)
        super().__init__(crew, piece, full, mine, buf)
        self.steps = [self.start, self.turn, self.over, self.cross, self.finish]

    def turn(self):
        crew = self.crew
        self.own.wait()
        for copy in self.lines:
            copy.wait_recv()
        mine = self.full.at[:, crew.narrow, :, self.cut]
        self.row = crew.send(mine, mine, crew.row)
        self.others = [crew.send(mine, mine, crew.grp)]

    def over(self):
        crew = self.crew
        self.row.wait_recv()
        other = self.full.at[:, crew.at_row, :, self.cut]
        self.others.append(crew.send(other, other, crew.grp))

    def cross(self):
        crew = self.crew
        for copy in self.others:
            copy.wait_recv()
        mine, other = self.full.at[:, crew.narrow], self.full.at[:, crew.at_row]
        self.core = crew.send(mine, mine, crew.core)
        self.far = crew.send(other, other, crew.core)
        self.cut = slice(None)


class Scatter:
    def __init__(self, crew, whole, cut, index):
        rows = whole.part.shape[2]
        self.crew, self.part, self.cut, self.index = crew, whole.part, cut, index
        self.pair = whole.slots.at[index % 2, :, :, pl.ds(0, rows), pl.ds(0, cut.size)]
        self.single = whole.single.at[:, :, cut]
        self.lines = whole.lines.at[:, :, cut]
        self.out = whole.out.at[:, :, cut]
        self.steps = [self.start, self.turn, self.along, self.over, self.finish]

    def start(self):
        crew, part = self.crew, self.part
        if self.index >= 2:
            pl.semaphore_wait(crew.credit, 1)
        self.core = crew.send(part.at[:, crew.at_core, :, self.cut], self.pair.at[0], crew.core)
        self.far = crew.send(part.at[:, crew.at_cross, :, self.cut], self.pair.at[1], crew.core)

    def add(self, place, landing):
        part, cut = self.part, self.cut

        def one(i, carry):
            total = part[i, place, :, cut].astype(F32) + landing[i].astype(F32)
            part[i, place, :, cut] = total.astype(part.dtype)
            return carry

        lax.fori_loop(0, part.shape[0], one, 0)

    def turn(self):
        crew = self.crew
        self.far.wait_recv()
        self.add(crew.at_row, self.pair.at[1])
        self.row = crew.send(self.part.at[:, crew.at_row, :, self.cut], self.single, crew.row)
        self.core.wait_recv()
        self.add(crew.narrow, self.pair.at[0])
        if self.index < crew.slotted - 2:
            pl.semaphore_signal(crew.credit, inc=1, device_id=crew.core, device_id_type=MESH)

    def along(self):
        crew, part = self.crew, self.part
        self.row.wait_recv()
        self.add(crew.narrow, self.single)
        self.copies = [
            crew.send(part.at[place, crew.narrow, :, self.cut], self.lines.at[i], target)
            for i, (place, target) in enumerate(zip(crew.places, crew.line))
        ]

    def over(self):
        crew, part = self.crew, self.part
        for copy in self.copies:
            copy.wait_recv()
        total = part[crew.wide, crew.narrow, :, self.cut].astype(F32)
        for i in range(3):
            total = total + self.lines[i].astype(F32)
        own = self.out.at[crew.group]
        own[...] = total.astype(part.dtype)
        self.other = crew.send(own, own, crew.grp)

    def finish(self):
        self.other.wait_recv()


class ScatterLine(Scatter):
    def __init__(self, crew, whole, cut, index):
        super().__init__(crew, whole, cut, index)
        self.steps = [self.start, self.turn, self.along, self.over, self.finish]

    def turn(self):
        crew, part = self.crew, self.part
        self.far.wait_recv()
        self.add(crew.at_row, self.pair.at[1])
        self.core.wait_recv()
        self.add(crew.narrow, self.pair.at[0])
        if self.index < crew.slotted - 2:
            pl.semaphore_signal(crew.credit, inc=1, device_id=crew.core, device_id_type=MESH)
        self.copies = [
            [
                crew.send(part.at[place, narrow, :, self.cut], landing.at[i], target)
                for i, (place, target) in enumerate(zip(crew.places, crew.line))
            ]
            for narrow, landing in ((crew.at_row, self.single), (crew.narrow, self.lines))
        ]

    def total(self, copies, narrow, landing):
        crew = self.crew
        for copy in copies:
            copy.wait_recv()
        total = self.part[crew.wide, narrow, :, self.cut].astype(F32)
        for i in range(3):
            total = total + landing[i].astype(F32)
        return total.astype(self.part.dtype)

    def along(self):
        crew, part = self.crew, self.part
        own = part.at[crew.wide, crew.at_row, :, self.cut]
        own[...] = self.total(self.copies[0], crew.at_row, self.single)
        self.row = crew.send(own, self.single.at[3], crew.row)

    def over(self):
        crew = self.crew
        total = self.total(self.copies[1], crew.narrow, self.lines)
        self.row.wait_recv()
        own = self.out.at[crew.group]
        total = total.astype(F32) + self.single[3].astype(F32)
        own[...] = total.astype(self.part.dtype)
        self.other = crew.send(own, own, crew.grp)


class Summed:
    def __init__(self, part, single, lines, out, slots, kind):
        self.part, self.single, self.lines, self.out, self.slots = part, single, lines, out, slots
        self.kind = kind


class Pipe:
    def __init__(self, ahead):
        self.ahead, self.queue, self.jobs, self.pending = ahead, [], [], None

    def plan(self, job):
        job.at = 0
        self.queue.append(job)

    def begin(self, job):
        job.steps[0]()
        job.at = 1
        self.jobs.append(job)

    def fill(self):
        while self.queue and sum(job.at == 1 for job in self.jobs) < self.ahead:
            self.begin(self.queue.pop(0))

    def settle(self):
        if self.pending is not None:
            self.pending.turn()
            self.pending.at = 2
            self.jobs.append(self.pending)
            self.pending = None

    def add(self, job):
        job.start()
        self.settle()
        self.pending = job

    def go(self, job):
        job.steps[job.at]()
        job.at += 1
        if job.at == len(job.steps):
            self.jobs.remove(job)

    def pump(self, lag=1):
        before = self.pending
        self.settle()
        waiting = {}
        for job in self.jobs:
            if job is not before:
                waiting.setdefault(job.at, []).append(job)
        for at in sorted(waiting, reverse=True):
            if at == 1 or len(waiting[at]) > lag:
                self.go(waiting[at][0])
        self.fill()

    def need(self, job):
        while job.at < len(job.steps):
            self.pump()
            if job.at and job.at < len(job.steps):
                self.go(job)

    def drain(self):
        while self.jobs or self.queue or self.pending is not None:
            self.pump(0)


class Matrix:
    def __init__(self, buf, pipe):
        self.buf, self.pipe, self.jobs, self.load = buf, pipe, [], None
        self.loaded = []

    def need(self, index=None):
        wanted = [job for i, job in enumerate(self.jobs) if index is None or index == i]
        for job in wanted:
            self.pipe.need(job)
        for job in self.jobs:
            if job.at == len(job.steps):
                job.fetch()
        for job in wanted:
            if job not in self.loaded:
                job.load.wait()
                self.loaded.append(job)
        if self.load is not None:
            self.load.wait()
            self.load = None

    def cols(self, cut):
        value = self.buf[..., cut]
        return value.reshape(-1, value.shape[-1])

    def rows(self, i):
        if len(self.buf.shape) == 4:
            return self.buf[i].reshape(-1, self.buf.shape[3])
        height = self.buf.shape[0] // 4
        return self.buf[pl.ds(i * height, height), :]

    def all(self):
        return self.cols(slice(None))


class Part:
    def __init__(self, body, **named):
        self.body = body
        self.ins = named.get("ins", {})
        self.far = named.get("far", {})
        self.outs = named.get("outs", {})
        self.scratch = named.get("scratch", {})
        self.given = named.get("given", {})
        self.links = named.get("links", {})
        self.packs = named.get("packs", {})
        self.late = named.get("late", {})
        self.halves = named.get("halves", {})
        self.shapes = named.get("shapes", {})
        self.moved = named.get("moved", {})
        self.sums = named.get("sums", {})


def cuts_of(piece):
    cols = piece.shape[1]
    width = width_of(cols)
    return [pl.ds(first, width) for first in range(0, cols, width)]


def width_of(cols):
    for width in (512, 384):
        if cols % width == 0:
            return width
    return cols


def grad_scratch(rows, cols, dtype):
    return pltpu.VMEM((4, rows, cols), dtype), pltpu.VMEM((3, rows, cols), dtype)


def run(parts, collective, lines, order=(), ahead=4, links=0, flops=0, moved=0, limit=63):
    arrays, in_specs, out_shapes, out_specs, scratch = [], [], [], [], []
    layout = []
    for part in parts:
        named = []
        for name, value in part.ins.items():
            arrays.append(value)
            in_specs.append(VMEM)
        for name, value in part.far.items():
            arrays.append(value)
            in_specs.append(HBM)
        for name, value in part.given.items():
            arrays.append(value)
            in_specs.append(HBM)
            scratch.append(pltpu.VMEM(value.shape, BF16))
        for name, value in part.halves.items():
            arrays.append(value)
            in_specs.append(HBM)
            scratch.append(pltpu.VMEM((value.shape[0] // 2,) + value.shape[1:], BF16))
        for name, (_, _, piece, cuts, loaded) in part.moved.items():
            arrays.append(piece)
            in_specs.append(HBM)
            shape = (4, 4) + part.shapes.get(name, piece.shape)
            out_shapes.append(shape_of(shape, piece.dtype))
            out_specs.append(HBM)
            if loaded and name not in part.late:
                scratch.append(pltpu.VMEM(shape, piece.dtype))
        for name, shape in part.packs.items():
            out_shapes.append(shape_of((4, 4) + shape, F32))
            out_specs.append(HBM)
            scratch.append(pltpu.VMEM((4, 4) + shape, F32))
            scratch.append(pltpu.VMEM(shape, F32))
        for name, value in part.outs.items():
            out_shapes.append(value)
            out_specs.append(VMEM)
        for name, (kind, rows, cols, weight, dtype) in part.sums.items():
            out_shapes.append(shape_of((2, rows, cols), dtype))
            out_specs.append(VMEM)
            scratch.extend(grad_scratch(rows, cols, dtype))
            if weight is None:
                scratch.append(pltpu.VMEM((4, 4, rows, cols), dtype))
        for name, value in part.scratch.items():
            scratch.append(value)
    n_in, n_out = len(arrays), len(out_shapes)
    count = max(links, 1)
    summed = [entry for part in parts for entry in part.sums.values()]
    slotted = sum(cols // width_of(cols) for _, _, cols, _, _ in summed)
    if summed:
        depth = max(rows for _, rows, _, _, _ in summed)
        span = max(width_of(cols) for _, _, cols, _, _ in summed)
        scratch.append(pltpu.VMEM((2, 2, 4, depth, span), summed[0][4]))
        scratch.append(pltpu.SemaphoreType.REGULAR)
    scratch = scratch + [pltpu.SemaphoreType.DMA((count,))] * 3

    def kernel(*refs):
        ins, outs = iter(refs[:n_in]), iter(refs[n_in : n_in + n_out])
        rest = iter(refs[n_in + n_out : -3])
        crew = Crew(*refs[-3:], lines)
        slots = None
        if summed:
            slots, crew.credit = refs[-5:-3]
            crew.slotted = slotted
        pipe = Pipe(ahead)
        crew.greet()
        planned, spaces, loads = [], [], []
        for part in parts:
            space = types.SimpleNamespace()
            for name in part.ins:
                setattr(space, name, next(ins))
            for name in part.far:
                setattr(space, name, next(ins))
            for name in part.given:
                matrix = Matrix(next(rest), pipe)
                loads.append((matrix, next(ins)))
                setattr(space, name, matrix)
            for name in part.halves:
                matrix = Matrix(next(rest), pipe)
                height = matrix.buf.shape[0]
                first = pl.multiple_of(crew.group * height, height)
                loads.append((matrix, next(ins).at[pl.ds(first, height)]))
                setattr(space, name, matrix)
            for name, (kind, rank, piece, cuts, loaded) in part.moved.items():
                source, full = next(ins), next(outs)
                buf = next(rest) if loaded and name not in part.late else None
                matrix = Matrix(buf, pipe)
                setattr(space, name, matrix)
                for i, cut in enumerate(cuts):
                    job = kind(crew, source, full, cut, buf)
                    matrix.jobs.append(job)
                    planned.append((rank + 0.01 * i, job))
            for name in part.packs:
                matrix = Matrix(next(rest), pipe)
                matrix.piece = next(rest)
                matrix.jobs.append(Gather(crew, matrix.piece, next(outs), slice(None), matrix.buf))
                setattr(space, name, matrix)
            for name in part.outs:
                setattr(space, name, next(outs))
            for name, (kind, rows, cols, weight, dtype) in part.sums.items():
                out = next(outs)
                single, lines_in = next(rest), next(rest)
                own = next(rest) if weight is None else getattr(space, weight).buf
                setattr(space, "d_" + name, Summed(own, single, lines_in, out, slots, kind))
            for name in part.scratch:
                setattr(space, name, next(rest))
            spaces.append(space)
        for part, space in zip(parts, spaces):
            for name, (other, known) in part.links.items():
                setattr(space, name, getattr(spaces[parts.index(other)], known))
        for part, space in zip(parts, spaces):
            for name, (held, _) in part.late.items():
                rows_in, cols = part.shapes.get(name, part.moved[name][2].shape)
                matrix = getattr(space, name)
                matrix.buf = getattr(space, held).at[:, :, pl.ds(0, rows_in), pl.ds(0, cols)]
                for job in matrix.jobs:
                    job.buf, job.late = matrix.buf, part.late[name][1]
        for _, job in sorted(planned, key=lambda entry: entry[0]):
            pipe.plan(job)
        pipe.fill()
        for matrix, source in loads:
            matrix.load = crew.keep(source, matrix.buf)
        strands = [part.body(space, crew, pipe) for part, space in zip(parts, spaces)]
        for i in order:
            next(strands[i], None)
        while strands:
            for strand in list(strands):
                if next(strand, True):
                    strands.remove(strand)
        pipe.drain()
        for matrix, _ in loads:
            matrix.need()
        crew.close()

    results = pl.pallas_call(
        kernel,
        out_shape=out_shapes,
        in_specs=in_specs,
        out_specs=out_specs,
        scratch_shapes=scratch,
        compiler_params=pltpu.CompilerParams(
            vmem_limit_bytes=limit * MIB, collective_id=collective, has_side_effects=True
        ),
        cost_estimate=pl.CostEstimate(
            flops=int(flops), bytes_accessed=int(moved), transcendentals=0
        ),
    )(*arrays)
    results = iter(results)
    given = []
    for part in parts:
        space = types.SimpleNamespace()
        for name in part.moved:
            setattr(space, name, next(results))
        for name in part.packs:
            setattr(space, name, next(results))
        for name in part.outs:
            setattr(space, name, next(results))
        for name in part.sums:
            setattr(space, "d_" + name, next(results))
        given.append(space)
    return given


def normalise(x):
    centered = x - jnp.mean(x, -1, keepdims=True)
    scale = lax.rsqrt(jnp.mean(centered * centered, -1, keepdims=True) + NORM_EPS)
    return centered * scale, scale


def norm_back(values, gain, grad):
    xhat, scale = normalise(values)
    inner = grad * gain
    term = inner - jnp.mean(inner, -1, keepdims=True)
    term = term - xhat * jnp.mean(inner * xhat, -1, keepdims=True)
    return (
        term * scale,
        jnp.sum(grad * xhat, 0, keepdims=True),
        jnp.sum(grad, 0, keepdims=True),
    )


def column_sums(value):
    return jnp.sum(value.astype(F32), 0, keepdims=True)


def gelu_pair(pre):
    cdf = 0.5 * (1.0 + lax.erf(pre * 0.7071067811865476))
    return cdf, pre * cdf


def gelu_both(pre):
    cdf, act = gelu_pair(pre)
    return act, cdf + pre * (0.3989422804014327 * jnp.exp(-0.5 * pre * pre))


def head_masks(rows):
    lane = lax.broadcasted_iota(jnp.int32, (rows, 2 * HEAD), 1)
    return [lane < HEAD, lane >= HEAD]


class Spread:
    def __init__(self, crew, keyvals):
        self.crew, self.keyvals, self.copies = crew, keyvals, []

    def give(self, slot):
        copy = self.crew.send(
            self.keyvals.at[slot], self.keyvals.at[slot + 1], self.crew.core
        )
        self.copies.append(copy)

    def finish(self):
        for copy in self.copies:
            copy.wait_recv()


class Fold:
    def __init__(self, crew, dkeyvals, landing):
        self.crew, self.dkeyvals, self.landing = crew, dkeyvals, landing
        self.core = crew.send(dkeyvals.at[1], landing.at[0], crew.core)
        self.far = crew.send(dkeyvals.at[3], landing.at[1], crew.core)

    def turn(self):
        dkeyvals, landing = self.dkeyvals, self.landing
        self.far.wait_recv()
        dkeyvals[2] = (dkeyvals[2].astype(F32) + landing[1].astype(F32)).astype(BF16)
        self.row = self.crew.send(dkeyvals.at[2], landing.at[2], self.crew.row)

    def finish(self):
        landing = self.landing
        self.core.wait_recv()
        own = self.dkeyvals[0].astype(F32) + landing[0].astype(F32)
        self.row.wait_recv()
        return (own + landing[2].astype(F32)).astype(BF16)


def attend(q_ref, keyvals, out_ref, out_first, sums_ref, half, first, last):
    rows = q_ref.shape[0]
    masks = head_masks(rows)

    def pair(i, carry):
        cut = pl.ds(pl.multiple_of(i * 2 * HEAD, 2 * HEAD), 2 * HEAD)
        cut_v = pl.ds(pl.multiple_of(half + i * 2 * HEAD, 2 * HEAD), 2 * HEAD)
        q_now = q_ref[:, cut] * BF16(HEAD**-0.5)
        parts = []
        for a in range(2):
            q_head = jnp.where(masks[a], q_now, BF16(0))
            scores = [dot_right(keyvals[j, :, cut], q_head) for j in range(4)]
            top = functools.reduce(jnp.maximum, [jnp.max(s, 0, keepdims=True) for s in scores])
            total, mixed = 0.0, 0.0
            for j in range(4):
                e = jnp.exp(scores[j] - top)
                total = total + jnp.sum(e, 0, keepdims=True)
                mixed = mixed + dot_left(keyvals[j, :, cut_v], e.astype(BF16))
            parts.append(mixed[a * HEAD : (a + 1) * HEAD] * (1.0 / total))
            sums_ref[i, a : a + 1, :] = top + jnp.log(total)
        place = pl.ds(pl.multiple_of(out_first + i * 2 * HEAD, 2 * HEAD), 2 * HEAD)
        out_ref[:, place] = jnp.concatenate(parts, 0).T.astype(BF16)
        return carry

    lax.fori_loop(first, last, pair, 0)


def attend_back(q_ref, keyvals, sums_ref, g_ref, dq_ref, dkeyvals, half, first, last):
    rows = q_ref.shape[0]
    masks = head_masks(rows)

    def pair(i, carry):
        cut = pl.ds(pl.multiple_of(i * 2 * HEAD, 2 * HEAD), 2 * HEAD)
        cut_v = pl.ds(pl.multiple_of(half + i * 2 * HEAD, 2 * HEAD), 2 * HEAD)
        q_now = q_ref[:, cut] * BF16(HEAD**-0.5)
        parts, dk_first, dv_first = [], [], []
        for a in range(2):
            q_head = jnp.where(masks[a], q_now, BF16(0))
            g_head = jnp.where(masks[a], g_ref[:, cut], BF16(0))
            log_sum = sums_ref[i, a : a + 1, :]
            weights, dweights, delta = [], [], 0.0
            for j in range(4):
                p = jnp.exp(dot_right(keyvals[j, :, cut], q_head) - log_sum)
                dp = dot_right(keyvals[j, :, cut_v], g_head)
                delta = delta + jnp.sum(p * dp, 0, keepdims=True)
                weights.append(p)
                dweights.append(dp)
            mixed = 0.0
            for j in range(4):
                ds = (weights[j] * (dweights[j] - delta)).astype(BF16)
                dk = dot_plain(ds, q_head)
                dv = dot_plain(weights[j].astype(BF16), g_head)
                mixed = mixed + dot_left(keyvals[j, :, cut], ds)
                if a == 0:
                    dk_first.append(dk)
                    dv_first.append(dv)
                else:
                    dkeyvals[j, :, cut] = (dk_first[j] + dk).astype(BF16)
                    dkeyvals[j, :, cut_v] = (dv_first[j] + dv).astype(BF16)
            parts.append(mixed[a * HEAD : (a + 1) * HEAD] * HEAD**-0.5)
        dq_ref[:, cut] = jnp.concatenate(parts, 0).T.astype(BF16)
        return carry

    lax.fori_loop(first, last, pair, 0)


def own_cut(crew, half):
    return pl.ds(pl.multiple_of(crew.group * half, half), half)


def send_half(crew, buffer, half):
    cut = own_cut(crew, half)
    return crew.send(buffer.at[:, cut], buffer.at[:, cut], crew.grp)


def grad_into(crew, whole, pipe, x, grad, begin=0, end=None):
    part = whole.part
    wide, narrow, rows, cols = part.shape
    width = width_of(cols)
    turned = x[...].T
    for first in range(begin, cols if end is None else end, width):
        cut = pl.ds(first, width)
        term = dot_plain(turned, grad[:, first : first + width])
        part[:, :, :, cut] = term.astype(part.dtype).reshape(wide, narrow, rows, width)
        scatter(crew, whole, pipe, cut)


def scatter(crew, whole, pipe, cut):
    pipe.add(whole.kind(crew, whole, cut, crew.given))
    crew.given += 1


def laid(rows, count, first):
    span, cols = rows.shape[1], 16 * count

    def place_of(shape):
        col = lax.broadcasted_iota(jnp.int32, shape, 1)
        owner = jnp.floor((col.astype(F32) + 0.5) * (1.0 / count)).astype(jnp.int32)
        return owner, col - owner * count

    lane = lax.broadcasted_iota(jnp.int32, (span, cols), 0)
    pick = jnp.where(lane == place_of((span, cols))[1] + first, 1.0, 0.0)
    out = dot_plain(to_bf16(rows), to_bf16(pick))
    block = lax.broadcasted_iota(jnp.int32, (16, cols), 0)
    kept = block == place_of((16, cols))[0]
    return [
        jnp.sum(jnp.where(kept, out[16 * k : 16 * k + 16], 0.0), 0, keepdims=True)
        for k in range(rows.shape[0] // 16)
    ]


SMALL = [chr(97 + i) + "_in" for i in range(11)]


def begin_part(cam, mod, small, enc_width, dec_width, enc_inner, dec_inner):
    depth, width = mod.shape
    half = enc_width // 2

    def body(r, crew, pipe):
        cams = r.cams
        copies = [
            crew.send(r.cam.at[place * 4 + crew.narrow], cams.at[crew.wide], target)
            for place, target in zip(crew.places, crew.line)
        ]
        cams[crew.wide] = r.cam[crew.wide * 4 + crew.narrow]
        row = 0
        r.small.piece[...] = jnp.zeros((16, 128), F32)
        for name in SMALL:
            value = getattr(r, name)[...].astype(F32)
            for first in range(0, value.shape[1], 128):
                cut = value[:, first : first + 128]
                r.small.piece[row : row + 1, 0 : cut.shape[1]] = cut
                row += 1
        pipe.begin(r.small.jobs[0])
        yield
        for copy in copies:
            copy.wait_recv()
        rows = cams[...].reshape(4, cams.shape[2])[:, :depth]
        high = to_bf16(rows)
        left = rows - high.astype(F32)
        middle = to_bf16(left)
        low = to_bf16(left - middle.astype(F32))
        rows = jnp.concatenate([high.astype(F32), middle.astype(F32), low.astype(F32)], 0)
        terms = dot_plain(to_bf16(rows), r.mod[...])
        r.terms[...] = (terms[0:4] + (terms[4:8] + terms[8:12])).reshape(4, 1, width)
        copies = [
            crew.send(r.terms.at[place], r.landed.at[i], target)
            for i, (place, target) in enumerate(zip(crew.places, crew.line))
        ]
        r.small.need()
        rows = r.small.buf[...].reshape(16, 16, 128)
        names = (r.gain_one, r.shift_one, r.bias_proj, r.gain_two, r.shift_two, r.bias_fc2)
        six = jnp.concatenate([rows[:, i] for i in range(6)], 0)
        for name, vector in zip(names, laid(six, enc_width // 16, 0)):
            name[...] = vector
        (r.bias_qv[...],) = laid(rows[:, 6], enc_width // 8, 0)
        for i in range(2):
            source = pl.ds(pl.multiple_of(i * enc_width + crew.group * half, half), half)
            r.bias_qkv[:, pl.ds(2 * i * half, half)] = r.bias_qv[:, source]
        r.bias_qkv[:, pl.ds(half, half)] = jnp.zeros((1, half), F32)
        for copy in copies:
            copy.wait_recv()
        r.held[0] = r.terms[crew.wide] + (r.landed[0] + r.landed[1] + r.landed[2])
        copy = crew.send(r.held.at[0], r.held.at[1], crew.core)
        two = jnp.concatenate([rows[:, 7], rows[:, 8]], 1)
        (r.bias_fc1[...],) = laid(two, enc_inner, crew.group * enc_inner)
        copy.wait_recv()
        r.held[2] = r.held[0] + r.held[1]
        copy = crew.send(r.held.at[2], r.held.at[3], crew.row)
        two = jnp.concatenate([rows[:, 9], rows[:, 10]], 1)
        (r.bias_dfc1[...],) = laid(two, dec_inner, crew.group * dec_inner)
        (r.bias_dfc2[...],) = laid(rows[:, 11], dec_width // 16, 0)
        pipe.pump()
        copy.wait_recv()
        pipe.pump()
        for i in range(6):
            cut = pl.ds(i * dec_width, dec_width)
            r.modulation[pl.ds(i, 1), :] = r.held[2, :, cut] + r.held[3, :, cut]

    vector = shape_of((1, enc_width), F32)
    ins = dict(cam=cam, mod=mod)
    ins.update({SMALL[i]: value for i, value in enumerate(small)})
    return Part(
        body,
        ins=ins,
        packs=dict(small=(16, 128)),
        outs=dict(
            modulation=shape_of((6, dec_width), F32),
            cams=shape_of((4, 1, 128), F32),
            gain_one=vector,
            gain_two=vector,
        ),
        scratch=dict(
            terms=pltpu.VMEM((4, 1, width), F32),
            landed=pltpu.VMEM((3, 1, width), F32),
            held=pltpu.VMEM((4, 1, width), F32),
            shift_one=pltpu.VMEM((1, enc_width), F32),
            shift_two=pltpu.VMEM((1, enc_width), F32),
            bias_proj=pltpu.VMEM((1, enc_width), F32),
            bias_fc2=pltpu.VMEM((1, enc_width), F32),
            bias_qv=pltpu.VMEM((1, 2 * enc_width), F32),
            bias_qkv=pltpu.VMEM((1, 3 * half), F32),
            bias_fc1=pltpu.VMEM((1, 16 * enc_inner), F32),
            bias_dfc1=pltpu.VMEM((1, 16 * dec_inner), F32),
            bias_dfc2=pltpu.VMEM((1, dec_width), F32),
        ),
    )


def encoder_part(x, params, links, given, moved, late, shapes, inner, cross_half):
    rows, width = x.shape
    half = width // 2
    pairs = half // (2 * HEAD)

    def body(r, crew, pipe):
        copy = crew.send(r.x, r.x_row, crew.row)
        yield
        x_now = r.x[...].astype(F32)
        normed = to_bf16(normalise(x_now)[0] * r.gain_one[...] + r.shift_one[...])
        r.normed_one[...] = normed
        copy.wait_recv()
        x_now = r.x_row[...].astype(F32)
        other = to_bf16(normalise(x_now)[0] * r.gain_one[...] + r.shift_one[...])
        r.qkv.need()
        weight = r.qkv.all()
        bias = r.bias_qkv[...]
        out = dot_plain(normed, weight) + bias
        r.queries[...] = to_bf16(out[:, :half])
        r.keyvals[0] = to_bf16(out[:, half:])
        spread = Spread(crew, r.keyvals)
        spread.give(0)
        r.keyvals[2] = to_bf16(dot_plain(other, weight[:, half:]) + bias[:, half:])
        spread.give(2)
        pipe.pump()
        yield
        spread.finish()
        attend(r.queries, r.keyvals, r.attended, crew.group * half, r.sums, half, 0, pairs)
        copy = send_half(crew, r.attended, half)
        pipe.pump()
        yield
        r.proj.need()
        copy.wait_recv()
        hidden = r.x[...].astype(F32) + dot_plain(r.attended[...], r.proj.all())
        hidden = hidden + r.bias_proj[...]
        r.hidden[...] = hidden
        normed = normalise(hidden)[0] * r.gain_two[...] + r.shift_two[...]
        r.normed_two[...] = to_bf16(normed)
        step = inner // 4
        total = 0.0
        for i in range(4):
            if i == 0:
                r.fc1.need()
            cut = pl.ds(i * step, step)
            pre = dot_plain(r.normed_two[...], r.fc1.cols(cut)) + r.bias_fc1[:, cut]
            r.pre[:, cut] = pre
            act = to_bf16(gelu_pair(pre)[1])
            if i == 0:
                r.fc2.need()
            total = total + dot_plain(act, r.fc2.rows(i))
        r.term[...] = to_bf16(total)
        copy = crew.send(r.term, r.landed, crew.grp)
        pipe.pump()
        yield
        copy.wait_recv()
        both = r.term[...].astype(F32) + r.landed[...].astype(F32)
        r.image[...] = to_bf16(r.hidden[...] + both + r.bias_fc2[...])
        copy = crew.send(r.image, r.x_row, crew.row)
        r.cross_kv.need()
        spread = Spread(crew, r.cross_keyvals)
        r.cross_keyvals[0] = to_bf16(dot_plain(r.image[...], r.cross_kv.all()))
        spread.give(0)
        yield
        copy.wait_recv()
        r.cross_keyvals[2] = to_bf16(dot_plain(r.x_row[...], r.cross_kv.all()))
        spread.give(2)
        yield
        spread.finish()

    ins = dict(x=x)
    ins.update(params)
    return Part(
        body,
        ins=ins,
        links=links,
        given=given,
        moved=moved,
        late=late,
        shapes=shapes,
        outs=dict(
            normed_one=shape_of((rows, width), BF16),
            queries=shape_of((rows, half), BF16),
            keyvals=shape_of((4, rows, width), BF16),
            attended=shape_of((rows, width), BF16),
            sums=shape_of((pairs, 2, rows), F32),
            hidden=shape_of((rows, width), F32),
            normed_two=shape_of((rows, width), BF16),
            pre=shape_of((rows, inner), F32),
            image=shape_of((rows, width), BF16),
            cross_keyvals=shape_of((4, rows, 2 * cross_half), BF16),
        ),
        scratch=dict(
            x_row=pltpu.VMEM((rows, width), BF16),
            term=pltpu.VMEM((rows, width), BF16),
            landed=pltpu.VMEM((rows, width), BF16),
        ),
    )


def self_part(x, params, links, given, moved, late, shapes, scratch):
    rows, width = x.shape
    half = width // 2
    pairs = half // (2 * HEAD)

    def body(r, crew, pipe):
        copy = crew.send(r.x, r.x_row, crew.row)
        yield
        gain, shift = 1.0 + r.modulation[0:1], r.modulation[1:2]
        r.normed_one[...] = to_bf16(normalise(r.x[...].astype(F32))[0] * gain + shift)
        copy.wait_recv()
        r.x_row[...] = to_bf16(normalise(r.x_row[...].astype(F32))[0] * gain + shift)
        spread = Spread(crew, r.keyvals)
        for i in (1, 2, 0):
            cut = pl.ds(i * half, half)
            r.qkv.need(i)
            if i == 0:
                r.queries[...] = to_bf16(dot_plain(r.normed_one[...], r.qkv.cols(cut)))
            else:
                place = pl.ds((i - 1) * half, half)
                r.keyvals[0, :, place] = to_bf16(
                    dot_plain(r.normed_one[...], r.qkv.cols(cut))
                )
                r.keyvals[2, :, place] = to_bf16(dot_plain(r.x_row[...], r.qkv.cols(cut)))
            if i == 2:
                spread.give(0)
                spread.give(2)
        pipe.pump()
        yield
        spread.finish()
        first = crew.group * half
        attend(r.queries, r.keyvals, r.attended, first, r.sums, half, 0, pairs // 2)
        pipe.pump()
        attend(r.queries, r.keyvals, r.attended, first, r.sums, half, pairs // 2, pairs)
        copy = send_half(crew, r.attended, half)
        pipe.pump()
        yield
        r.proj.need()
        copy.wait_recv()
        after = r.x[...].astype(F32) + dot_plain(r.attended[...], r.proj.all())
        r.after_self[...] = after
        normed = normalise(after)[0] * (1.0 + r.modulation[2:3]) + r.modulation[3:4]
        r.normed_two[...] = to_bf16(normed)
        r.cross_q.need()
        r.cross_queries[...] = to_bf16(dot_plain(r.normed_two[...], r.cross_q.all()))
        pipe.pump()

    ins = dict(x=x)
    ins.update(params)
    scratch = dict(scratch)
    scratch.update(x_row=pltpu.VMEM((rows, width), BF16))
    return Part(
        body,
        ins=ins,
        links=links,
        given=given,
        moved=moved,
        late=late,
        shapes=shapes,
        outs=dict(
            normed_one=shape_of((rows, width), BF16),
            queries=shape_of((rows, half), BF16),
            keyvals=shape_of((4, rows, width), BF16),
            attended=shape_of((rows, width), BF16),
            sums=shape_of((pairs, 2, rows), F32),
            after_self=shape_of((rows, width), F32),
            normed_two=shape_of((rows, width), BF16),
            cross_queries=shape_of((rows, half), BF16),
        ),
        scratch=scratch,
    )


def cross_part(rows, width, inner, ins, links, given, moved, late, shapes):
    half = width // 2
    pairs = half // (2 * HEAD)

    def body(r, crew, pipe):
        first = crew.group * half
        attend(r.queries, r.keyvals, r.attended, first, r.sums, half, 0, pairs // 2)
        pipe.pump()
        attend(r.queries, r.keyvals, r.attended, first, r.sums, half, pairs // 2, pairs)
        copy = send_half(crew, r.attended, half)
        pipe.pump()
        r.proj.need()
        copy.wait_recv()
        after = r.after_self[...] + dot_plain(r.attended[...], r.proj.all())
        r.after_cross[...] = after
        normed = normalise(after)[0] * (1.0 + r.modulation[4:5]) + r.modulation[5:6]
        r.normed_three[...] = to_bf16(normed)
        step = inner // 4
        for i in range(4):
            r.fc1.need(i)
            cut = pl.ds(i * step, step)
            pre = dot_plain(r.normed_three[...], r.fc1.cols(cut)) + r.bias_fc1[:, cut]
            r.pre[:, cut] = pre
            r.act[:, cut] = to_bf16(gelu_pair(pre)[1])
        copies = []
        for i in range(2):
            r.fc2.need(i)
            cut = pl.ds(i * half, half)
            r.term[:, cut] = to_bf16(dot_plain(r.act[...], r.fc2.cols(cut)))
            copies.append(crew.send(r.term.at[:, cut], r.landed.at[:, cut], crew.grp))
        for i, copy in enumerate(copies):
            cut = pl.ds(i * half, half)
            copy.wait_recv()
            both = r.term[:, cut].astype(F32) + r.landed[:, cut].astype(F32)
            r.final[:, cut] = r.after_cross[:, cut] + both + r.bias_fc2[:, cut]
        yield

    return Part(
        body,
        ins=ins,
        links=links,
        given=given,
        moved=moved,
        late=late,
        shapes=shapes,
        outs=dict(
            attended=shape_of((rows, width), BF16),
            sums=shape_of((pairs, 2, rows), F32),
            after_cross=shape_of((rows, width), F32),
            normed_three=shape_of((rows, width), BF16),
            pre=shape_of((rows, inner), F32),
            final=shape_of((rows, width), F32),
        ),
        scratch=dict(
            act=pltpu.VMEM((rows, inner), BF16),
            term=pltpu.VMEM((rows, width), BF16),
            landed=pltpu.VMEM((rows, width), BF16),
        ),
    )


def feed_back(r, grad):
    inner = r.pre.shape[1]
    step = inner // 4
    total = 0.0
    r.fc2.need()
    for i in range(4):
        cut = pl.ds(i * step, step)
        dact = dot_right(grad, r.fc2.rows(i))
        act, slope = gelu_both(r.pre[:, cut])
        r.act[:, cut] = to_bf16(act)
        dpre = to_bf16(slope * dact)
        r.dpre[:, cut] = dpre
        r.pre_sums[:, cut] = column_sums(dpre)
        if i == 0:
            r.fc1.need()
        total = total + dot_right(dpre, r.fc1.cols(cut))
    return to_bf16(total)


def both_of(r):
    return r.term[...].astype(F32) + r.landed[...].astype(F32)


def cross_back_part(ins, given, halves, sums):
    rows, width = ins["after_cross"].shape
    inner = ins["pre"].shape[1]
    held, image_width = ins["image"].shape
    half = width // 2
    pairs = half // (2 * HEAD)
    moving = bool(sums)

    def body(r, crew, pipe):
        r.branch[...] = to_bf16(r.grad[...])
        r.term[...] = feed_back(r, r.branch[...])
        copy = crew.send(r.term, r.landed, crew.grp)
        if moving:
            grad_into(crew, r.d_fc2, pipe, r.act, r.branch)
            grad_into(crew, r.d_fc1, pipe, r.normed_three, r.dpre)
        copy.wait_recv()
        gain = 1.0 + r.modulation[4:5]
        grad_in, r.gamma_three[...], r.beta_three[...] = norm_back(
            r.after_cross[...], gain, both_of(r)
        )
        after = r.grad[...] + grad_in
        r.grad_after[...] = after
        r.cross_branch[...] = to_bf16(after)
        r.proj.need()
        r.dattended[...] = to_bf16(dot_right(r.cross_branch[...], r.proj.all()))
        if moving:
            branch = r.cross_branch[:, own_cut(crew, half)]
            grad_into(crew, r.d_proj, pipe, r.attended, branch)
        pipe.pump()
        args = (r.queries, r.keyvals, r.sums, r.dattended, r.cross_dq, r.dkeyvals, half)
        for i in range(0, pairs, 2):
            attend_back(*args, i, i + 1)
            pipe.pump()
            attend_back(*args, i + 1, i + 2)
            pipe.pump()
        fold = Fold(crew, r.dkeyvals, r.landing)
        r.cross_q.need()
        r.term_two[...] = to_bf16(dot_right(r.cross_dq[...], r.cross_q.all()))
        copy = crew.send(r.term_two, r.landed_two, crew.grp)
        fold.turn()
        if moving:
            grad_into(crew, r.d_cross_q, pipe, r.normed_two, r.cross_dq)
        pipe.pump()
        copy.wait_recv()
        gain = 1.0 + r.modulation[2:3]
        both = r.term_two[...].astype(F32) + r.landed_two[...].astype(F32)
        grad_in, r.gamma_two[...], r.beta_two[...] = norm_back(r.after_self[...], gain, both)
        r.cross_dkv[...] = fold.finish()
        r.cross_kv.need()
        r.term_image[...] = to_bf16(dot_right(r.cross_dkv[...], r.cross_kv.all()))
        copy = crew.send(r.term_image, r.landed_image, crew.grp)
        r.grad_self[...] = r.grad_after[...] + grad_in
        pipe.pump()
        copy.wait_recv()
        both = r.term_image[...].astype(F32) + r.landed_image[...].astype(F32)
        r.image_grad[...] = to_bf16(both)
        yield

    outs = dict(
        pre_sums=shape_of((1, inner), F32),
        gamma_three=shape_of((1, width), F32),
        beta_three=shape_of((1, width), F32),
        gamma_two=shape_of((1, width), F32),
        beta_two=shape_of((1, width), F32),
        cross_branch=shape_of((rows, width), BF16),
        cross_dq=shape_of((rows, half), BF16),
        cross_dkv=shape_of((held, width), BF16),
        grad_self=shape_of((rows, width), F32),
        image_grad=shape_of((held, image_width), BF16),
    )
    wide_row = pltpu.VMEM((rows, width), BF16)
    scratch = dict(
        branch=wide_row,
        term=wide_row,
        landed=wide_row,
        term_two=wide_row,
        landed_two=wide_row,
        grad_after=pltpu.VMEM((rows, width), F32),
        dattended=pltpu.VMEM((rows, half), BF16),
        dkeyvals=pltpu.VMEM((4, held, width), BF16),
        landing=pltpu.VMEM((3, held, width), BF16),
        term_image=pltpu.VMEM((held, image_width), BF16),
        landed_image=pltpu.VMEM((held, image_width), BF16),
    )
    if moving:
        scratch.update(
            act=pltpu.VMEM((rows, inner), BF16), dpre=pltpu.VMEM((rows, inner), BF16)
        )
    else:
        outs.update(act=shape_of((rows, inner), BF16), dpre=shape_of((rows, inner), BF16))
    return Part(
        body, ins=ins, given=given, halves=halves, sums=sums, outs=outs, scratch=scratch
    )


def self_back_part(ins, far, given, halves, sums):
    rows, width = far["x"].shape
    half = width // 2
    pairs = half // (2 * HEAD)
    moving = bool(sums)

    def body(r, crew, pipe):
        crew.keep(r.grad_self, r.x_grad).wait()
        branch = r.drows if moving else r.branch
        whole = pl.ds(0, width)
        branch[:, whole] = to_bf16(r.x_grad[...])
        r.proj.need()
        r.term[:, pl.ds(0, half)] = to_bf16(dot_right(branch[:, whole], r.proj.all()))
        if moving:
            grad_into(crew, r.d_proj, pipe, r.attended, branch[:, own_cut(crew, half)])
        args = (r.queries, r.keyvals, r.sums, r.term, r.drows, r.dkeyvals, half)
        attend_back(*args, 0, pairs // 2)
        pipe.pump(2)
        attend_back(*args, pairs // 2, pairs)
        fold = Fold(crew, r.dkeyvals, r.landing)
        first, rest = pl.ds(0, half), pl.ds(half, 2 * half)
        r.qkv.need()
        r.term[...] = to_bf16(dot_right(r.drows[:, first], r.qkv.cols(first)))
        fold.turn()
        if moving:
            grad_into(crew, r.d_qkv, pipe, r.normed_one, r.drows, 0, half)
            grad_into(crew, r.d_cross_kv, pipe, r.image, r.cross_dkv)
        pipe.pump(2)
        yield
        r.drows[:, rest] = fold.finish()
        term = r.term[...].astype(F32) + dot_right(r.drows[:, rest], r.qkv.cols(rest))
        r.term[...] = to_bf16(term)
        copy = crew.send(r.term, r.landed, crew.grp)
        if moving:
            grad_into(crew, r.d_qkv, pipe, r.normed_one, r.drows, half)
        held = (r.drows if moving else r.held).at[:, pl.ds(0, width)]
        fetch = crew.keep(r.x, held)
        yield
        fetch.wait()
        copy.wait_recv()
        gain = 1.0 + r.modulation[0:1]
        grad_in, r.gamma_one[...], r.beta_one[...] = norm_back(
            held[...].astype(F32), gain, both_of(r)
        )
        r.x_grad[...] += grad_in

    outs = dict(
        gamma_one=shape_of((1, width), F32),
        beta_one=shape_of((1, width), F32),
        x_grad=shape_of((rows, width), F32),
    )
    wide_row = pltpu.VMEM((rows, width), BF16)
    scratch = dict(
        term=wide_row,
        landed=wide_row,
        dkeyvals=pltpu.VMEM((4, rows, width), BF16),
        landing=pltpu.VMEM((3, rows, width), BF16),
    )
    if moving:
        scratch.update(drows=pltpu.VMEM((rows, 3 * half), BF16))
    else:
        scratch.update(held=wide_row)
        outs.update(
            branch=shape_of((rows, width), BF16), drows=shape_of((rows, 3 * half), BF16)
        )
    return Part(
        body, ins=ins, far=far, given=given, halves=halves, sums=sums, outs=outs, scratch=scratch
    )


def encoder_back_part(ins, far, given, halves, sums):
    rows, width = far["x"].shape
    half = width // 2
    pairs = half // (2 * HEAD)
    inner = ins["pre"].shape[1]
    moving = bool(sums)

    def body(r, crew, pipe):
        r.term[...] = feed_back(r, r.image_grad[...])
        copy = crew.send(r.term, r.landed, crew.grp)
        if moving:
            grad_into(crew, r.d_fc2, pipe, r.act, r.image_grad)
            grad_into(crew, r.d_fc1, pipe, r.normed_two, r.dpre)
        yield
        copy.wait_recv()
        grad_in, r.gain_two_grad[...], r.shift_two_grad[...] = norm_back(
            r.hidden[...], r.gain_two[...], both_of(r)
        )
        grad_hidden = r.image_grad[...].astype(F32) + grad_in
        r.x_grad[...] = grad_hidden
        branch = r.drows if moving else r.branch
        whole = pl.ds(0, width)
        branch[:, whole] = to_bf16(grad_hidden)
        r.branch_sums[...] = column_sums(branch[:, whole])
        r.proj.need()
        r.term_two[:, pl.ds(0, half)] = to_bf16(dot_right(branch[:, whole], r.proj.all()))
        if moving:
            grad_into(crew, r.d_proj, pipe, r.attended, branch[:, own_cut(crew, half)])
        pipe.pump(2)
        args = (r.queries, r.keyvals, r.sums, r.term_two, r.drows, r.dkeyvals, half)
        attend_back(*args, 0, pairs)
        fold = Fold(crew, r.dkeyvals, r.landing)
        first, rest = pl.ds(0, half), pl.ds(half, 2 * half)
        r.qkv.need()
        r.term_two[...] = to_bf16(dot_right(r.drows[:, first], r.qkv.cols(first)))
        fold.turn()
        r.row_sums[:, first] = column_sums(r.drows[:, first])
        if moving:
            grad_into(crew, r.d_qkv, pipe, r.normed_one, r.drows, 0, half)
        pipe.pump(2)
        yield
        r.drows[:, rest] = fold.finish()
        r.row_sums[:, rest] = column_sums(r.drows[:, rest])
        term = r.term_two[...].astype(F32) + dot_right(r.drows[:, rest], r.qkv.cols(rest))
        r.term_two[...] = to_bf16(term)
        copy = crew.send(r.term_two, r.landed_two, crew.grp)
        if moving:
            grad_into(crew, r.d_qkv, pipe, r.normed_one, r.drows, half)
        held = (r.drows if moving else r.held).at[:, pl.ds(0, width)]
        fetch = crew.keep(r.x, held)
        yield
        fetch.wait()
        copy.wait_recv()
        both = r.term_two[...].astype(F32) + r.landed_two[...].astype(F32)
        grad_in, r.gain_one_grad[...], r.shift_one_grad[...] = norm_back(
            held[...].astype(F32), r.gain_one[...], both
        )
        r.x_grad[...] += grad_in

    vector = shape_of((1, width), F32)
    outs = dict(
        pre_sums=shape_of((1, inner), F32),
        gain_two_grad=vector,
        shift_two_grad=vector,
        branch_sums=vector,
        row_sums=shape_of((1, 3 * half), F32),
        gain_one_grad=vector,
        shift_one_grad=vector,
        x_grad=shape_of((rows, width), F32),
    )
    wide_row = pltpu.VMEM((rows, width), BF16)
    scratch = dict(
        term=wide_row,
        landed=wide_row,
        term_two=wide_row,
        landed_two=wide_row,
        dkeyvals=pltpu.VMEM((4, rows, width), BF16),
        landing=pltpu.VMEM((3, rows, width), BF16),
    )
    if moving:
        scratch.update(
            act=pltpu.VMEM((rows, inner), BF16),
            dpre=pltpu.VMEM((rows, inner), BF16),
            drows=pltpu.VMEM((rows, 3 * half), BF16),
        )
    else:
        scratch.update(held=wide_row)
        outs.update(
            branch=shape_of((rows, width), BF16),
            act=shape_of((rows, inner), BF16),
            dpre=shape_of((rows, inner), BF16),
            drows=shape_of((rows, 3 * half), BF16),
        )
    return Part(
        body, ins=ins, far=far, given=given, halves=halves, sums=sums, outs=outs, scratch=scratch
    )


def end_part(small, mods):
    width = mods.shape[1]

    def body(r, crew, pipe):
        r.d_small.part[...] = r.packed[...]
        scatter(crew, r.d_small, pipe, pl.ds(0, 128))
        copy = crew.send(r.mods, r.held.at[0], crew.core)
        copy.wait_recv()
        r.held[1] = r.mods[...] + r.held[0]
        copy = crew.send(r.held.at[1], r.held.at[2], crew.row)
        pipe.pump(0)
        copy.wait_recv()
        r.held[3] = r.held[1] + r.held[2]
        r.everyone[crew.wide] = r.held[3]
        copies = [
            crew.send(r.held.at[3], r.everyone.at[crew.wide], target) for target in crew.line
        ]
        pipe.pump(0)
        for copy in copies:
            copy.wait_recv()
        yield

    return Part(
        body,
        ins=dict(packed=small, mods=mods),
        outs=dict(everyone=shape_of((4, 1, width), F32)),
        sums=dict(small=(Scatter, small.shape[2], small.shape[3], None, F32)),
        scratch=dict(held=pltpu.VMEM((4, 1, width), F32)),
    )


def plain_grad(x, grad):
    term = to_bf16(dot_left(x, grad))
    return lax.psum_scatter(term, BLOCKS, scatter_dimension=0, tiled=True)


def take(value, index, axis):
    return lax.dynamic_index_in_dim(value, index, axis, False)


def ray_loss(final_rows, head_weight, target_rgb, foreground, valid_rays):
    predicted = jnp.dot(final_rows, head_weight, precision=PRECISE)
    colour = jax.nn.sigmoid(predicted[:, :3])
    residue = colour - jnp.swapaxes(target_rgb, 0, 1)
    opacity = predicted[:, 3]
    per_ray = jnp.sum(residue * residue, -1) + jax.nn.softplus(opacity) - foreground * opacity
    return jnp.sum(valid_rays * per_ray)


def local(
    img_in,
    tri_in,
    cam,
    targets,
    fg_mask,
    counts,
    ln1_gain,
    ln1_bias,
    enc_qkv,
    enc_qv_bias,
    enc_proj,
    enc_proj_bias,
    ln2_gain,
    ln2_bias,
    enc_fc1,
    enc_fc1_bias,
    enc_fc2,
    enc_fc2_bias,
    dec_mod,
    dec_qkv,
    dec_proj,
    dec_cross_q,
    dec_cross_kv,
    dec_cross_proj,
    dec_fc1,
    dec_fc1_bias,
    dec_fc2,
    dec_fc2_bias,
    dec_head,
):
    group = lax.axis_index("grp")
    wide = lax.axis_index("wide")
    narrow = lax.axis_index("narrow")
    wides = lax.axis_size("wide")
    blocks = wides * lax.axis_size("narrow")
    block = wide * lax.axis_size("narrow") + narrow
    moving = wides == 4
    enc_width = img_in.shape[2]
    plane_rows, dec_width = tri_in.shape[1:]
    enc_half, dec_half = enc_width // 2, dec_width // 2
    enc_ff, dec_ff = enc_fc1.shape[1], dec_fc1.shape[1]
    enc_inner, dec_inner = enc_ff // blocks // 2, dec_ff // blocks // 2
    mod_rows = dec_mod.shape[0]

    def columns(shard, parts, width):
        cut = take(shard.reshape(shard.shape[0], parts, 2, width), group, 2)
        return cut.reshape(shard.shape[0], parts * width)

    def half_rows(shard):
        return take(shard.reshape(2, shard.shape[0] // 2, shard.shape[1]), group, 0)

    small_parts = (
        ln1_gain,
        ln1_bias,
        enc_proj_bias,
        ln2_gain,
        ln2_bias,
        enc_fc2_bias,
        enc_qv_bias,
        enc_fc1_bias,
        dec_fc1_bias,
        dec_fc2_bias,
        dec_head.reshape(-1),
    )
    piece = types.SimpleNamespace(
        enc_qkv=columns(enc_qkv, 3, enc_half),
        dec_qkv=columns(dec_qkv, 3, dec_half),
        enc_proj=enc_proj,
        enc_fc1=columns(enc_fc1, blocks, enc_inner),
        enc_fc2=half_rows(enc_fc2),
        dec_proj=dec_proj,
        cross_q=columns(dec_cross_q, 1, dec_half),
        cross_kv=columns(dec_cross_kv, 2, dec_half),
        cross_proj=dec_cross_proj,
        dec_fc1=columns(dec_fc1, blocks, dec_inner),
        dec_fc2=half_rows(dec_fc2),
    )
    shape = types.SimpleNamespace(**{name: value.shape for name, value in vars(piece).items()})
    raw = types.SimpleNamespace(
        enc_qkv=enc_qkv,
        dec_qkv=dec_qkv,
        enc_fc2=enc_fc2,
        cross_q=dec_cross_q,
        cross_kv=dec_cross_kv,
        dec_fc2=dec_fc2,
    )

    ray_slots = plane_rows * lax.axis_size("narrow") // VIEWS
    row_index = narrow * plane_rows + jnp.arange(plane_rows, dtype=jnp.int32)
    view_index, slot_index = row_index // ray_slots, row_index % ray_slots
    view_ids = jnp.arange(VIEWS, dtype=jnp.int32)
    limits = jnp.sum(jnp.where(view_index[:, None] == view_ids[None, :], counts, 0), -1)
    valid_rays = (slot_index < limits).astype(F32)
    foreground = fg_mask[0].astype(F32)

    if moving:
        small = [part.reshape(1, -1) for part in small_parts]
        cam_blocks = jnp.pad(cam.reshape(blocks, 1, mod_rows), ((0, 0), (0, 0), (0, 128 - mod_rows)))
        begin = begin_part(cam_blocks, dec_mod, small, enc_width, dec_width, enc_inner, dec_inner)
        wide_buffer = pltpu.VMEM((4, 4, dec_fc1.shape[0], dec_ff // 2), BF16)
        tall_buffer = pltpu.VMEM((4, 4, dec_fc2.shape[0] // 2, dec_width), BF16)
        square_buffer = pltpu.VMEM((4, 4, dec_proj.shape[0], dec_width), BF16)
        own_part = self_part(
            tri_in[0],
            dict(),
            dict(modulation=(begin, "modulation")),
            dict(),
            dict(
                qkv=(Gather, 2, raw.dec_qkv, cuts_of(piece.dec_qkv), True),
                proj=(GatherShared, 6, piece.dec_proj, [None], True),
                cross_q=(Gather, 7, raw.cross_q, cuts_of(piece.cross_q), True),
            ),
            dict(qkv=("broad", False), proj=("square", False)),
            dict(qkv=shape.dec_qkv, cross_q=shape.cross_q),
            dict(broad=wide_buffer, tall=tall_buffer, square=square_buffer),
        )
        enc_part = encoder_part(
            img_in[0],
            dict(),
            dict(
                gain_one=(begin, "gain_one"),
                shift_one=(begin, "shift_one"),
                bias_qkv=(begin, "bias_qkv"),
                bias_proj=(begin, "bias_proj"),
                gain_two=(begin, "gain_two"),
                shift_two=(begin, "shift_two"),
                bias_fc1=(begin, "bias_fc1"),
                bias_fc2=(begin, "bias_fc2"),
                tall=(own_part, "tall"),
            ),
            dict(),
            dict(
                qkv=(Gather, 1, raw.enc_qkv, cuts_of(piece.enc_qkv), True),
                proj=(GatherShared, 3, piece.enc_proj, [None], True),
                fc1=(Gather, 4, piece.enc_fc1, cuts_of(piece.enc_fc1), True),
                fc2=(Gather, 5, raw.enc_fc2, cuts_of(piece.enc_fc2), True),
                cross_kv=(Gather, 8, raw.cross_kv, cuts_of(piece.cross_kv), True),
            ),
            dict(fc2=("tall", False)),
            dict(qkv=shape.enc_qkv, fc2=shape.enc_fc2, cross_kv=shape.cross_kv),
            enc_ff // 2,
            dec_half,
        )
        last_part = cross_part(
            plane_rows,
            dec_width,
            dec_ff // 2,
            dict(),
            dict(
                queries=(own_part, "cross_queries"),
                keyvals=(enc_part, "cross_keyvals"),
                after_self=(own_part, "after_self"),
                modulation=(begin, "modulation"),
                bias_fc1=(begin, "bias_dfc1"),
                bias_fc2=(begin, "bias_dfc2"),
                broad=(own_part, "broad"),
                tall=(own_part, "tall"),
                square=(own_part, "square"),
            ),
            dict(),
            dict(
                proj=(GatherShared, 9, piece.cross_proj, [None], True),
                fc1=(Gather, 10, piece.dec_fc1, cuts_of(piece.dec_fc1), True),
                fc2=(Gather, 11, raw.dec_fc2, cuts_of(piece.dec_fc2), True),
            ),
            dict(fc1=("broad", True), fc2=("tall", True), proj=("square", True)),
            dict(fc2=shape.dec_fc2),
        )
        first, enc, own, cross = run(
            [begin, enc_part, own_part, last_part],
            2,
            True,
            order=(1, 0, 0, 2, 1, 2, 1, 2, 1, 2, 1, 1, 1),
            ahead=2,
            links=320,
        )
        modulation, cam_cut = first.modulation, first.cams.reshape(4, 128)[:, :mod_rows]
        gain_one, gain_two = first.gain_one, first.gain_two
        head = first.small.reshape(blocks, 16, 128)[:, 12:14]
        head = head.reshape(dec_width, 4)
        full = types.SimpleNamespace(
            enc_qkv=enc.qkv,
            enc_proj=enc.proj,
            enc_fc1=enc.fc1,
            enc_fc2=enc.fc2,
            cross_kv=enc.cross_kv,
            dec_qkv=own.qkv,
            dec_proj=own.proj,
            cross_q=own.cross_q,
            cross_proj=cross.proj,
            dec_fc1=cross.fc1,
            dec_fc2=cross.fc2,
        )
    else:
        small_all = lax.all_gather(jnp.concatenate(small_parts), BLOCKS, axis=0)
        unpacked, offset = [], 0
        for part in small_parts:
            length = part.shape[0]
            unpacked.append(small_all[:, offset : offset + length].reshape(1, -1).astype(F32))
            offset += length
        (
            gain_one,
            shift_one,
            bias_proj,
            gain_two,
            shift_two,
            bias_fc2,
            bias_qv,
            bias_fc1,
            bias_dfc1,
            bias_dfc2,
            head_flat,
        ) = unpacked
        head = head_flat.reshape(dec_width, 4)
        qv_half = take(bias_qv.reshape(2, 2, enc_half), group, 1)
        bias_qkv = jnp.concatenate([qv_half[0], jnp.zeros((enc_half,), F32), qv_half[1]])
        bias_qkv = bias_qkv.reshape(1, -1)
        fc1_half = take(bias_fc1.reshape(blocks, 2, enc_inner), group, 1).reshape(1, -1)
        dfc1_half = take(bias_dfc1.reshape(blocks, 2, dec_inner), group, 1).reshape(1, -1)
        cam_all = lax.all_gather(cam, "wide", axis=0, tiled=True)
        cam_cut = lax.dynamic_slice_in_dim(cam_all, block * mod_rows, mod_rows, 1)
        term = jnp.dot(cam_cut, dec_mod.astype(F32), precision=PRECISE)
        term = lax.psum(term, "narrow")
        modulation = lax.psum_scatter(term, "wide", scatter_dimension=0, tiled=True)
        modulation = modulation.reshape(6, dec_width)
        full = types.SimpleNamespace(
            **{
                name: lax.all_gather(value, BLOCKS, axis=0, tiled=True)
                for name, value in vars(piece).items()
            }
        )
        enc, own = run(
            [
                encoder_part(
                    img_in[0],
                    dict(
                        gain_one=gain_one,
                        shift_one=shift_one,
                        bias_qkv=bias_qkv,
                        bias_proj=bias_proj,
                        gain_two=gain_two,
                        shift_two=shift_two,
                        bias_fc1=fc1_half,
                        bias_fc2=bias_fc2,
                    ),
                    dict(),
                    dict(
                        qkv=full.enc_qkv,
                        proj=full.enc_proj,
                        fc1=full.enc_fc1,
                        fc2=full.enc_fc2,
                        cross_kv=full.cross_kv,
                    ),
                    dict(),
                    dict(),
                    dict(),
                    enc_ff // 2,
                    dec_half,
                ),
                self_part(
                    tri_in[0],
                    dict(modulation=modulation),
                    dict(),
                    dict(qkv=full.dec_qkv, proj=full.dec_proj, cross_q=full.cross_q),
                    dict(),
                    dict(),
                    dict(),
                    dict(),
                ),
            ],
            2,
            False,
            links=32,
        )
        (cross,) = run(
            [
                cross_part(
                    plane_rows,
                    dec_width,
                    dec_ff // 2,
                    dict(
                        queries=own.cross_queries,
                        keyvals=enc.cross_keyvals,
                        after_self=own.after_self,
                        modulation=modulation,
                        bias_fc1=dfc1_half,
                        bias_fc2=bias_dfc2,
                    ),
                    dict(),
                    dict(proj=full.cross_proj, fc1=full.dec_fc1, fc2=full.dec_fc2),
                    dict(),
                    dict(),
                    dict(),
                )
            ],
            3,
            False,
            links=32,
        )

    def ray_total(rows_in, head_in):
        return ray_loss(rows_in, head_in, targets[0], foreground, valid_rays)

    total, ray_pull = jax.vjp(ray_total, cross.final, head)
    grad_final, grad_head = ray_pull(jnp.ones((), F32))

    def sums_of(**named):
        return named if moving else {}

    (late,) = run(
        [
            cross_back_part(
                dict(
                    grad=grad_final,
                    pre=cross.pre,
                    normed_three=cross.normed_three,
                    after_cross=cross.after_cross,
                    modulation=modulation,
                    queries=own.cross_queries,
                    keyvals=enc.cross_keyvals,
                    sums=cross.sums,
                    after_self=own.after_self,
                    image=enc.image,
                    attended=cross.attended,
                    normed_two=own.normed_two,
                ),
                dict(
                    fc2=full.dec_fc2,
                    fc1=full.dec_fc1,
                    cross_q=full.cross_q,
                    cross_kv=full.cross_kv,
                ),
                dict(proj=full.cross_proj),
                sums_of(
                    fc2=(Scatter, piece.dec_fc2.shape[0], dec_width, "fc2", BF16),
                    fc1=(Scatter, piece.dec_fc1.shape[0], dec_ff // 2, "fc1", BF16),
                    proj=(ScatterLine, dec_cross_proj.shape[0], dec_half, None, BF16),
                    cross_q=(ScatterLine, dec_cross_q.shape[0], dec_half, "cross_q", BF16),
                ),
            )
        ],
        4,
        moving,
        links=128,
    )
    self_rows, enc_rows = dec_qkv.shape[0], enc_qkv.shape[0]
    front, back = run(
        [
            self_back_part(
                dict(
                    attended=own.attended,
                    queries=own.queries,
                    keyvals=own.keyvals,
                    sums=own.sums,
                    normed_one=own.normed_one,
                    modulation=modulation,
                    image=enc.image,
                    cross_dkv=late.cross_dkv,
                ),
                dict(grad_self=late.grad_self, x=tri_in[0]),
                dict(qkv=full.dec_qkv),
                dict(proj=full.dec_proj),
                sums_of(
                    cross_kv=(ScatterLine, enc_rows, dec_width, None, BF16),
                    proj=(Scatter, self_rows, dec_half, None, BF16),
                    qkv=(Scatter, self_rows, 3 * dec_half, "qkv", BF16),
                ),
            ),
            encoder_back_part(
                dict(
                    image_grad=late.image_grad,
                    pre=enc.pre,
                    hidden=enc.hidden,
                    normed_one=enc.normed_one,
                    normed_two=enc.normed_two,
                    attended=enc.attended,
                    queries=enc.queries,
                    keyvals=enc.keyvals,
                    sums=enc.sums,
                    gain_one=gain_one,
                    gain_two=gain_two,
                ),
                dict(x=img_in[0]),
                dict(fc2=full.enc_fc2, fc1=full.enc_fc1, qkv=full.enc_qkv),
                dict(proj=full.enc_proj),
                sums_of(
                    fc2=(Scatter, piece.enc_fc2.shape[0], enc_width, "fc2", BF16),
                    fc1=(ScatterLine, enc_rows, enc_ff // 2, "fc1", BF16),
                    proj=(Scatter, enc_rows, enc_half, None, BF16),
                    qkv=(Scatter, enc_rows, 3 * enc_half, "qkv", BF16),
                ),
            )
        ],
        5,
        moving,
        order=(1, 0, 1, 0, 1, 0, 1),
        links=200,
    )

    def placed(half, count, width):
        cut = half.reshape(count, 1, width)
        zero = jnp.zeros_like(cut)
        low = jnp.where(group == 0, cut, zero)
        high = jnp.where(group == 0, zero, cut)
        return jnp.concatenate([low, high], 1).reshape(-1)

    row_sums = back.row_sums[0]
    qv_sums = jnp.concatenate([row_sums[:enc_half], row_sums[2 * enc_half :]])
    loss_terms = jnp.stack([total, jnp.sum(valid_rays)])
    small_grads = (
        0.5 * back.gain_one_grad,
        0.5 * back.shift_one_grad,
        placed(qv_sums, 2, enc_half),
        0.5 * back.branch_sums,
        0.5 * back.gain_two_grad,
        0.5 * back.shift_two_grad,
        placed(back.pre_sums, blocks, enc_inner),
        0.5 * column_sums(late.image_grad),
        placed(late.pre_sums, blocks, dec_inner),
        0.5 * column_sums(to_bf16(grad_final)),
        0.5 * grad_head,
        jnp.tile(0.5 * loss_terms, blocks),
    )
    packed = jnp.concatenate([part.reshape(blocks, -1) for part in small_grads], 1)
    grad_mod = jnp.concatenate(
        [
            front.gamma_one,
            front.beta_one,
            late.gamma_two,
            late.beta_two,
            late.gamma_three,
            late.beta_three,
        ],
        1,
    )
    length = packed.shape[1]
    if moving:
        packed = jnp.pad(packed, ((0, 0), (0, 16 * 128 - length))).reshape(4, 4, 16, 128)
        (last,) = run([end_part(packed, grad_mod)], 7, True, links=32)
        small_sum = (last.d_small[0] + last.d_small[1]).reshape(-1)[:length]
        mod_all = last.everyone.reshape(4, -1)
    else:
        small_sum = take(lax.psum(packed, ("grp", "wide", "narrow")), block, 0)
        mod_all = lax.all_gather(lax.psum(grad_mod, "narrow"), "wide", axis=0, tiled=True)
    small_out, offset = [], 0
    for part in small_grads:
        count = part.size // blocks
        small_out.append(small_sum[offset : offset + count])
        offset += count
    loss = small_out[11][0] / small_out[11][1]
    grad_wmod = jnp.dot(jnp.transpose(cam_cut), mod_all, precision=PRECISE)

    def own_half(value):
        return take(value.reshape(value.shape[0], 2, -1), group, 1)

    def halves_of(reduced, x, grad):
        if not moving:
            half = plain_grad(x, grad)
            other = lax.ppermute(half, "grp", [(0, 1), (1, 0)])
            pair = jnp.stack([half, other])
            reduced = jnp.where(group == 0, pair, pair[::-1])
        return reduced.astype(F32)

    def full_columns(halves, parts):
        width = halves.shape[2] // parts
        cut = [
            halves[g, :, p * width : (p + 1) * width] for p in range(parts) for g in range(2)
        ]
        return jnp.concatenate(cut, 1)

    def full_rows(halves):
        return halves.reshape(-1, halves.shape[2])

    def reduced_of(space, name):
        return getattr(space, name, None)

    if moving:
        self_branch = enc_branch = enc_dpre = dec_dpre = enc_drows = dec_drows = None
        enc_act = dec_act = None
    else:
        self_branch, enc_branch = own_half(front.branch), own_half(back.branch)
        enc_act, dec_act = back.act, late.act
        enc_dpre, dec_dpre, enc_drows, dec_drows = back.dpre, late.dpre, back.drows, front.drows
    cross_branch = own_half(late.cross_branch)
    get = reduced_of
    out_qkv = halves_of(get(back, "d_qkv"), enc.normed_one, enc_drows)
    out_proj = halves_of(get(back, "d_proj"), enc.attended, enc_branch)
    out_fc1 = halves_of(get(back, "d_fc1"), enc.normed_two, enc_dpre)
    out_fc2 = halves_of(get(back, "d_fc2"), enc_act, late.image_grad)
    out_dqkv = halves_of(get(front, "d_qkv"), own.normed_one, dec_drows)
    out_dproj = halves_of(get(front, "d_proj"), own.attended, self_branch)
    out_cq = halves_of(get(late, "d_cross_q"), own.normed_two, late.cross_dq)
    out_ckv = halves_of(get(front, "d_cross_kv"), enc.image, late.cross_dkv)
    out_cproj = halves_of(get(late, "d_proj"), cross.attended, cross_branch)
    out_dfc1 = halves_of(get(late, "d_fc1"), cross.normed_three, dec_dpre)
    out_dfc2 = halves_of(get(late, "d_fc2"), dec_act, to_bf16(grad_final))

    return (
        loss,
        back.x_grad[None],
        front.x_grad[None],
        small_out[0],
        small_out[1],
        full_columns(out_qkv, 3),
        small_out[2],
        full_columns(out_proj, 1),
        small_out[3],
        small_out[4],
        small_out[5],
        full_columns(out_fc1, blocks),
        small_out[6],
        full_rows(out_fc2),
        small_out[7],
        grad_wmod,
        full_columns(out_dqkv, 3),
        full_columns(out_dproj, 1),
        full_columns(out_cq, 1),
        full_columns(out_ckv, 2),
        full_columns(out_cproj, 1),
        full_columns(out_dfc1, blocks),
        small_out[8],
        full_rows(out_dfc2),
        small_out[9],
        small_out[10].reshape(-1, 4),
    )


def solution(mesh):
    tokens = P("wide", "narrow", None)
    matrix = P(BLOCKS, None)
    vector = P(BLOCKS)
    objects = P("wide", None)
    rays = (P("wide", None, "narrow"), P("wide", "narrow"))
    encoder = (vector, vector, matrix, vector, matrix, vector, vector, vector, matrix, vector)
    encoder = encoder + (matrix, vector)
    decoder = (matrix,) * 7 + (vector, matrix, vector, matrix)
    return jax.shard_map(
        local,
        mesh=mesh,
        in_specs=(tokens, tokens, objects) + rays + (objects,) + encoder + decoder,
        out_specs=(P(), tokens, tokens) + encoder + decoder,
        check_vma=False,
    )
```
